128 devices in a mesh: rep: 16 (over x_hi, y, core), shard: 8 (over z, x_lo).
Axes of the slice: x: 4 (x_hi: 2, x_lo: 2; x = x_hi * 2 + x_lo), y: 4, z: 4, core: 2. Of those that a mesh axis runs over, the one named last changes fastest.
Arguments:
- hidden_in: bfloat16 [16384, 1024], P(('rep', 'shard')), may hold values from -6 to 6
- out_grad: bfloat16 [16384, 1024], P(('rep', 'shard')), may hold values from -6 to 6
- segment_ids: int32 [16384], P(('rep', 'shard')), may hold values from 0 to 1023, as said below
- first_gain: bfloat16 [1024], P('shard'), may hold values from 0.25 to 1.75
- first_shift: bfloat16 [1024], P('shard'), may hold values from -1.75 to 1.75
- second_gain: bfloat16 [1024], P('shard'), may hold values from 0.25 to 1.75
- second_shift: bfloat16 [1024], P('shard'), may hold values from -1.75 to 1.75
- qkv_weight: bfloat16 [1024, 3072], P('shard'), may hold values from -0.1875 to 0.1875
- qkv_bias: bfloat16 [3072], P('shard'), may hold values from -1.75 to 1.75
- dense_weight: bfloat16 [1024, 1024], P('shard'), may hold values from -2 to 2
- dense_bias: bfloat16 [1024], P('shard'), may hold values from -1.75 to 1.75
- up_weight: bfloat16 [1024, 4096], P('shard'), may hold values from -0.1875 to 0.1875
- up_bias: bfloat16 [4096], P('shard'), may hold values from -1.75 to 1.75
- down_weight: bfloat16 [4096, 1024], P('shard'), may hold values from -0.09375 to 0.09375
- down_bias: bfloat16 [1024], P('shard'), may hold values from -1.75 to 1.75
Outputs:
- output: bfloat16 [16384, 1024], P(('rep', 'shard'))
- input_grad: bfloat16 [16384, 1024], P(('rep', 'shard'))
- grad_first_gain: float32 [1024], P('shard')
- grad_first_shift: float32 [1024], P('shard')
- grad_second_gain: float32 [1024], P('shard')
- grad_second_shift: float32 [1024], P('shard')
- grad_qkv_weight: float32 [1024, 3072], P('shard')
- grad_qkv_bias: float32 [3072], P('shard')
- grad_dense_weight: float32 [1024, 1024], P('shard')
- grad_dense_bias: float32 [1024], P('shard')
- grad_up_weight: float32 [1024, 4096], P('shard')
- grad_up_bias: float32 [4096], P('shard')
- grad_down_weight: float32 [4096, 1024], P('shard')
- grad_down_bias: float32 [1024], P('shard')
The draws below stay inside these ranges and needn't reach their ends.
Inputs may be any that keep to these rules, and one draw needn't show every extreme that they name: `segment_ids`: along each packed row of 1024 tokens the ids start at 0 and never fall; equal ids in a row are one document. The last document of every row has id 1024 - 1. In every row one document begins within the row's first 128 tokens and ends within its last 128 tokens.
All inputs are finite; a program needn't handle non-finite values.
Results may differ from the reference program's by a relative error of at most 0.011.
Values may be sent and summed in bfloat16 or wider, within the bound.
A program may use at most 192 MiB of HBM per device.

```python
import jax
import jax.numpy as jnp
from jax import lax

D = 1024
HEADS = 16
FF = 4096
LEN = 1024
ROWS = 128
TOKENS = 16384


def draw_segment_ids(key, part):
    key = jax.random.fold_in(key, 11)
    key_first, key_last, key_cuts = jax.random.split(key, 3)
    packed = TOKENS // LEN
    first = jax.random.randint(key_first, (packed, 1), 1, ROWS)
    last = jax.random.randint(key_last, (packed, 1), LEN - ROWS + 1, LEN)
    places = jnp.arange(LEN, dtype=jnp.int32)[None, :]
    cuts = (jax.random.randint(key_cuts, (packed, LEN), 0, 6) == 0).astype(jnp.int32)
    inside = (places > first) & (places < last)
    bounds = jnp.where((places == first) | (places == last), 1, jnp.where(inside | (places == 0), 0, cuts))
    counted = jnp.cumsum(bounds, axis=1).astype(jnp.int32)
    final = jnp.max(counted, axis=1, keepdims=True)
    renamed = jnp.where(counted == final, LEN - 1, counted)
    return renamed.reshape(packed * LEN).astype(jnp.int32)


def steps_of(stream_key, shape, cuts, low, top_value):
    loudness, own = 1.0, jax.random.fold_in(stream_key, 6)
    for axis_at, parts in cuts:
        heights = jnp.exp(jax.random.uniform(jax.random.fold_in(own, axis_at), (parts,), jnp.float32, low / len(cuts), top_value / len(cuts)))
        loudness = loudness * jnp.repeat(heights, shape[axis_at] // parts).reshape([-1 if axis == axis_at else 1 for axis in range(len(shape))])
    return loudness


def centred(rng, dims, scale, limit, cuts=(), kind=jnp.bfloat16):
    array = jax.random.normal(rng, dims, jnp.float32) * scale
    if len(cuts) > 0:
        array = steps_of(rng, dims, cuts, -0.22, 0.18) * array
    return jnp.clip(array, min=-limit, max=limit).astype(kind)


def setup_inputs(seed: int = 0) -> dict:
    streams_of = jax.random.split(jax.random.key(seed), 16)
    hidden_in = centred(streams_of[0], (TOKENS, D), 1.0, 6.0, ((0, 128),))
    out_grad = centred(streams_of[1], (TOKENS, D), 1.0, 6.0, ((0, 128),))
    segment_ids = draw_segment_ids(jax.random.fold_in(streams_of[15], 71), 0)
    first_gain = jnp.clip(1.0 + 0.15 * jax.random.normal(streams_of[3], (D,), jnp.float32), 0.25, 1.75).astype(jnp.bfloat16)
    first_shift = centred(streams_of[4], (D,), 0.3, 1.75, ((0, 8),))
    second_gain = jnp.clip(1.0 + 0.15 * jax.random.normal(streams_of[5], (D,), jnp.float32), 0.25, 1.75).astype(jnp.bfloat16)
    second_shift = centred(streams_of[6], (D,), 0.3, 1.75, ((0, 8),))
    qkv_weight = centred(streams_of[7], (D, 3 * D), D ** -0.5, 0.1875, ((0, 8),))
    qkv_bias = centred(streams_of[8], (3 * D,), 0.3, 1.75, ((0, 8),))
    dense_weight = centred(streams_of[9], (D, D), (max(D // 128, 1)) ** -0.5, 2.0, ((0, 8),))
    dense_bias = centred(streams_of[10], (D,), 0.3, 1.75, ((0, 8),))
    up_weight = centred(streams_of[11], (D, FF), D ** -0.5, 0.1875, ((0, 8),))
    up_bias = centred(streams_of[12], (FF,), 0.3, 1.75, ((0, 8),))
    down_weight = centred(streams_of[13], (FF, D), FF ** -0.5, 0.09375, ((0, 8),))
    down_bias = centred(streams_of[14], (D,), 0.3, 1.75, ((0, 8),))
    return dict(hidden_in=hidden_in, out_grad=out_grad, segment_ids=segment_ids, first_gain=first_gain, first_shift=first_shift, second_gain=second_gain, second_shift=second_shift, qkv_weight=qkv_weight, qkv_bias=qkv_bias, dense_weight=dense_weight, dense_bias=dense_bias, up_weight=up_weight, up_bias=up_bias, down_weight=down_weight, down_bias=down_bias)


@jax.custom_vjp
def low(v):
    return lax.optimization_barrier(v.astype(jnp.bfloat16)).astype(jnp.float32)

@jax.custom_vjp
def low_back(v):
    return v

def low_keep(v):
    return (low(v), None)

def low_pass(kept, grad):
    return (grad,)

def back_keep(v):
    return (v, None)

def back_low(kept, grad):
    return (low(grad),)
low.defvjp(low_keep, low_pass)
low_back.defvjp(back_keep, back_low)

def matmul(left, right):
    return jnp.dot(left, right, precision=lax.Precision.HIGHEST, preferred_element_type=jnp.float32)

def layer_norm(values, gain, shift):
    center = values - lax.optimization_barrier(jnp.mean(values, axis=-1, keepdims=True))
    spread = lax.optimization_barrier(jnp.mean(center * center, axis=-1, keepdims=True))
    return center * lax.rsqrt(spread + 1e-05) * gain + shift

def angle_tables(positions, rotary):
    inverse = jnp.power(10000.0, -jnp.arange(0, rotary, 2, dtype=jnp.float32) / rotary)
    angles = positions[:, None] * inverse[None, :]
    doubled = jnp.concatenate([angles, angles], axis=1)
    return (jnp.cos(doubled), jnp.sin(doubled))

def rotate(tensor, cosine, sine):
    rotary = cosine.shape[1]
    half = rotary // 2
    part = tensor[..., :rotary]
    turned = jnp.concatenate([-part[..., half:], part[..., :half]], axis=-1)
    moved = part * cosine[:, None, :] + turned * sine[:, None, :]
    return jnp.concatenate([moved, tensor[..., rotary:]], axis=-1)

def positions_of(local_ids, row_ids, places):
    starts = lax.optimization_barrier(jnp.sum((row_ids[None, :] < local_ids[:, None]).astype(jnp.int32), axis=1))
    return (places - starts).astype(jnp.float32)

def forward(params, hidden, row_ids):
    first_gain, first_shift, second_gain, second_shift, qkv_weight, qkv_bias, dense_weight, dense_bias, up_weight, up_bias, down_weight, down_bias = params
    length = hidden.shape[0]
    width = hidden.shape[1]
    size = width // HEADS
    normed1 = low(layer_norm(hidden, first_gain, first_shift))
    normed2 = low(layer_norm(hidden, second_gain, second_shift))
    mixed = low_back(matmul(normed1, qkv_weight) + qkv_bias)
    places = jnp.arange(length, dtype=jnp.int32)
    cosine, sine = angle_tables(positions_of(row_ids, row_ids, places), size // 4)
    queries = low(rotate(mixed[:, :width].reshape(length, HEADS, size), cosine, sine))
    keys = low(rotate(mixed[:, width:2 * width].reshape(length, HEADS, size), cosine, sine))
    values = low(mixed[:, 2 * width:].reshape(length, HEADS, size))
    scores = jnp.einsum('qhd,khd->hqk', queries, keys, precision=lax.Precision.HIGHEST) * size ** (-0.5)
    allowed = (row_ids[None, :] == row_ids[:, None]) & (places[None, :] <= places[:, None])
    scores = low_back(jnp.where(allowed[None], scores, -1000000000.0))
    probs = low(jax.nn.softmax(scores, axis=-1))
    context = jnp.einsum('hqk,khd->qhd', probs, values, precision=lax.Precision.HIGHEST).reshape(length, width)
    context = low_back(low(context))
    attended = matmul(context, dense_weight) + dense_bias
    gate = low_back(matmul(normed2, up_weight) + up_bias)
    active = low(jax.nn.gelu(gate, approximate=False))
    return hidden + attended + matmul(active, down_weight) + down_bias

def reference(hidden_in, out_grad, segment_ids, first_gain, first_shift, second_gain, second_shift, qkv_weight, qkv_bias, dense_weight, dense_bias, up_weight, up_bias, down_weight, down_bias):
    params = (first_gain.astype(jnp.float32), first_shift.astype(jnp.float32), second_gain.astype(jnp.float32), second_shift.astype(jnp.float32), qkv_weight.astype(jnp.float32), qkv_bias.astype(jnp.float32), dense_weight.astype(jnp.float32), dense_bias.astype(jnp.float32), up_weight.astype(jnp.float32), up_bias.astype(jnp.float32), down_weight.astype(jnp.float32), down_bias.astype(jnp.float32))
    width = hidden_in.shape[1]
    packed = segment_ids.shape[0] // LEN
    hidden = hidden_in.astype(jnp.float32).reshape(packed, LEN, width)
    cotangent = out_grad.astype(jnp.float32).reshape(packed, LEN, width)
    row_table = segment_ids.reshape(packed, LEN)

    def add_pair(first, second):
        return first + second

    def one_row(totals, item):
        row_hidden, row_cotangent, row_ids = item

        def local_forward(weights, inputs):
            return forward(weights, inputs, row_ids)
        result, pullback = jax.vjp(local_forward, params, row_hidden)
        grads, input_grads = pullback(row_cotangent)
        totals = jax.tree.map(add_pair, totals, grads)
        return (totals, (result, input_grads))
    zeros = tuple((jnp.zeros_like(param) for param in params))
    totals, (results, input_grads) = lax.scan(one_row, zeros, (hidden, cotangent, row_table))
    return (results.reshape(packed * LEN, width).astype(jnp.bfloat16), input_grads.reshape(packed * LEN, width).astype(jnp.bfloat16), totals[0], totals[1], totals[2], totals[3], totals[4], totals[5], totals[6], totals[7], totals[8], totals[9], totals[10], totals[11])
```

```python
import functools

import jax
import jax.numpy as jnp
from jax import lax
from jax.experimental import pallas as pl
from jax.experimental.pallas import tpu as pltpu
from jax.sharding import PartitionSpec as P

BF = jnp.bfloat16
F32 = jnp.float32
MESH = pl.DeviceIdType.MESH
SEMS = 176


def flip(value, mask):
    out = value
    bit = 1
    while bit <= mask:
        if mask & bit:
            out = out + bit - 2 * bit * lax.rem(lax.div(value, bit), 2)
        bit *= 2
    return out


def nt(left, right):
    return lax.dot_general(left, right, (((1,), (1,)), ((), ())), preferred_element_type=F32)


def nn(left, right):
    return jnp.dot(left, right, preferred_element_type=F32)


def fold(block):
    return jnp.sum(block.reshape(block.shape[0] // 8, 8, block.shape[1]), axis=0)


def kernel(
    hid_ref, g_ref, seg_ref, pack_ref, wqkv_ref, wup_ref, wdense_ref, wdown_ref,
    out_ref, ing_ref, f1_ref, f2_ref, f3_ref, gvec_ref,
    HB, GB, SG, PK, WQ, WU, VEC, B24, XH, N1, N2, QKP, TAB, START, QTM, QM, KT, K, V, VT,
    GP, ACT, ACTT, PT, CTXT, CTX, DCM, DCTM, DG, DGT, DQT, DK, DV, M, MT,
    PB, PRA, PRB, PRX, PRZ, PTX, PUB, DB, DRA, DRB, DRX, DRZ, DTX, DUB, ACC,
    G1, X1, C1, R1, S1, G2, X2, C2, R2, S2, A2, G3, X3, C3, R3, S3, A3,
    SUMS, CG, CDG, SV, SVR, LV, LVX, LC, LCR,
    ssem, rsem, lsem,
):
    r = lax.axis_index("rep")
    s = lax.axis_index("shard")
    c = lax.rem(r, 2)
    chip = lax.div(r, 2)
    z = lax.div(s, 2)
    l = lax.rem(s, 2)
    other = 1 - l
    half = lax.rem(c + s, 2)

    def shard_to(k):
        return {"shard": flip(s, k)}

    def chip_to(k):
        return {"rep": flip(chip, k) * 2 + c}

    partner = {"rep": chip * 2 + 1 - c}
    zk = [None] + [flip(z, k) for k in (1, 2, 3)]

    barrier = pltpu.get_barrier_semaphore()
    peers = [shard_to(k) for k in range(1, 8)] + [chip_to(k) for k in range(1, 8)] + [partner]
    for peer in peers:
        pl.semaphore_signal(barrier, inc=1, device_id=peer, device_id_type=MESH)
    pl.semaphore_wait(barrier, len(peers))

    used = [0]
    sent = []

    def remote(src, dst, device):
        at = used[0]
        used[0] += 1
        copy = pltpu.make_async_remote_copy(
            src_ref=src, dst_ref=dst, send_sem=ssem.at[at], recv_sem=rsem.at[at],
            device_id=device, device_id_type=MESH,
        )
        copy.start()
        sent.append(copy)
        return copy

    def lanes(start, size):
        return pl.ds(pl.multiple_of(start, 128), size)

    def rows(start, size):
        return pl.ds(pl.multiple_of(start, 16), size)

    def gather_start(x_ref, XB):
        first = remote(x_ref.at[0:64], XB.at[z, l, 0:64], shard_to(1))
        whole = [remote(x_ref, XB.at[z, l], shard_to(2 * k)) for k in (1, 3, 2)]
        last = remote(x_ref.at[64:128], XB.at[z, l, 64:128], shard_to(1))
        return XB, first, whole, last

    def gather_forward(state):
        XB, first, whole, last = state
        first.wait_recv()
        rest = [last]
        for k in (1, 3, 2):
            rest.append(remote(XB.at[z, other, 0:64], XB.at[z, other, 0:64], shard_to(2 * k)))
        for copy, k in zip(whole, (1, 3, 2)):
            copy.wait_recv()
            rest.append(remote(XB.at[zk[k], l, 64:128], XB.at[zk[k], l, 64:128], shard_to(1)))
        return rest

    def arrived(copies):
        for copy in copies:
            copy.wait_recv()

    small = [remote(pack_ref, PK.at[s], shard_to(k)) for k in range(1, 8)]
    small += [remote(seg_ref, SG.at[s], shard_to(k)) for k in range(1, 8)]
    part = rows(64 * c, 64)
    gather_h = gather_start(hid_ref, HB)
    weights = []
    for k in range(1, 8):
        sp = flip(s, k)
        for j in range(3):
            weights.append(remote(
                wqkv_ref.at[part, lanes(1024 * j + 128 * sp, 128)],
                WQ.at[s, part, 128 * j : 128 * j + 128], shard_to(k)))
        weights.append(remote(wup_ref.at[part, lanes(512 * sp, 512)], WU.at[s, part], shard_to(k)))
    local = []
    for j in range(3):
        local.append(pltpu.make_async_copy(
            wqkv_ref.at[part, lanes(1024 * j + 128 * s, 128)],
            WQ.at[s, part, 128 * j : 128 * j + 128], lsem.at[j]))
    local.append(pltpu.make_async_copy(wup_ref.at[part, lanes(512 * s, 512)], WU.at[s, part], lsem.at[3]))
    for copy in local:
        copy.start()
    HB[z, l] = hid_ref[...]
    GB[z, l] = g_ref[...]
    PK[s] = pack_ref[...]
    SG[s] = seg_ref[...]
    rest_h = gather_forward(gather_h)
    for copy in local:
        copy.wait()
    arrived(weights)
    across = [remote(WQ.at[:, part], WQ.at[:, part], partner), remote(WU.at[:, part], WU.at[:, part], partner)]
    gather_g = gather_start(g_ref, GB)

    arrived(small)
    for sp in range(8):
        block = PK[sp].astype(F32)
        at = slice(128 * sp, 128 * sp + 128)
        for j in range(4):
            VEC[j : j + 1, at] = block[j : j + 1]
        VEC[4:5, at] = block[7:8] + block[12:13]
        B24[3 * sp : 3 * sp + 3] = block[4:7]
    own = PK[s].astype(F32)
    bias_up = jnp.concatenate([own[8 + j : 9 + j] for j in range(4)], axis=1)
    bias_q = jnp.concatenate([B24[pl.ds(8 * j + s, 1)] for j in range(3)], axis=1)
    own_bias = own[7:8] + own[12:13]
    del own_bias
    seg_row = jnp.concatenate([SG[sp, 0:1] for sp in range(8)], axis=1).astype(F32)
    count = jnp.zeros((1, 1024), F32)
    for sp in range(8):
        column = jnp.transpose(jnp.broadcast_to(SG[sp, 0:1].astype(F32), (128, 128)))[:, 0:1]
        count = count + jnp.sum((column < seg_row).astype(F32), axis=0, keepdims=True)
    START[...] = jnp.broadcast_to(count.astype(jnp.int32), (8, 1024))
    place = lax.broadcasted_iota(jnp.int32, (8, 1024), 1).astype(F32)
    row8 = lax.broadcasted_iota(jnp.int32, (8, 1024), 0)
    inverse = jnp.zeros((8, 1024), F32)
    for j in range(8):
        inverse = jnp.where(row8 == j, 10000.0 ** (-j / 8.0), inverse)
    angles = (place - count) * inverse
    TAB[0] = jnp.cos(angles)
    TAB[1] = jnp.sin(angles)
    arrived(rest_h)
    arrived(across)

    gain1, shift1, gain2, shift2 = (VEC[j : j + 1] for j in range(4))

    @pl.loop(0, 4)
    def _(i):
        at = rows(256 * i, 256)
        cols = lanes(256 * i, 256)
        block = HB[i].reshape(256, 1024).astype(F32)
        center = block - jnp.mean(block, axis=-1, keepdims=True)
        spread = jnp.mean(center * center, axis=-1, keepdims=True)
        xhat = center * lax.rsqrt(spread + 1e-05)
        XH[at] = xhat.astype(BF)
        n1 = (xhat * gain1 + shift1).astype(BF)
        n2 = (xhat * gain2 + shift2).astype(BF)
        N1[at] = n1
        N2[at] = n2
        mixed = nn(n1, WQ[...].reshape(1024, 384)) + bias_q
        QKP[:, cols] = jnp.transpose(mixed[:, :256])
        V[at] = mixed[:, 256:].astype(BF)
        VT[:, cols] = jnp.transpose(mixed[:, 256:]).astype(BF)
        gate = nn(n2, WU[...].reshape(1024, 512)) + bias_up
        phi = 0.5 + 0.5 * lax.erf(gate * 0.7071067811865476)
        GP[at] = phi + gate * jnp.exp(-0.5 * gate * gate) * 0.3989422804014327
        active = gate * phi
        ACT[at] = active.astype(BF)
        ACTT[:, cols] = jnp.transpose(active).astype(BF)

    rest_g = gather_forward(gather_g)

    cosine = TAB[0]
    sine = TAB[1]
    for base in (0, 64, 128, 192):
        one = QKP[base : base + 8]
        two = QKP[base + 8 : base + 16]
        QKP[base : base + 8] = one * cosine - two * sine
        QKP[base + 8 : base + 16] = two * cosine + one * sine
    queries = QKP[0:128].astype(BF).astype(F32) * 0.125
    keys = QKP[128:256]
    low_rows = lax.broadcasted_iota(jnp.int32, (128, 1024), 0) < 64
    low_cols = lax.broadcasted_iota(jnp.int32, (1024, 128), 1) < 64
    QTM[0] = jnp.where(low_rows, queries, 0.0).astype(BF)
    QTM[1] = jnp.where(low_rows, 0.0, queries).astype(BF)
    back = jnp.transpose(queries)
    QM[0] = jnp.where(low_cols, back, 0.0).astype(BF)
    QM[1] = jnp.where(low_cols, 0.0, back).astype(BF)
    KT[...] = keys.astype(BF)
    K[...] = jnp.transpose(keys).astype(BF)

    @pl.loop(0, 2)
    def _(head):
        hr = rows(64 * head, 64)
        for j in range(4):
            top = 256 * (j + 1)
            q = slice(256 * j, 256 * j + 256)
            scores = nn(K[0:top], QTM[head, :, q])
            ki = lax.broadcasted_iota(jnp.int32, (top, 256), 0)
            qi = lax.broadcasted_iota(jnp.int32, (top, 256), 1) + 256 * j
            allowed = (ki <= qi) & (ki >= START[0:1, q])
            scores = jnp.where(allowed, scores, -1e9)
            weight = jnp.exp(scores - jnp.max(scores, axis=0, keepdims=True))
            probs = (weight * (1.0 / jnp.sum(weight, axis=0, keepdims=True))).astype(BF)
            PT[head, 0:top, q] = probs
            CTXT[hr, q] = nn(VT[hr, 0:top], probs).astype(BF)

    CTX[...] = jnp.transpose(CTXT[...].astype(F32)).astype(BF)

    def scatter_start(TB, RA, RB):
        a = [remote(TB.at[zk[k], :, 0:64], RA.at[k - 1], shard_to(2 * k)) for k in (1, 3, 2)]
        b = remote(TB.at[:, other, 64:128], RB, shard_to(1))
        return a, b

    def scatter_middle(state, TB, RA, RB, RX, RZ, TX, UB):
        a, b = state
        arrived(a)
        TX[...] = (
            TB[z, other, 0:64].astype(F32) + RA[0, other].astype(F32)
            + RA[1, other].astype(F32) + RA[2, other].astype(F32)
        ).astype(BF)
        out = [remote(TX, RX, shard_to(1))]
        b.wait_recv()
        for k in (1, 3, 2):
            UB[k - 1] = (TB[zk[k], l, 64:128].astype(F32) + RB[zk[k]].astype(F32)).astype(BF)
            out.append(remote(UB.at[k - 1], RZ.at[k - 1], shard_to(2 * k)))
        return out

    def scatter_end(out, TB, RA, RB, RX, RZ):
        arrived(out)
        ACC[0:64] = (
            TB[z, l, 0:64].astype(F32) + RA[0, l].astype(F32) + RA[1, l].astype(F32)
            + RA[2, l].astype(F32) + RX[...].astype(F32)
        )
        ACC[64:128] = (
            TB[z, l, 64:128].astype(F32) + RB[z].astype(F32) + RZ[0].astype(F32)
            + RZ[1].astype(F32) + RZ[2].astype(F32)
        )

    @pl.loop(0, 4)
    def _(i):
        at = rows(256 * i, 256)
        total = nn(CTX[at], wdense_ref[...]) + nn(ACT[at], wdown_ref[...])
        PB[i] = total.astype(BF).reshape(2, 128, 1024)

    out_state = scatter_start(PB, PRA, PRB)
    arrived(rest_g)

    CG[...] = jnp.zeros_like(CG)
    CDG[...] = jnp.zeros_like(CDG)
    low_256 = lax.broadcasted_iota(jnp.int32, (256, 128), 1) < 64
    low_t256 = lax.broadcasted_iota(jnp.int32, (128, 256), 0) < 64

    @pl.loop(0, 4)
    def _(i):
        at = rows(256 * i, 256)
        cols = lanes(256 * i, 256)
        block = GB[i].reshape(256, 1024)
        CG[...] += fold(block.astype(F32))
        grad = nt(block, wdense_ref[...])
        DCM[0, at] = jnp.where(low_256, grad, 0.0).astype(BF)
        DCM[1, at] = jnp.where(low_256, 0.0, grad).astype(BF)
        turned = jnp.transpose(grad)
        DCTM[0, :, cols] = jnp.where(low_t256, turned, 0.0).astype(BF)
        DCTM[1, :, cols] = jnp.where(low_t256, 0.0, turned).astype(BF)
        gate_grad = (nt(block, wdown_ref[...]) * GP[at]).astype(BF)
        DG[at] = gate_grad
        wide = gate_grad.astype(F32)
        CDG[...] += fold(wide)
        DGT[:, cols] = jnp.transpose(wide).astype(BF)

    mine = half

    def pair_start(GR, X):
        return remote(GR.at[:, lanes(512 * (1 - mine), 512)], X, partner)

    def spread_start(pair, GR, X, C, R, size):
        pair.wait_recv()
        C[...] = (GR[:, lanes(512 * mine, 512)].astype(F32) + X[...].astype(F32)).astype(BF)
        return [
            remote(C.at[rows(size * flip(chip, k), size)], R.at[k - 1], chip_to(k)) for k in range(1, 8)
        ]

    def spread_sum(copies, C, R, S, size):
        arrived(copies)
        total = C[rows(size * chip, size)].astype(F32)
        for k in range(7):
            total = total + R[k].astype(F32)
        S[...] = total.astype(BF)

    grads = GB[...].reshape(1024, 1024)
    G1[0:512] = nn(ACTT[...], grads).astype(BF)
    G1[512:640] = nn(CTXT[...], grads).astype(BF)
    pair1 = pair_start(G1, X1)
    G2[...] = nn(DGT[...], N2[...]).astype(BF)
    pair2 = pair_start(G2, X2)
    spread1 = spread_start(pair1, G1, X1, C1, R1, 80)
    out_rest = scatter_middle(out_state, PB, PRA, PRB, PRX, PRZ, PTX, PUB)
    spread2 = spread_start(pair2, G2, X2, C2, R2, 64)

    DK[...] = jnp.zeros_like(DK)
    DV[...] = jnp.zeros_like(DV)

    @pl.loop(0, 2)
    def _(head):
        hr = rows(64 * head, 64)
        for j in range(4):
            top = 256 * (j + 1)
            q = slice(256 * j, 256 * j + 256)
            probs = PT[head, 0:top, q]
            soft = probs.astype(F32)
            probs_grad = nn(V[0:top], DCTM[head, :, q])
            middle = jnp.sum(soft * probs_grad, axis=0, keepdims=True)
            score_grad = (soft * (probs_grad - middle)).astype(BF)
            DQT[hr, q] = nn(KT[hr, 0:top], score_grad) * 0.125
            DK[0:top] += nn(score_grad, QM[head, q])
            DV[0:top] += nn(probs, DCM[head, q])

    dk = jnp.transpose(DK[...])
    QKP[0:128] = DQT[...]
    QKP[128:256] = dk
    for base in (0, 64, 128, 192):
        one = QKP[base : base + 8]
        two = QKP[base + 8 : base + 16]
        QKP[base : base + 8] = one * cosine + two * sine
        QKP[base + 8 : base + 16] = two * cosine - one * sine
    MT[0:256] = QKP[...].astype(BF)
    MT[256:384] = jnp.transpose(DV[...]).astype(BF)
    M[:, 0:256] = jnp.transpose(QKP[...]).astype(BF)
    M[:, 256:384] = DV[...].astype(BF)
    G3[...] = nn(MT[...], N1[...]).astype(BF)
    pair3 = pair_start(G3, X3)

    SUMS[...] = jnp.zeros_like(SUMS)

    @pl.loop(0, 4)
    def _(i):
        at = rows(256 * i, 256)
        xhat = XH[at].astype(F32)
        one = nt(M[at], WQ[...].reshape(1024, 384))
        two = nt(DG[at], WU[...].reshape(1024, 512))
        DB[i] = (one * gain1 + two * gain2).astype(BF).reshape(2, 128, 1024)
        SUMS[0] += fold(one * xhat)
        SUMS[1] += fold(one)
        SUMS[2] += fold(two * xhat)
        SUMS[3] += fold(two)

    in_state = scatter_start(DB, DRA, DRB)

    SV[...] = jnp.zeros_like(SV)
    bias_grad = jnp.sum(fold(M[...].astype(F32)), axis=0, keepdims=True)
    B24[...] = jnp.zeros_like(B24)
    for j in range(3):
        B24[pl.ds(8 * j + s, 1)] = bias_grad[:, 128 * j : 128 * j + 128]
    for sp in range(8):
        at = slice(128 * sp, 128 * sp + 128)
        for j in range(4):
            SV[sp, j : j + 1] = jnp.sum(SUMS[j, :, at], axis=0, keepdims=True)
        SV[sp, 4:7] = B24[3 * sp : 3 * sp + 3]
    vectors = [remote(SV.at[flip(s, k)], SVR.at[k - 1], shard_to(k)) for k in range(1, 8)]

    spread3 = spread_start(pair3, G3, X3, C3, R3, 48)

    def give(S, out, size):
        at = rows(size * chip, size)
        out[at, lanes(512 * mine, 512)] = S[...]
        return [
            remote(S, out.at[at, lanes(512 * mine, 512)], chip_to(k)) for k in range(1, 8)
        ]

    spread_sum(spread1, C1, R1, S1, 80)
    give1 = give(S1, f1_ref, 80)

    source = lax.rem(lax.div(s, 4) + c, 2)

    def turn(S, A, size):
        base = used[0]
        used[0] += 4
        slot = lax.div(s, 2)

        def descriptor(m, device):
            return pltpu.make_async_remote_copy(
                src_ref=S.at[:, 128 * m : 128 * m + 128], dst_ref=A.at[slot],
                send_sem=ssem.at[base + m], recv_sem=rsem.at[base + slot],
                device_id={"shard": device}, device_id_type=MESH,
            )

        for m in range(4):
            device = 4 * half + m

            @pl.when(device != s)
            def _():
                descriptor(m, device).start()

            @pl.when(device == s)
            def _():
                A[slot] = S[:, 128 * m : 128 * m + 128]

        return base

    def turned(base, S, A, size):
        for m in range(4):
            @pl.when(4 * half + m != s)
            def _():
                pltpu.make_async_remote_copy(
                    src_ref=S.at[:, 128 * m : 128 * m + 128], dst_ref=A.at[m],
                    send_sem=ssem.at[base + m], recv_sem=rsem.at[base + m],
                    device_id={"shard": flip(s, 1)}, device_id_type=MESH,
                ).wait_send()

            @pl.when(2 * m + source != s)
            def _():
                pltpu.make_async_remote_copy(
                    src_ref=S.at[:, 128 * m : 128 * m + 128], dst_ref=A.at[m],
                    send_sem=ssem.at[base + m], recv_sem=rsem.at[base + m],
                    device_id={"shard": flip(s, 1)}, device_id_type=MESH,
                ).wait_recv()

    def give_turned(A, out, size):
        at = rows(size * chip, size)
        out[source, :, at] = A[...]
        return [remote(A, out.at[source, :, at], chip_to(k)) for k in range(1, 8)]

    spread_sum(spread2, C2, R2, S2, 64)
    turn2 = turn(S2, A2, 64)
    out_end = out_rest
    scatter_end(out_end, PB, PRA, PRB, PRX, PRZ)
    out_ref[...] = (hid_ref[...].astype(F32) + ACC[...] + VEC[4:5]).astype(BF)

    in_rest = scatter_middle(in_state, DB, DRA, DRB, DRX, DRZ, DTX, DUB)
    turned(turn2, S2, A2, 64)
    give2 = give_turned(A2, f2_ref, 64)

    spread_sum(spread3, C3, R3, S3, 48)
    turn3 = turn(S3, A3, 48)
    arrived(vectors)
    LV[...] = jnp.zeros_like(LV)
    total = SV[s]
    for k in range(7):
        total = total + SVR[k]
    LV[0:7] = total[0:7]
    up_grad = jnp.sum(CDG[...], axis=0, keepdims=True)
    for j in range(4):
        LV[8 + j : 9 + j] = up_grad[:, 128 * j : 128 * j + 128]
    LV[12:13] = jnp.sum(CG[:, lanes(128 * s, 128)], axis=0, keepdims=True)
    pair_v = remote(LV, LVX, partner)

    turned(turn3, S3, A3, 48)
    give3 = give_turned(A3, f3_ref, 48)
    pair_v.wait_recv()
    LC[...] = LV[...] + LVX[...]
    LCR[chip] = LC[...]
    spread_v = [remote(LC, LCR.at[chip], chip_to(k)) for k in range(1, 8)]

    arrived(give1)
    last1 = remote(f1_ref.at[:, lanes(512 * mine, 512)], f1_ref.at[:, lanes(512 * mine, 512)], partner)
    arrived(give2)
    last2 = remote(f2_ref.at[source], f2_ref.at[source], partner)

    scatter_end(in_rest, DB, DRA, DRB, DRX, DRZ)
    block = hid_ref[...].astype(F32)
    center = block - jnp.mean(block, axis=-1, keepdims=True)
    spread = jnp.mean(center * center, axis=-1, keepdims=True)
    scale = lax.rsqrt(spread + 1e-05)
    xhat = center * scale
    grad = ACC[...]
    grad = grad - jnp.mean(grad, axis=-1, keepdims=True) - xhat * jnp.mean(grad * xhat, axis=-1, keepdims=True)
    ing_ref[...] = (g_ref[...].astype(F32) + scale * grad).astype(BF)

    arrived(spread_v)
    total = LCR[0]
    for k in range(1, 8):
        total = total + LCR[k]
    gvec_ref[...] = total

    arrived(give3)
    last3 = remote(f3_ref.at[source], f3_ref.at[source], partner)
    arrived([last1, last2, last3])
    for copy in sent:
        copy.wait_send()
    assert used[0] <= SEMS, used[0]


def block_call(*args):
    vm = pltpu.VMEM
    scratch = [
        vm((4, 2, 128, 1024), BF), vm((4, 2, 128, 1024), BF), vm((8, 8, 128), jnp.int32), vm((8, 16, 128), BF),
        vm((8, 128, 384), BF), vm((8, 128, 512), BF), vm((8, 1024), F32), vm((24, 128), F32),
        vm((1024, 1024), BF), vm((1024, 1024), BF), vm((1024, 1024), BF), vm((256, 1024), F32),
        vm((2, 8, 1024), F32), vm((8, 1024), jnp.int32),
        vm((2, 128, 1024), BF), vm((2, 1024, 128), BF), vm((128, 1024), BF), vm((1024, 128), BF),
        vm((1024, 128), BF), vm((128, 1024), BF),
        vm((1024, 512), F32), vm((1024, 512), BF), vm((512, 1024), BF), vm((2, 1024, 1024), BF),
        vm((128, 1024), BF), vm((1024, 128), BF), vm((2, 1024, 128), BF), vm((2, 128, 1024), BF),
        vm((1024, 512), BF), vm((512, 1024), BF), vm((128, 1024), F32), vm((1024, 128), F32), vm((1024, 128), F32),
        vm((1024, 384), BF), vm((384, 1024), BF),
    ]
    for _ in range(2):
        scratch += [
            vm((4, 2, 128, 1024), BF), vm((3, 2, 64, 1024), BF), vm((4, 64, 1024), BF), vm((64, 1024), BF),
            vm((3, 64, 1024), BF), vm((64, 1024), BF), vm((3, 64, 1024), BF),
        ]
    scratch += [vm((128, 1024), F32)]
    scratch += [vm((640, 1024), BF), vm((640, 512), BF), vm((640, 512), BF), vm((7, 80, 512), BF), vm((80, 512), BF)]
    for size in (64, 48):
        scratch += [
            vm((8 * size, 1024), BF), vm((8 * size, 512), BF), vm((8 * size, 512), BF), vm((7, size, 512), BF),
            vm((size, 512), BF), vm((4, size, 128), BF),
        ]
    scratch += [
        vm((4, 8, 1024), F32), vm((8, 1024), F32), vm((8, 512), F32), vm((8, 16, 128), F32), vm((7, 16, 128), F32),
        vm((16, 128), F32), vm((16, 128), F32), vm((16, 128), F32), vm((8, 16, 128), F32),
        pltpu.SemaphoreType.DMA((SEMS,)), pltpu.SemaphoreType.DMA((SEMS,)), pltpu.SemaphoreType.DMA((4,)),
    ]
    return pl.pallas_call(
        kernel,
        out_shape=(
            jax.ShapeDtypeStruct((128, 1024), BF), jax.ShapeDtypeStruct((128, 1024), BF),
            jax.ShapeDtypeStruct((640, 1024), BF), jax.ShapeDtypeStruct((2, 4, 512, 128), BF),
            jax.ShapeDtypeStruct((2, 4, 384, 128), BF), jax.ShapeDtypeStruct((16, 128), F32),
        ),
        in_specs=[pl.BlockSpec(memory_space=pltpu.VMEM)] * 8,
        out_specs=[pl.BlockSpec(memory_space=pltpu.VMEM)] * 6,
        scratch_shapes=scratch,
        compiler_params=pltpu.CompilerParams(
            collective_id=0, has_side_effects=True, vmem_limit_bytes=62 * 2**20
        ),
    )(*args)


def shards(
    hidden_in, out_grad, segment_ids, first_gain, first_shift, second_gain, second_shift,
    qkv_weight, qkv_bias, dense_weight, dense_bias, up_weight, up_bias, down_weight, down_bias,
):
    pack = jnp.concatenate([
        first_gain, first_shift, second_gain, second_shift, qkv_bias, dense_bias, up_bias, down_bias,
        jnp.zeros((384,), BF),
    ]).reshape(16, 128)
    seg = jnp.broadcast_to(segment_ids.reshape(1, 128), (8, 128))
    out, ing, first, second, third, vectors = block_call(
        hidden_in, out_grad, seg, pack, qkv_weight, up_weight, dense_weight, down_weight
    )
    third = third.astype(F32).reshape(2, 4, 3, 128, 128)
    grad_qkv = jnp.transpose(third, (4, 2, 1, 0, 3)).reshape(128, 3072)
    grad_up = jnp.transpose(second.astype(F32), (3, 1, 0, 2)).reshape(128, 4096)
    first = first.astype(F32)
    return (
        out, ing, vectors[0], vectors[1], vectors[2], vectors[3],
        grad_qkv, vectors[4:7].reshape(384),
        first[512:640], vectors[12],
        grad_up, vectors[8:12].reshape(512),
        first[0:512], vectors[12],
    )


def solution(mesh):
    both, one, wide = P(("rep", "shard"), None), P("shard"), P("shard", None)
    placed = (
        both, both, P(("rep", "shard")), one, one, one, one, wide, one, wide, one, wide, one, wide, one,
    )
    return jax.shard_map(
        shards, mesh=mesh, in_specs=placed,
        out_specs=(both, both, one, one, one, one, wide, one, wide, one, wide, one, wide, one),
        check_vma=False,
    )
```

```python
import functools

import jax
import jax.numpy as jnp
from jax import lax
from jax.experimental import pallas as pl
from jax.experimental.pallas import tpu as pltpu
from jax.sharding import PartitionSpec as P

BF = jnp.bfloat16
F32 = jnp.float32
MESH = pl.DeviceIdType.MESH
SEMS = 176


def flip(value, mask):
    out = value
    bit = 1
    while bit <= mask:
        if mask & bit:
            out = out + bit - 2 * bit * lax.rem(lax.div(value, bit), 2)
        bit *= 2
    return out


def nt(left, right):
    return lax.dot_general(left, right, (((1,), (1,)), ((), ())), preferred_element_type=F32)


def nn(left, right):
    return jnp.dot(left, right, preferred_element_type=F32)


def fold(block):
    return jnp.sum(block.reshape(block.shape[0] // 8, 8, block.shape[1]), axis=0)


def kernel(
    hid_ref, g_ref, seg_ref, gain1_ref, shift1_ref, gain2_ref, shift2_ref, wqkv_ref, bqkv_ref, wdense_ref,
    bdense_ref, wup_ref, bup_ref, wdown_ref, bdown_ref,
    out_ref, ing_ref, f1_ref, o2_ref, o3_ref, v1_ref, v2_ref, v3_ref, v4_ref, vq_ref, vd_ref, vu_ref, vw_ref,
    f2_ref, f3_ref, PKO, SGO, WD, WN,
    HB, GB, SG, PK, WQ, WU, VEC, B24, XH, N1, N2, QKP, TAB, START, QTM, QM, KT, K, V, VT,
    GP, ACT, ACTT, PT, CTXT, CTX, DCM, DCTM, DG, DGT, DQT, DK, DV, M, MT,
    PB, PRA, PRB, PRX, PRZ, PTX, PUB, DB, DRA, DRB, DRX, DRZ, DTX, DUB, ACC,
    G1, X1, C1, R1, S1, G2, X2, C2, R2, S2, A2, G3, X3, C3, R3, S3, A3,
    SUMS, CG, CDG, SV, SVR, LV, LVX, LC, LCR,
    ssem, rsem, lsem,
):
    r = lax.axis_index("rep")
    s = lax.axis_index("shard")
    c = lax.rem(r, 2)
    chip = lax.div(r, 2)
    y = lax.rem(chip, 4)
    z = lax.div(s, 2)
    l = lax.rem(s, 2)
    other = 1 - l
    half = lax.rem(c + s, 2)
    ahead = lax.rem(z + 1, 4)
    behind = lax.rem(z + 3, 4)
    across_z = lax.rem(z + 2, 4)

    def shard_to(k):
        return {"shard": flip(s, k)}

    def chip_to(k):
        return {"rep": flip(chip, k) * 2 + c}

    partner = {"rep": chip * 2 + 1 - c}
    zk = [None] + [flip(z, k) for k in (1, 2, 3)]

    def lanes(start, size):
        return pl.ds(pl.multiple_of(start, 128), size)

    def rows(start, size):
        return pl.ds(pl.multiple_of(start, 16), size)

    barrier = pltpu.get_barrier_semaphore()
    peers = [shard_to(k) for k in range(1, 8)] + [chip_to(k) for k in range(1, 8)] + [partner]
    for peer in peers:
        pl.semaphore_signal(barrier, inc=1, device_id=peer, device_id_type=MESH)

    mine16 = rows(64 * c + 16 * y, 16)
    local = [
        pltpu.make_async_copy(hid_ref, HB.at[z, l], lsem.at[0]),
        pltpu.make_async_copy(g_ref, GB.at[z, l], lsem.at[1]),
        pltpu.make_async_copy(wdense_ref, WD, lsem.at[2]),
        pltpu.make_async_copy(wdown_ref, WN, lsem.at[3]),
        pltpu.make_async_copy(wup_ref.at[mine16, lanes(512 * s, 512)], WU.at[s, mine16], lsem.at[4]),
    ]
    for j in range(3):
        local.append(pltpu.make_async_copy(
            wqkv_ref.at[mine16, lanes(1024 * j + 128 * s, 128)],
            WQ.at[s, mine16, 128 * j : 128 * j + 128], lsem.at[5 + j]))
    for copy in local:
        copy.start()
    PKO[...] = jnp.zeros_like(PKO)
    at = 0
    for ref in (gain1_ref, shift1_ref, gain2_ref, shift2_ref, bqkv_ref, bdense_ref, bup_ref, bdown_ref):
        size = ref.shape[0] // 128
        PKO[at : at + size] = ref[...].astype(F32).reshape(size, 128)
        at += size
    PK[s] = PKO[...]
    SGO[...] = jnp.broadcast_to(seg_ref[...].reshape(1, 128), (8, 128))
    SG[s] = SGO[...]
    for copy in local:
        copy.wait()
    pl.semaphore_wait(barrier, len(peers))

    used = [0]
    sent = []

    def remote(src, dst, device):
        at = used[0]
        used[0] += 1
        copy = pltpu.make_async_remote_copy(
            src_ref=src, dst_ref=dst, send_sem=ssem.at[at], recv_sem=rsem.at[at],
            device_id=device, device_id_type=MESH,
        )
        copy.start()
        sent.append(copy)
        return copy

    def arrived(copies):
        for copy in copies:
            copy.wait_recv()

    up = {"shard": ahead * 2 + l}
    down = {"shard": behind * 2 + l}

    def pass_on(XB, zz, ll, part, device):
        return remote(XB.at[zz, ll, part], XB.at[zz, ll, part], device)

    def gather_start(x_ref, XB):
        first = remote(x_ref.at[0:64], XB.at[z, l, 0:64], shard_to(1))
        za = remote(x_ref, XB.at[z, l], up)
        zb = remote(x_ref, XB.at[z, l], down)
        last = remote(x_ref.at[64:128], XB.at[z, l, 64:128], shard_to(1))
        return XB, first, za, zb, last

    low = slice(0, 64)
    high = slice(64, 128)

    def gather_next(state):
        XB, first, za, zb, last = state
        first.wait_recv()
        xa = pass_on(XB, z, other, low, up)
        xb = pass_on(XB, z, other, low, down)
        za.wait_recv()
        d2a = pass_on(XB, behind, l, low, up)
        fa = pass_on(XB, behind, l, high, shard_to(1))
        zb.wait_recv()
        d2b = pass_on(XB, ahead, l, high, down)
        fb = pass_on(XB, ahead, l, high, shard_to(1))
        return XB, xa, xb, d2a, d2b, [last, fa, fb]

    def gather_last(state):
        XB, xa, xb, d2a, d2b, rest = state
        xa.wait_recv()
        x2a = pass_on(XB, behind, other, slice(0, 32), up)
        xb.wait_recv()
        x2b = pass_on(XB, ahead, other, slice(32, 64), down)
        d2b.wait_recv()
        fc = pass_on(XB, across_z, l, high, shard_to(1))
        return rest + [d2a, x2a, x2b, fc]

    def turn_weights(ref, W, width, blocks):
        copies = []
        for k in range(1, 8):
            for j in range(blocks):
                copies.append(remote(
                    ref.at[mine16, lanes(1024 * j + width * flip(s, k), width)],
                    W.at[s, mine16, width * j : width * j + width], shard_to(k)))
        return copies

    def along_y(W):
        return [remote(W.at[:, mine16], W.at[:, mine16], chip_to(k)) for k in (1, 3, 2)]

    mine64 = rows(64 * c, 64)
    turn_q = turn_weights(wqkv_ref, WQ, 128, 3)
    gather_h = gather_start(hid_ref, HB)
    turn_u = turn_weights(wup_ref, WU, 512, 1)
    small = [remote(PKO, PK.at[s], shard_to(k)) for k in range(1, 8)]
    small += [remote(SGO, SG.at[s], shard_to(k)) for k in range(1, 8)]
    arrived(turn_q)
    y_q = along_y(WQ)
    gather_h = gather_next(gather_h)
    arrived(turn_u)
    y_u = along_y(WU)
    rest_h = gather_last(gather_h)
    arrived(y_q)
    core_q = remote(WQ.at[:, mine64], WQ.at[:, mine64], partner)
    gather_g = gather_start(g_ref, GB)
    arrived(small)

    for sp in range(8):
        block = PK[sp]
        at = slice(128 * sp, 128 * sp + 128)
        for j in range(4):
            VEC[j : j + 1, at] = block[j : j + 1]
        VEC[4:5, at] = block[7:8] + block[12:13]
        B24[3 * sp : 3 * sp + 3] = block[4:7]
    own = PKO[...]
    bias_up = jnp.concatenate([own[8 + j : 9 + j] for j in range(4)], axis=1)
    bias_q = jnp.concatenate([B24[pl.ds(8 * j + s, 1)] for j in range(3)], axis=1)
    seg_row = jnp.concatenate([SG[sp, 0:1] for sp in range(8)], axis=1).astype(F32)
    count = jnp.zeros((1, 1024), F32)
    for sp in range(8):
        column = jnp.transpose(jnp.broadcast_to(SG[sp, 0:1].astype(F32), (128, 128)))[:, 0:1]
        count = count + jnp.sum((column < seg_row).astype(F32), axis=0, keepdims=True)
    START[...] = jnp.broadcast_to(count.astype(jnp.int32), (8, 1024))
    place = lax.broadcasted_iota(jnp.int32, (8, 1024), 1).astype(F32)
    row8 = lax.broadcasted_iota(jnp.int32, (8, 1024), 0)
    inverse = jnp.zeros((8, 1024), F32)
    for j in range(8):
        inverse = jnp.where(row8 == j, 10000.0 ** (-j / 8.0), inverse)
    angles = (place - count) * inverse
    TAB[0] = jnp.cos(angles)
    TAB[1] = jnp.sin(angles)
    arrived(y_u)
    core_u = remote(WU.at[:, mine64], WU.at[:, mine64], partner)
    arrived(rest_h)
    core_q.wait_recv()

    gain1, shift1, gain2, shift2 = (VEC[j : j + 1] for j in range(4))

    @pl.loop(0, 4)
    def _(i):
        at = rows(256 * i, 256)
        cols = lanes(256 * i, 256)
        block = HB[i].reshape(256, 1024).astype(F32)
        center = block - jnp.mean(block, axis=-1, keepdims=True)
        spread = jnp.mean(center * center, axis=-1, keepdims=True)
        xhat = center * lax.rsqrt(spread + 1e-05)
        XH[at] = xhat.astype(BF)
        n1 = (xhat * gain1 + shift1).astype(BF)
        N1[at] = n1
        N2[at] = (xhat * gain2 + shift2).astype(BF)
        mixed = nn(n1, WQ[...].reshape(1024, 384)) + bias_q
        QKP[:, cols] = jnp.transpose(mixed[:, :256])
        V[at] = mixed[:, 256:].astype(BF)
        VT[:, cols] = jnp.transpose(mixed[:, 256:]).astype(BF)

    gather_g = gather_next(gather_g)

    cosine = TAB[0]
    sine = TAB[1]
    for base in (0, 64, 128, 192):
        one = QKP[base : base + 8]
        two = QKP[base + 8 : base + 16]
        QKP[base : base + 8] = one * cosine - two * sine
        QKP[base + 8 : base + 16] = two * cosine + one * sine
    queries = QKP[0:128].astype(BF).astype(F32) * 0.125
    keys = QKP[128:256]
    low_rows = lax.broadcasted_iota(jnp.int32, (128, 1024), 0) < 64
    low_cols = lax.broadcasted_iota(jnp.int32, (1024, 128), 1) < 64
    QTM[0] = jnp.where(low_rows, queries, 0.0).astype(BF)
    QTM[1] = jnp.where(low_rows, 0.0, queries).astype(BF)
    back = jnp.transpose(queries)
    QM[0] = jnp.where(low_cols, back, 0.0).astype(BF)
    QM[1] = jnp.where(low_cols, 0.0, back).astype(BF)
    KT[...] = keys.astype(BF)
    K[...] = jnp.transpose(keys).astype(BF)

    @pl.loop(0, 2)
    def _(head):
        hr = rows(64 * head, 64)
        for j in range(4):
            top = 256 * (j + 1)
            q = slice(256 * j, 256 * j + 256)
            scores = nn(K[0:top], QTM[head, :, q])
            ki = lax.broadcasted_iota(jnp.int32, (top, 256), 0)
            qi = lax.broadcasted_iota(jnp.int32, (top, 256), 1) + 256 * j
            allowed = (ki <= qi) & (ki >= START[0:1, q])
            scores = jnp.where(allowed, scores, -1e9)
            weight = jnp.exp(scores - jnp.max(scores, axis=0, keepdims=True))
            probs = (weight * (1.0 / jnp.sum(weight, axis=0, keepdims=True))).astype(BF)
            PT[head, 0:top, q] = probs
            CTXT[hr, q] = nn(VT[hr, 0:top], probs).astype(BF)

    def scatter_start(TB, RA, RB):
        a = [remote(TB.at[zk[k], :, 0:64], RA.at[k - 1], shard_to(2 * k)) for k in (1, 3, 2)]
        b = remote(TB.at[:, other, 64:128], RB, shard_to(1))
        return a, b

    def scatter_middle(state, TB, RA, RB, RX, RZ, TX, UB):
        a, b = state
        arrived(a)
        TX[...] = (
            TB[z, other, 0:64].astype(F32) + RA[0, other].astype(F32)
            + RA[1, other].astype(F32) + RA[2, other].astype(F32)
        ).astype(BF)
        out = [remote(TX, RX, shard_to(1))]
        b.wait_recv()
        for k in (1, 3, 2):
            UB[k - 1] = (TB[zk[k], l, 64:128].astype(F32) + RB[zk[k]].astype(F32)).astype(BF)
            out.append(remote(UB.at[k - 1], RZ.at[k - 1], shard_to(2 * k)))
        return out

    def scatter_end(out, TB, RA, RB, RX, RZ):
        arrived(out)
        ACC[0:64] = (
            TB[z, l, 0:64].astype(F32) + RA[0, l].astype(F32) + RA[1, l].astype(F32)
            + RA[2, l].astype(F32) + RX[...].astype(F32)
        )
        ACC[64:128] = (
            TB[z, l, 64:128].astype(F32) + RB[z].astype(F32) + RZ[0].astype(F32)
            + RZ[1].astype(F32) + RZ[2].astype(F32)
        )

    CTX[...] = jnp.transpose(CTXT[...].astype(F32)).astype(BF)
    rest_g = gather_last(gather_g)
    core_u.wait_recv()

    @pl.loop(0, 4)
    def _(i):
        at = rows(256 * i, 256)
        cols = lanes(256 * i, 256)
        gate = nn(N2[at], WU[...].reshape(1024, 512)) + bias_up
        phi = 0.5 + 0.5 * lax.erf(gate * 0.7071067811865476)
        GP[at] = phi + gate * jnp.exp(-0.5 * gate * gate) * 0.3989422804014327
        active = gate * phi
        rounded = active.astype(BF)
        ACT[at] = rounded
        ACTT[:, cols] = jnp.transpose(active).astype(BF)
        total = nn(CTX[at], WD[...]) + nn(rounded, WN[...])
        PB[i] = total.astype(BF).reshape(2, 128, 1024)

    out_state = scatter_start(PB, PRA, PRB)
    arrived(rest_g)

    low_256 = lax.broadcasted_iota(jnp.int32, (256, 128), 1) < 64
    low_t256 = lax.broadcasted_iota(jnp.int32, (128, 256), 0) < 64

    @pl.loop(0, 4)
    def _(i):
        at = rows(256 * i, 256)
        cols = lanes(256 * i, 256)
        grad = nt(GB[i].reshape(256, 1024), WD[...])
        DCM[0, at] = jnp.where(low_256, grad, 0.0).astype(BF)
        DCM[1, at] = jnp.where(low_256, 0.0, grad).astype(BF)
        turned = jnp.transpose(grad)
        DCTM[0, :, cols] = jnp.where(low_t256, turned, 0.0).astype(BF)
        DCTM[1, :, cols] = jnp.where(low_t256, 0.0, turned).astype(BF)

    DK[...] = jnp.zeros_like(DK)
    DV[...] = jnp.zeros_like(DV)

    @pl.loop(0, 2)
    def _(head):
        hr = rows(64 * head, 64)
        for j in range(4):
            top = 256 * (j + 1)
            q = slice(256 * j, 256 * j + 256)
            probs = PT[head, 0:top, q]
            soft = probs.astype(F32)
            probs_grad = nn(V[0:top], DCTM[head, :, q])
            middle = jnp.sum(soft * probs_grad, axis=0, keepdims=True)
            score_grad = (soft * (probs_grad - middle)).astype(BF)
            DQT[hr, q] = nn(KT[hr, 0:top], score_grad) * 0.125
            DK[0:top] += nn(score_grad, QM[head, q])
            DV[0:top] += nn(probs, DCM[head, q])

    QKP[0:128] = DQT[...]
    QKP[128:256] = jnp.transpose(DK[...])
    for base in (0, 64, 128, 192):
        one = QKP[base : base + 8]
        two = QKP[base + 8 : base + 16]
        QKP[base : base + 8] = one * cosine + two * sine
        QKP[base + 8 : base + 16] = two * cosine - one * sine
    MT[0:256] = QKP[...].astype(BF)
    MT[256:384] = jnp.transpose(DV[...]).astype(BF)

    mine = half

    def pair_start(GR, X):
        return remote(GR.at[:, lanes(512 * (1 - mine), 512)], X, partner)

    def spread_start(pair, GR, X, C, R, size):
        pair.wait_recv()
        C[...] = (GR[:, lanes(512 * mine, 512)].astype(F32) + X[...].astype(F32)).astype(BF)
        return [
            remote(C.at[rows(size * flip(chip, k), size)], R.at[k - 1], chip_to(k)) for k in range(1, 8)
        ]

    def spread_sum(copies, C, R, S, size):
        arrived(copies)
        total = C[rows(size * chip, size)].astype(F32)
        for k in range(7):
            total = total + R[k].astype(F32)
        S[...] = total.astype(BF)

    G3[...] = nn(MT[...], N1[...]).astype(BF)
    pair3 = pair_start(G3, X3)
    M[:, 0:256] = jnp.transpose(QKP[...]).astype(BF)
    M[:, 256:384] = DV[...].astype(BF)

    CG[...] = jnp.zeros_like(CG)
    CDG[...] = jnp.zeros_like(CDG)

    @pl.loop(0, 4)
    def _(i):
        at = rows(256 * i, 256)
        cols = lanes(256 * i, 256)
        block = GB[i].reshape(256, 1024)
        CG[...] += fold(block.astype(F32))
        gate_grad = (nt(block, WN[...]) * GP[at]).astype(BF)
        DG[at] = gate_grad
        wide = gate_grad.astype(F32)
        CDG[...] += fold(wide)
        DGT[:, cols] = jnp.transpose(wide).astype(BF)

    spread3 = spread_start(pair3, G3, X3, C3, R3, 48)
    G2[...] = nn(DGT[...], N2[...]).astype(BF)
    pair2 = pair_start(G2, X2)
    grads = GB[...].reshape(1024, 1024)
    G1[0:512] = nn(ACTT[...], grads).astype(BF)
    G1[512:640] = nn(CTXT[...], grads).astype(BF)
    pair1 = pair_start(G1, X1)
    out_rest = scatter_middle(out_state, PB, PRA, PRB, PRX, PRZ, PTX, PUB)
    spread2 = spread_start(pair2, G2, X2, C2, R2, 64)

    SUMS[...] = jnp.zeros_like(SUMS)

    @pl.loop(0, 4)
    def _(i):
        at = rows(256 * i, 256)
        xhat = XH[at].astype(F32)
        one = nt(M[at], WQ[...].reshape(1024, 384))
        two = nt(DG[at], WU[...].reshape(1024, 512))
        DB[i] = (one * gain1 + two * gain2).astype(BF).reshape(2, 128, 1024)
        SUMS[0] += fold(one * xhat)
        SUMS[1] += fold(one)
        SUMS[2] += fold(two * xhat)
        SUMS[3] += fold(two)

    in_state = scatter_start(DB, DRA, DRB)
    spread1 = spread_start(pair1, G1, X1, C1, R1, 80)

    def give(S, out, size):
        at = rows(size * chip, size)
        out[at, lanes(512 * mine, 512)] = S[...]
        return [
            remote(S, out.at[at, lanes(512 * mine, 512)], chip_to(k)) for k in range(1, 8)
        ]

    source = lax.rem(lax.div(s, 4) + c, 2)
    def turn(S, A, size):
        base = used[0]
        used[0] += 4
        slot = lax.div(s, 2)

        def descriptor(m, device):
            return pltpu.make_async_remote_copy(
                src_ref=S.at[:, 128 * m : 128 * m + 128], dst_ref=A.at[slot],
                send_sem=ssem.at[base + m], recv_sem=rsem.at[base + slot],
                device_id={"shard": device}, device_id_type=MESH,
            )

        for m in range(4):
            device = 4 * half + m

            @pl.when(device != s)
            def _():
                descriptor(m, device).start()

            @pl.when(device == s)
            def _():
                A[slot] = S[:, 128 * m : 128 * m + 128]

        return base

    def turned(base, S, A, size):
        for m in range(4):
            @pl.when(4 * half + m != s)
            def _():
                pltpu.make_async_remote_copy(
                    src_ref=S.at[:, 128 * m : 128 * m + 128], dst_ref=A.at[m],
                    send_sem=ssem.at[base + m], recv_sem=rsem.at[base + m],
                    device_id={"shard": flip(s, 1)}, device_id_type=MESH,
                ).wait_send()

            @pl.when(2 * m + source != s)
            def _():
                pltpu.make_async_remote_copy(
                    src_ref=S.at[:, 128 * m : 128 * m + 128], dst_ref=A.at[m],
                    send_sem=ssem.at[base + m], recv_sem=rsem.at[base + m],
                    device_id={"shard": flip(s, 1)}, device_id_type=MESH,
                ).wait_recv()

    def give_turned(A, out, size):
        at = rows(size * chip, size)
        out[source, :, at] = A[...]
        return [remote(A, out.at[source, :, at], chip_to(k)) for k in range(1, 8)]

    spread_sum(spread3, C3, R3, S3, 48)
    turn3 = turn(S3, A3, 48)

    SV[...] = jnp.zeros_like(SV)
    bias_grad = jnp.sum(fold(M[...].astype(F32)), axis=0, keepdims=True)
    B24[...] = jnp.zeros_like(B24)
    for j in range(3):
        B24[pl.ds(8 * j + s, 1)] = bias_grad[:, 128 * j : 128 * j + 128]
    for sp in range(8):
        at = slice(128 * sp, 128 * sp + 128)
        for j in range(4):
            SV[sp, j : j + 1] = jnp.sum(SUMS[j, :, at], axis=0, keepdims=True)
        SV[sp, 4:7] = B24[3 * sp : 3 * sp + 3]
    vectors = [remote(SV.at[flip(s, k)], SVR.at[k - 1], shard_to(k)) for k in range(1, 8)]

    scatter_end(out_rest, PB, PRA, PRB, PRX, PRZ)
    out_ref[...] = (HB[z, l].astype(F32) + ACC[...] + VEC[4:5]).astype(BF)
    turned(turn3, S3, A3, 48)
    give3 = give_turned(A3, f3_ref, 48)
    spread_sum(spread2, C2, R2, S2, 64)
    turn2 = turn(S2, A2, 64)
    spread_sum(spread1, C1, R1, S1, 80)
    give1 = give(S1, f1_ref, 80)

    arrived(vectors)
    LV[...] = jnp.zeros_like(LV)
    total = SV[s]
    for k in range(7):
        total = total + SVR[k]
    LV[0:7] = total[0:7]
    up_grad = jnp.sum(CDG[...], axis=0, keepdims=True)
    for j in range(4):
        LV[8 + j : 9 + j] = up_grad[:, 128 * j : 128 * j + 128]
    LV[12:13] = jnp.sum(CG[:, lanes(128 * s, 128)], axis=0, keepdims=True)
    pair_v = remote(LV, LVX, partner)

    in_rest = scatter_middle(in_state, DB, DRA, DRB, DRX, DRZ, DTX, DUB)
    turned(turn2, S2, A2, 64)
    give2 = give_turned(A2, f2_ref, 64)
    pair_v.wait_recv()
    LC[...] = LV[...] + LVX[...]
    LCR[chip] = LC[...]
    spread_v = [remote(LC, LCR.at[chip], chip_to(k)) for k in range(1, 8)]

    def flat(F, p, i, out, size):
        block = F[p, i].astype(F32)
        for j in range(size // 128):
            out_at = 128 * (2 * i + p) + 1024 * j if size == 384 else 512 * (2 * i + p) + 128 * j
            piece = jnp.transpose(block[128 * j : 128 * j + 128]).astype(BF)
            out[:, lanes(out_at, 128)] = piece

    arrived(give3)
    last3 = remote(f3_ref.at[source], f3_ref.at[source], partner)
    for i in range(4):
        flat(f3_ref, source, i, o3_ref, 384)
    arrived(give1)
    last1 = remote(f1_ref.at[:, lanes(512 * mine, 512)], f1_ref.at[:, lanes(512 * mine, 512)], partner)
    last3.wait_recv()
    for i in range(4):
        flat(f3_ref, 1 - source, i, o3_ref, 384)
    arrived(give2)
    last2 = remote(f2_ref.at[source], f2_ref.at[source], partner)
    for i in range(4):
        flat(f2_ref, source, i, o2_ref, 512)

    arrived(spread_v)
    total = LCR[0]
    for k in range(1, 8):
        total = total + LCR[k]
    v1_ref[...] = total[0:1].reshape(128)
    v2_ref[...] = total[1:2].reshape(128)
    v3_ref[...] = total[2:3].reshape(128)
    v4_ref[...] = total[3:4].reshape(128)
    vq_ref[...] = total[4:7].reshape(384)
    vu_ref[...] = total[8:12].reshape(512)
    vd_ref[...] = total[12:13].reshape(128)
    vw_ref[...] = total[12:13].reshape(128)
    last2.wait_recv()
    for i in range(4):
        flat(f2_ref, 1 - source, i, o2_ref, 512)

    scatter_end(in_rest, DB, DRA, DRB, DRX, DRZ)
    block = HB[z, l].astype(F32)
    center = block - jnp.mean(block, axis=-1, keepdims=True)
    spread = jnp.mean(center * center, axis=-1, keepdims=True)
    scale = lax.rsqrt(spread + 1e-05)
    xhat = center * scale
    grad = ACC[...]
    grad = grad - jnp.mean(grad, axis=-1, keepdims=True) - xhat * jnp.mean(grad * xhat, axis=-1, keepdims=True)
    ing_ref[...] = (GB[z, l].astype(F32) + scale * grad).astype(BF)

    last1.wait_recv()
    for copy in sent:
        copy.wait_send()
    assert used[0] <= SEMS, used[0]


def block_call(*args):
    vm = pltpu.VMEM
    scratch = [
        vm((2, 4, 512, 128), BF), vm((2, 4, 384, 128), BF), vm((16, 128), F32), vm((8, 128), jnp.int32),
        vm((128, 1024), BF), vm((512, 1024), BF),
        vm((4, 2, 128, 1024), BF), vm((4, 2, 128, 1024), BF), vm((8, 8, 128), jnp.int32), vm((8, 16, 128), F32),
        vm((8, 128, 384), BF), vm((8, 128, 512), BF), vm((8, 1024), F32), vm((24, 128), F32),
        vm((1024, 1024), BF), vm((1024, 1024), BF), vm((1024, 1024), BF), vm((256, 1024), F32),
        vm((2, 8, 1024), F32), vm((8, 1024), jnp.int32),
        vm((2, 128, 1024), BF), vm((2, 1024, 128), BF), vm((128, 1024), BF), vm((1024, 128), BF),
        vm((1024, 128), BF), vm((128, 1024), BF),
        vm((1024, 512), F32), vm((1024, 512), BF), vm((512, 1024), BF), vm((2, 1024, 1024), BF),
        vm((128, 1024), BF), vm((1024, 128), BF), vm((2, 1024, 128), BF), vm((2, 128, 1024), BF),
        vm((1024, 512), BF), vm((512, 1024), BF), vm((128, 1024), F32), vm((1024, 128), F32), vm((1024, 128), F32),
        vm((1024, 384), BF), vm((384, 1024), BF),
    ]
    for _ in range(2):
        scratch += [
            vm((4, 2, 128, 1024), BF), vm((3, 2, 64, 1024), BF), vm((4, 64, 1024), BF), vm((64, 1024), BF),
            vm((3, 64, 1024), BF), vm((64, 1024), BF), vm((3, 64, 1024), BF),
        ]
    scratch += [vm((128, 1024), F32)]
    scratch += [vm((640, 1024), BF), vm((640, 512), BF), vm((640, 512), BF), vm((7, 80, 512), BF), vm((80, 512), BF)]
    for size in (64, 48):
        scratch += [
            vm((8 * size, 1024), BF), vm((8 * size, 512), BF), vm((8 * size, 512), BF), vm((7, size, 512), BF),
            vm((size, 512), BF), vm((4, size, 128), BF),
        ]
    scratch += [
        vm((4, 8, 1024), F32), vm((8, 1024), F32), vm((8, 512), F32), vm((8, 16, 128), F32), vm((7, 16, 128), F32),
        vm((16, 128), F32), vm((16, 128), F32), vm((16, 128), F32), vm((8, 16, 128), F32),
        pltpu.SemaphoreType.DMA((SEMS,)), pltpu.SemaphoreType.DMA((SEMS,)), pltpu.SemaphoreType.DMA((8,)),
    ]
    return pl.pallas_call(
        kernel,
        out_shape=(
            jax.ShapeDtypeStruct((128, 1024), BF), jax.ShapeDtypeStruct((128, 1024), BF),
            jax.ShapeDtypeStruct((640, 1024), BF), jax.ShapeDtypeStruct((128, 4096), BF),
            jax.ShapeDtypeStruct((128, 3072), BF),
        ) + tuple(jax.ShapeDtypeStruct((size,), F32) for size in (128, 128, 128, 128, 384, 128, 512, 128)),
        in_specs=[
            pl.BlockSpec(memory_space=pl.ANY if len(arg.shape) == 2 else pltpu.VMEM) for arg in args
        ],
        out_specs=[pl.BlockSpec(memory_space=pltpu.VMEM)] * 13,
        scratch_shapes=scratch,
        compiler_params=pltpu.CompilerParams(
            collective_id=0, has_side_effects=True, vmem_limit_bytes=62 * 2**20
        ),
    )(*args)


def shards(*args):
    out, ing, first, up, qkv, v1, v2, v3, v4, vq, vd, vu, vw = block_call(*args)
    first = first.astype(F32)
    return (
        out, ing, v1, v2, v3, v4, qkv.astype(F32), vq, first[512:640], vd, up.astype(F32), vu, first[0:512], vw,
    )


def solution(mesh):
    both, one, wide = P(("rep", "shard"), None), P("shard"), P("shard", None)
    placed = (
        both, both, P(("rep", "shard")), one, one, one, one, wide, one, wide, one, wide, one, wide, one,
    )
    return jax.shard_map(
        shards, mesh=mesh, in_specs=placed,
        out_specs=(both, both, one, one, one, one, wide, one, wide, one, wide, one, wide, one),
        check_vma=False,
    )
```

```python
import functools

import jax
import jax.numpy as jnp
from jax import lax
from jax.experimental import pallas as pl
from jax.experimental.pallas import tpu as pltpu
from jax.sharding import PartitionSpec as P

BF = jnp.bfloat16
F32 = jnp.float32
MESH = pl.DeviceIdType.MESH
SEMS = 176


def flip(value, mask):
    out = value
    bit = 1
    while bit <= mask:
        if mask & bit:
            out = out + bit - 2 * bit * lax.rem(lax.div(value, bit), 2)
        bit *= 2
    return out


def nt(left, right):
    return lax.dot_general(left, right, (((1,), (1,)), ((), ())), preferred_element_type=F32)


def nn(left, right):
    return jnp.dot(left, right, preferred_element_type=F32)


def fold(block):
    return jnp.sum(block.reshape(block.shape[0] // 8, 8, block.shape[1]), axis=0)


def kernel(
    hid_ref, g_ref, seg_ref, gain1_ref, shift1_ref, gain2_ref, shift2_ref, wqkv_ref, bqkv_ref, wdense_ref,
    bdense_ref, wup_ref, bup_ref, wdown_ref, bdown_ref,
    out_ref, ing_ref, dn_ref, de_ref, o2_ref, o3_ref, v1_ref, v2_ref, v3_ref, v4_ref, vq_ref, vd_ref, vu_ref, vw_ref,
    f1_ref, f2_ref, f3_ref, PKO, SGO, SGX, WD, WN, OWNH, OWNG,
    HB, GB, SG, PK, WQ, WU, VEC, B24, XH, N1, N2, QKP, TAB, START, QTM, QM, KT, K, V, VT,
    GP, ACT, ACTT, PT, CTXT, CTX, DCM, DCTM, DG, DGT, DQT, DK, DV, M, MT,
    PB, PRA, PRT, PRZ, PFX, PRX, DB, DRA, DRT, DRZ, DFX, DRX, ACC,
    G1, X1, C1, R1, S1, CY1, RH1, G2, X2, C2, R2, S2, CY2, RH2, A2, G3, X3, C3, R3, S3, A3,
    SUMS, CG, CDG, SV, SVR, LV, LVX, LC, LCR,
    ssem, rsem, lsem,
):
    r = lax.axis_index("rep")
    s = lax.axis_index("shard")
    k = lax.rem(r, 2)
    chip = lax.div(r, 2)
    y = lax.rem(chip, 4)
    h = lax.div(chip, 4)
    z = lax.div(s, 2)
    l = lax.rem(s, 2)
    b = 2 * z + k
    home = k == l
    off = k != l
    zs = (lax.rem(z + 2, 4), lax.rem(z + 1, 4), lax.rem(z + 3, 4))
    across_z, ahead, behind = zs

    def shard_to(m):
        return {"shard": flip(s, m)}

    def chip_to(m):
        return {"rep": flip(chip, m) * 2 + k}

    def z_to(zz):
        return {"shard": 2 * zz + l}

    partner = {"rep": chip * 2 + 1 - k}
    x_near = {"shard": 2 * z + 1 - l}
    x_far = {"rep": (1 - h) * 8 + y * 2 + k, "shard": 2 * z + 1 - l}
    x_cross = {"rep": chip * 2 + 1 - k, "shard": 2 * z + 1 - l}

    def lanes(start, size):
        return pl.ds(pl.multiple_of(start, 128), size)

    def rows(start, size):
        return pl.ds(pl.multiple_of(start, 16), size)

    barrier = pltpu.get_barrier_semaphore()
    peers = [shard_to(m) for m in range(1, 8)] + [chip_to(m) for m in range(1, 8)] + [partner, x_far, x_cross]
    for peer in peers:
        pl.semaphore_signal(barrier, inc=1, device_id=peer, device_id_type=MESH)

    local = [
        pltpu.make_async_copy(hid_ref, OWNH, lsem.at[0]),
        pltpu.make_async_copy(g_ref, OWNG, lsem.at[1]),
        pltpu.make_async_copy(
            wup_ref.at[rows(32 * y, 32), lanes(512 * b, 512)], WU.at[z, l, rows(32 * y, 32)], lsem.at[2]),
    ]
    for j in range(3):
        local.append(pltpu.make_async_copy(
            wqkv_ref.at[:, lanes(1024 * j + 128 * b, 128)], WQ.at[z, l, :, 128 * j : 128 * j + 128], lsem.at[3 + j]))
    own_only = [
        pltpu.make_async_copy(hid_ref, HB.at[z, k], lsem.at[6]),
        pltpu.make_async_copy(g_ref, GB.at[z, k], lsem.at[7]),
        pltpu.make_async_copy(wdense_ref, WD, lsem.at[8]),
        pltpu.make_async_copy(wdown_ref, WN, lsem.at[9]),
    ]
    for copy in local:
        copy.start()

    @pl.when(home)
    def _():
        for copy in own_only:
            copy.start()

    PKO[...] = jnp.zeros_like(PKO)
    at = 0
    for ref in (gain1_ref, shift1_ref, gain2_ref, shift2_ref, bqkv_ref, bdense_ref, bup_ref, bdown_ref):
        size = ref.shape[0] // 128
        PKO[at : at + size] = ref[...].astype(F32).reshape(size, 128)
        at += size
    PK[s] = PKO[...]
    SGO[...] = jnp.broadcast_to(seg_ref[...].reshape(1, 128), (8, 128))
    SG[s] = SGO[...]
    for copy in local:
        copy.wait()

    @pl.when(home)
    def _():
        for copy in own_only:
            copy.wait()

    pl.semaphore_wait(barrier, len(peers))

    used = [0]
    sent = []

    class Copy:
        def __init__(self, src, dst, device, send, recv):
            at = used[0]
            used[0] += 1
            self.copy = pltpu.make_async_remote_copy(
                src_ref=src, dst_ref=dst, send_sem=ssem.at[at], recv_sem=rsem.at[at],
                device_id=device, device_id_type=MESH,
            )
            self.send = send
            self.recv = recv
            sent.append(self)
            self.under(send, self.copy.start)

        def under(self, role, action):
            if role is None:
                action()
            else:
                pl.when(role)(lambda: action())

        def wait_recv(self):
            self.under(self.recv, self.copy.wait_recv)

        def wait_send(self):
            self.under(self.send, self.copy.wait_send)

    def remote(src, dst, device, send=None, recv=None):
        return Copy(src, dst, device, send, recv)

    def arrived(copies):
        for copy in copies:
            copy.wait_recv()

    low = slice(0, 64)
    high = slice(64, 128)

    def same(ref, device):
        return remote(ref, ref, device)

    def gather_x(x_ref, XB):
        return remote(x_ref, XB.at[z, l], x_cross, off, off)

    def gather_z(first, XB):
        first.wait_recv()
        own = XB.at[z, k]
        return XB, same(own, z_to(ahead)), same(own, z_to(behind)), [same(own, partner)]

    def gather_next(state):
        XB, za, zb, cores = state
        za.wait_recv()
        d2a = same(XB.at[behind, k, low], z_to(ahead))
        cores.append(same(XB.at[behind, k], partner))
        zb.wait_recv()
        d2b = same(XB.at[ahead, k, high], z_to(behind))
        cores.append(same(XB.at[ahead, k], partner))
        return XB, d2a, d2b, cores

    def gather_last(state):
        XB, d2a, d2b, cores = state
        arrived([d2a, d2b])
        cores.append(same(XB.at[across_z, k], partner))
        return cores

    def weight_z(ref, W, width, blocks):
        return [
            [remote(
                ref.at[:, lanes(1024 * j + width * (2 * zz + k), width)],
                W.at[z, l, :, width * j : width * j + width], z_to(zz)) for j in range(blocks)]
            for zz in (ahead, behind, across_z)
        ]

    def weight_x(W, zz):
        return [same(W.at[zz, l, low], x_near), same(W.at[zz, l, high], x_far)]

    y_peers = [{"rep": (4 * h + flip(y, m)) * 2 + k} for m in (1, 3, 2)]
    near32 = rows(32 * y, 16)
    far32 = rows(32 * y + 16, 16)
    both32 = rows(32 * y, 32)
    both128 = rows(128 * y, 128)
    gather_h = gather_x(hid_ref, HB)
    up_z = [
        remote(wup_ref.at[both32, lanes(512 * (2 * zz + k), 512)], WU.at[z, l, both32], z_to(zz))
        for zz in (ahead, behind, across_z)
    ]
    outer_x = [
        remote(wdown_ref.at[rows(128 * y, 64)], WN.at[rows(128 * y, 64)], x_near, home, off),
        remote(wdown_ref.at[rows(128 * y + 64, 64)], WN.at[rows(128 * y + 64, 64)], x_far, home, off),
        remote(wdense_ref.at[near32], WD.at[near32], x_near, home, off),
        remote(wdense_ref.at[far32], WD.at[far32], x_far, home, off),
    ]
    qkv_z = weight_z(wqkv_ref, WQ, 128, 3)
    qkv_x = weight_x(WQ, z)
    gather_h = gather_z(gather_h, HB)
    small = [remote(PKO, PK.at[s], shard_to(m)) for m in range(1, 8)]
    small += [remote(SGO, SG.at[s], shard_to(m)) for m in range(1, 8)]
    arrived(up_z)
    up_x = [same(WU.at[:, l, near32], x_near), same(WU.at[:, l, far32], x_far)]
    arrived(outer_x)
    outer_y = [
        remote(ref.at[part], ref.at[part], peer, off, off)
        for peer in y_peers for ref, part in ((WN, both128), (WD, both32))
    ]
    for copies, zz in zip(qkv_z, (behind, ahead, across_z)):
        arrived(copies)
        qkv_x += weight_x(WQ, zz)
    arrived(up_x)
    up_y = [same(WU.at[:, :, both32], peer) for peer in y_peers]
    gather_h = gather_next(gather_h)
    gather_g = gather_x(g_ref, GB)
    arrived(small)
    seg_core = remote(SG, SGX, partner)
    rest_h = gather_last(gather_h)
    gather_g = gather_z(gather_g, GB)

    for sp in range(8):
        block = PK[sp]
        at = slice(128 * sp, 128 * sp + 128)
        for j in range(4):
            VEC[j : j + 1, at] = block[j : j + 1]
        VEC[4:5, at] = block[7:8] + block[12:13]
        B24[3 * sp : 3 * sp + 3] = block[4:7]
    own = PK[b]
    bias_up = jnp.concatenate([own[8 + j : 9 + j] for j in range(4)], axis=1)
    bias_q = jnp.concatenate([B24[pl.ds(8 * j + b, 1)] for j in range(3)], axis=1)
    seg_core.wait_recv()
    ids = [jnp.where(home, SG[sp, 0:1], SGX[sp, 0:1]).astype(F32) for sp in range(8)]
    seg_row = jnp.concatenate(ids, axis=1)
    count = jnp.zeros((1, 1024), F32)
    for sp in range(8):
        column = jnp.transpose(jnp.broadcast_to(ids[sp], (128, 128)))[:, 0:1]
        count = count + jnp.sum((column < seg_row).astype(F32), axis=0, keepdims=True)
    START[...] = jnp.broadcast_to(count.astype(jnp.int32), (8, 1024))
    place = lax.broadcasted_iota(jnp.int32, (8, 1024), 1).astype(F32)
    row8 = lax.broadcasted_iota(jnp.int32, (8, 1024), 0)
    inverse = jnp.zeros((8, 1024), F32)
    for j in range(8):
        inverse = jnp.where(row8 == j, 10000.0 ** (-j / 8.0), inverse)
    angles = (place - count) * inverse
    TAB[0] = jnp.cos(angles)
    TAB[1] = jnp.sin(angles)
    gain1, shift1, gain2, shift2 = (VEC[j : j + 1] for j in range(4))

    arrived(rest_h)
    arrived(qkv_x)

    @pl.loop(0, 4)
    def _(i):
        at = rows(256 * i, 256)
        cols = lanes(256 * i, 256)
        block = HB[i].reshape(256, 1024).astype(F32)
        center = block - jnp.mean(block, axis=-1, keepdims=True)
        spread = jnp.mean(center * center, axis=-1, keepdims=True)
        xhat = center * lax.rsqrt(spread + 1e-05)
        XH[at] = xhat.astype(BF)
        n1 = (xhat * gain1 + shift1).astype(BF)
        N1[at] = n1
        N2[at] = (xhat * gain2 + shift2).astype(BF)
        mixed = nn(n1, WQ[...].reshape(1024, 384)) + bias_q
        QKP[:, cols] = jnp.transpose(mixed[:, :256])
        V[at] = mixed[:, 256:].astype(BF)
        VT[:, cols] = jnp.transpose(mixed[:, 256:]).astype(BF)

    cosine = TAB[0]
    sine = TAB[1]
    for base in (0, 64, 128, 192):
        one = QKP[base : base + 8]
        two = QKP[base + 8 : base + 16]
        QKP[base : base + 8] = one * cosine - two * sine
        QKP[base + 8 : base + 16] = two * cosine + one * sine
    queries = QKP[0:128].astype(BF).astype(F32) * 0.125
    keys = QKP[128:256]
    low_rows = lax.broadcasted_iota(jnp.int32, (128, 1024), 0) < 64
    low_cols = lax.broadcasted_iota(jnp.int32, (1024, 128), 1) < 64
    QTM[0] = jnp.where(low_rows, queries, 0.0).astype(BF)
    QTM[1] = jnp.where(low_rows, 0.0, queries).astype(BF)
    back = jnp.transpose(queries)
    QM[0] = jnp.where(low_cols, back, 0.0).astype(BF)
    QM[1] = jnp.where(low_cols, 0.0, back).astype(BF)
    KT[...] = keys.astype(BF)
    K[...] = jnp.transpose(keys).astype(BF)

    def attention(head):
        hr = slice(64 * head, 64 * head + 64)
        for j in range(4):
            top = 256 * (j + 1)
            q = slice(256 * j, 256 * j + 256)
            scores = nn(K[0:top], QTM[head, :, q])
            ki = lax.broadcasted_iota(jnp.int32, (top, 256), 0)
            qi = lax.broadcasted_iota(jnp.int32, (top, 256), 1) + 256 * j
            allowed = (ki <= qi) & (ki >= START[0:1, q])
            scores = jnp.where(allowed, scores, -1e9)
            weight = jnp.exp(scores - jnp.max(scores, axis=0, keepdims=True))
            probs = (weight * (1.0 / jnp.sum(weight, axis=0, keepdims=True))).astype(BF)
            PT[head, 0:top, q] = probs
            CTXT[hr, q] = nn(VT[hr, 0:top], probs).astype(BF)

    attention(0)
    gather_g = gather_next(gather_g)
    attention(1)

    def scatter_core(TB, RA):
        return [remote(TB.at[zz, 1 - k], RA.at[zz], partner) for zz in (across_z, ahead, behind, z)]

    def scatter_z(copies, TB, RA, RT, RZ):
        out = []
        for j, zz in enumerate(zs):
            copies[j].wait_recv()
            RT[j] = (TB[zz, k].astype(F32) + RA[zz].astype(F32)).astype(BF)
            out.append(remote(RT.at[j], RZ.at[j], z_to(zz)))
        copies[3].wait_recv()
        return out

    def scatter_x(copies, TB, RA, RZ, FX, RX):
        arrived(copies)
        total = TB[z, k].astype(F32) + RA[z].astype(F32)
        for j in range(3):
            total = total + RZ[j].astype(F32)
        ACC[...] = total
        FX[...] = total.astype(BF)
        return remote(FX, RX, x_cross, off, off)

    def scatter_end(copy, RX):
        copy.wait_recv()

        @pl.when(off)
        def _():
            ACC[...] = RX[...].astype(F32)

    CTX[...] = jnp.transpose(CTXT[...].astype(F32)).astype(BF)
    rest_g = gather_last(gather_g)
    arrived(up_y)
    arrived(outer_y)

    @pl.loop(0, 4)
    def _(i):
        at = rows(256 * i, 256)
        cols = lanes(256 * i, 256)
        gate = nn(N2[at], WU[...].reshape(1024, 512)) + bias_up
        phi = 0.5 + 0.5 * lax.erf(gate * 0.7071067811865476)
        GP[at] = phi + gate * jnp.exp(-0.5 * gate * gate) * 0.3989422804014327
        active = gate * phi
        rounded = active.astype(BF)
        ACT[at] = rounded
        ACTT[:, cols] = jnp.transpose(active).astype(BF)
        total = nn(CTX[at], WD[...]) + nn(rounded, WN[...])
        PB[i] = total.astype(BF).reshape(2, 128, 1024)

    out_cores = scatter_core(PB, PRA)
    arrived(rest_g)

    def near_start(GR, X, size):
        part = lanes(512 * (1 - l), 512)
        top = slice(0, 4 * size)
        end = slice(4 * size, 8 * size)
        return [remote(GR.at[top, part], X.at[top], x_near), remote(GR.at[end, part], X.at[end], x_far)]

    def spread_start(near, GR, X, C, R, size):
        arrived(near)
        C[...] = (GR[:, lanes(512 * l, 512)].astype(F32) + X[...].astype(F32)).astype(BF)
        return [
            remote(C.at[rows(size * flip(chip, m), size)], R.at[m - 1], chip_to(m)) for m in range(1, 8)
        ]

    def spread_sum(copies, C, R, S, size):
        arrived(copies)
        total = C[rows(size * chip, size)].astype(F32)
        for m in range(7):
            total = total + R[m].astype(F32)
        S[...] = total.astype(BF)

    y_at = [flip(y, m) for m in (1, 3, 2)]
    h_peer = {"rep": (4 * (1 - h) + y) * 2 + k}

    def along_y(C, R, size, role=None):
        return [
            remote(C.at[rows(2 * size * yy, 2 * size)], R.at[m], y_peers[m], role, role) for m, yy in enumerate(y_at)
        ]

    def quarter_sum(copies, C, R, CY, size):
        arrived(copies)
        CY[...] = (
            C[rows(2 * size * y, 2 * size)].astype(F32) + R[0].astype(F32) + R[1].astype(F32) + R[2].astype(F32)
        ).astype(BF)

    def along_h(CY, RH, size, role=None):
        return remote(CY.at[rows(size * (1 - h), size)], RH, h_peer, role, role)

    def turn(S, A):
        A[z] = S[:, lanes(128 * z, 128)]
        return [remote(S.at[:, lanes(128 * zz, 128)], A.at[z], z_to(zz)) for zz in (ahead, behind, across_z)]

    def give(copies, A, out, size):
        arrived(copies)
        at = rows(size * chip, size)
        out[k, :, at] = A[...]
        return [remote(A, out.at[k, :, at], chip_to(m)) for m in range(1, 8)]

    def give_h(copies, A, out, size):
        arrived(copies)
        at = rows(size * (2 * y + h), size)
        out[k, :, at] = A[...]
        return remote(A, out.at[k, :, at], h_peer)

    def give_y(copy, out, size):
        copy.wait_recv()
        ref = out.at[k, :, rows(2 * size * y, 2 * size)]
        return [remote(ref, ref, peer) for peer in y_peers]

    def put(GR, total):
        for sp in range(8):
            at = 512 * (sp % 2) + 128 * (sp // 2)
            GR[:, at : at + 128] = total[:, 128 * sp : 128 * sp + 128].astype(BF)

    grads = GB[...].reshape(1024, 1024)
    G1[0:512] = nn(ACTT[...], grads).astype(BF)
    G1[512:640] = nn(CTXT[...], grads).astype(BF)
    y1 = along_y(G1, R1, 80)

    CG[...] = jnp.zeros_like(CG)
    CDG[...] = jnp.zeros_like(CDG)

    @pl.loop(0, 4)
    def _(i):
        at = rows(256 * i, 256)
        cols = lanes(256 * i, 256)
        block = GB[i].reshape(256, 1024)
        CG[...] += fold(block.astype(F32))
        gate_grad = (nt(block, WN[...]) * GP[at]).astype(BF)
        DG[at] = gate_grad
        wide = gate_grad.astype(F32)
        CDG[...] += fold(wide)
        DGT[:, cols] = jnp.transpose(wide).astype(BF)

    out_z = scatter_z(out_cores, PB, PRA, PRT, PRZ)
    put(G2, nn(DGT[...], N2[...]))
    near2 = near_start(G2, X2, 64)

    low_256 = lax.broadcasted_iota(jnp.int32, (256, 128), 1) < 64
    low_t256 = lax.broadcasted_iota(jnp.int32, (128, 256), 0) < 64

    @pl.loop(0, 4)
    def _(i):
        at = rows(256 * i, 256)
        cols = lanes(256 * i, 256)
        grad = nt(GB[i].reshape(256, 1024), WD[...])
        DCM[0, at] = jnp.where(low_256, grad, 0.0).astype(BF)
        DCM[1, at] = jnp.where(low_256, 0.0, grad).astype(BF)
        turned = jnp.transpose(grad)
        DCTM[0, :, cols] = jnp.where(low_t256, turned, 0.0).astype(BF)
        DCTM[1, :, cols] = jnp.where(low_t256, 0.0, turned).astype(BF)

    DK[...] = jnp.zeros_like(DK)
    DV[...] = jnp.zeros_like(DV)

    def attention_back(head):
        hr = slice(64 * head, 64 * head + 64)
        for j in range(4):
            top = 256 * (j + 1)
            q = slice(256 * j, 256 * j + 256)
            probs = PT[head, 0:top, q]
            soft = probs.astype(F32)
            probs_grad = nn(V[0:top], DCTM[head, :, q])
            middle = jnp.sum(soft * probs_grad, axis=0, keepdims=True)
            score_grad = (soft * (probs_grad - middle)).astype(BF)
            DQT[hr, q] = nn(KT[hr, 0:top], score_grad) * 0.125
            DK[0:top] += nn(score_grad, QM[head, q])
            DV[0:top] += nn(probs, DCM[head, q])

    attention_back(0)
    attention_back(1)
    arrived(near2)
    C2[...] = (G2[:, lanes(512 * l, 512)].astype(F32) + X2[...].astype(F32)).astype(BF)
    y2 = along_y(C2, R2, 64)

    QKP[0:128] = DQT[...]
    QKP[128:256] = jnp.transpose(DK[...])
    for base in (0, 64, 128, 192):
        one = QKP[base : base + 8]
        two = QKP[base + 8 : base + 16]
        QKP[base : base + 8] = one * cosine + two * sine
        QKP[base + 8 : base + 16] = two * cosine - one * sine
    MT[0:256] = QKP[...].astype(BF)
    MT[256:384] = jnp.transpose(DV[...]).astype(BF)

    put(G3, nn(MT[...], N1[...]))
    near3 = near_start(G3, X3, 48)
    M[:, 0:256] = jnp.transpose(QKP[...]).astype(BF)
    M[:, 256:384] = DV[...].astype(BF)
    SUMS[...] = jnp.zeros_like(SUMS)
    in_cores = []
    in_z = []

    def norm_grads(zz):
        at = rows(256 * zz, 256)
        xhat = XH[at].astype(F32)
        one = nt(M[at], WQ[...].reshape(1024, 384))
        two = nt(DG[at], WU[...].reshape(1024, 512))
        DB[zz] = (one * gain1 + two * gain2).astype(BF).reshape(2, 128, 1024)
        in_cores.append(remote(DB.at[zz, 1 - k], DRA.at[zz], partner))
        SUMS[0] += fold(one * xhat)
        SUMS[1] += fold(one)
        SUMS[2] += fold(two * xhat)
        SUMS[3] += fold(two)

    def norm_send(j):
        zz = zs[j]
        in_cores[j].wait_recv()
        DRT[j] = (DB[zz, k].astype(F32) + DRA[zz].astype(F32)).astype(BF)
        in_z.append(remote(DRT.at[j], DRZ.at[j], z_to(zz)))

    norm_grads(across_z)
    norm_grads(ahead)
    norm_send(0)
    quarter_sum(y1, G1, R1, CY1, 80)
    near1 = [
        remote(CY1.at[0:80], X1.at[0:80], x_near, off, home),
        remote(CY1.at[80:160], X1.at[80:160], x_far, off, home),
    ]
    norm_grads(behind)
    norm_send(1)
    norm_grads(z)
    norm_send(2)
    out_x = scatter_x(out_z, PB, PRA, PRZ, PFX, PRX)

    SV[...] = jnp.zeros_like(SV)
    bias_grad = jnp.sum(fold(M[...].astype(F32)), axis=0, keepdims=True)
    B24[...] = jnp.zeros_like(B24)
    for j in range(3):
        B24[pl.ds(8 * j + b, 1)] = bias_grad[:, 128 * j : 128 * j + 128]
    for sp in range(8):
        at = slice(128 * sp, 128 * sp + 128)
        for j in range(4):
            SV[sp, j : j + 1] = jnp.sum(SUMS[j, :, at], axis=0, keepdims=True)
        SV[sp, 4:7] = B24[3 * sp : 3 * sp + 3]
    up_grad = jnp.sum(CDG[...], axis=0, keepdims=True)
    for j in range(4):
        SV[b, 8 + j : 9 + j] = up_grad[:, 128 * j : 128 * j + 128]
    SV[b, 12:13] = jnp.sum(CG[:, lanes(128 * b, 128)], axis=0, keepdims=True)
    vectors = [remote(SV.at[flip(s, m)], SVR.at[m - 1], shard_to(m)) for m in range(1, 8)]

    spread3 = spread_start(near3, G3, X3, C3, R3, 48)
    quarter_sum(y2, C2, R2, CY2, 64)
    h2 = along_h(CY2, RH2, 64)
    arrived(near1)

    @pl.when(home)
    def _():
        C1[...] = (CY1[...].astype(F32) + X1[...].astype(F32)).astype(BF)

    h1 = along_h(C1, RH1, 80, home)
    scatter_end(out_x, PRX)
    out_ref[...] = (OWNH[...].astype(F32) + ACC[...] + VEC[4:5]).astype(BF)
    arrived(vectors)
    total = SV[s]
    for m in range(7):
        total = total + SVR[m]
    LV[...] = total
    pair_v = remote(LV, LVX, partner)
    h1.wait_recv()

    @pl.when(home)
    def _():
        S1[...] = (C1[rows(80 * h, 80)].astype(F32) + RH1[...].astype(F32)).astype(BF)
        f1_ref[y, h] = S1[...]

    give1 = [remote(S1, f1_ref.at[y, h], peer, home, home) for peer in y_peers]
    h2.wait_recv()
    S2[...] = (CY2[rows(64 * h, 64)].astype(F32) + RH2[...].astype(F32)).astype(BF)
    turn2 = turn(S2, A2)
    pair_v.wait_recv()
    LC[...] = LV[...] + LVX[...]
    LCR[chip] = LC[...]
    spread_v = [remote(LC, LCR.at[chip], chip_to(m)) for m in range(1, 8)]
    spread_sum(spread3, C3, R3, S3, 48)
    turn3 = turn(S3, A3)
    in_cores[3].wait_recv()
    in_x = scatter_x(in_z, DB, DRA, DRZ, DFX, DRX)
    arrived(give1)
    over1 = remote(f1_ref.at[:, h], f1_ref.at[:, h], h_peer, home, home)
    last1 = [remote(f1_ref.at[:, h], f1_ref.at[:, h], partner, home, off)]
    out_h2 = give_h(turn2, A2, f2_ref, 64)
    give3 = give(turn3, A3, f3_ref, 48)
    arrived(spread_v)
    total = LCR[0]
    for m in range(1, 8):
        total = total + LCR[m]
    v1_ref[...] = total[0:1].reshape(128)
    v2_ref[...] = total[1:2].reshape(128)
    v3_ref[...] = total[2:3].reshape(128)
    v4_ref[...] = total[3:4].reshape(128)
    vq_ref[...] = total[4:7].reshape(384)
    vu_ref[...] = total[8:12].reshape(512)
    vd_ref[...] = total[12:13].reshape(128)
    vw_ref[...] = total[12:13].reshape(128)

    give2 = give_y(out_h2, f2_ref, 64)
    scatter_end(in_x, DRX)
    block = OWNH[...].astype(F32)
    center = block - jnp.mean(block, axis=-1, keepdims=True)
    spread = jnp.mean(center * center, axis=-1, keepdims=True)
    scale = lax.rsqrt(spread + 1e-05)
    xhat = center * scale
    grad = ACC[...]
    grad = grad - jnp.mean(grad, axis=-1, keepdims=True) - xhat * jnp.mean(grad * xhat, axis=-1, keepdims=True)
    ing_ref[...] = (OWNG[...].astype(F32) + scale * grad).astype(BF)

    def flat(F, p, i, out, size):
        block = F[p, i].astype(F32)
        for j in range(size // 128):
            out_at = 128 * (2 * i + p) + 1024 * j if size == 384 else 512 * (2 * i + p) + 128 * j
            piece = jnp.transpose(block[128 * j : 128 * j + 128]).astype(BF)
            out[:, lanes(out_at, 128)] = piece

    arrived(give3)
    last3 = remote(f3_ref.at[k], f3_ref.at[k], partner)
    for i in range(4):
        flat(f3_ref, k, i, o3_ref, 384)
    over1.wait_recv()
    last1.append(remote(f1_ref.at[:, 1 - h], f1_ref.at[:, 1 - h], partner, home, off))
    arrived(give2)
    last2 = remote(f2_ref.at[k], f2_ref.at[k], partner)
    last3.wait_recv()
    for i in range(4):
        flat(f3_ref, 1 - k, i, o3_ref, 384)
    for i in range(4):
        flat(f2_ref, k, i, o2_ref, 512)
    last2.wait_recv()
    for i in range(4):
        flat(f2_ref, 1 - k, i, o2_ref, 512)
    arrived(last1)
    first = f1_ref[...].reshape(640, 1024)
    dn_ref[...] = first[0:512]
    de_ref[...] = first[512:640]
    for copy in sent:
        copy.wait_send()
    assert used[0] <= SEMS, used[0]


def block_call(*args):
    vm = pltpu.VMEM
    scratch = [
        vm((4, 2, 80, 1024), BF), vm((2, 4, 512, 128), BF), vm((2, 4, 384, 128), BF), vm((16, 128), F32), vm((8, 128), jnp.int32),
        vm((8, 8, 128), jnp.int32), vm((128, 1024), BF), vm((512, 1024), BF), vm((128, 1024), BF), vm((128, 1024), BF),
        vm((4, 2, 128, 1024), BF), vm((4, 2, 128, 1024), BF), vm((8, 8, 128), jnp.int32), vm((8, 16, 128), F32),
        vm((4, 2, 128, 384), BF), vm((4, 2, 128, 512), BF), vm((8, 1024), F32), vm((24, 128), F32),
        vm((1024, 1024), BF), vm((1024, 1024), BF), vm((1024, 1024), BF), vm((256, 1024), F32),
        vm((2, 8, 1024), F32), vm((8, 1024), jnp.int32),
        vm((2, 128, 1024), BF), vm((2, 1024, 128), BF), vm((128, 1024), BF), vm((1024, 128), BF),
        vm((1024, 128), BF), vm((128, 1024), BF),
        vm((1024, 512), F32), vm((1024, 512), BF), vm((512, 1024), BF), vm((2, 1024, 1024), BF),
        vm((128, 1024), BF), vm((1024, 128), BF), vm((2, 1024, 128), BF), vm((2, 128, 1024), BF),
        vm((1024, 512), BF), vm((512, 1024), BF), vm((128, 1024), F32), vm((1024, 128), F32), vm((1024, 128), F32),
        vm((1024, 384), BF), vm((384, 1024), BF),
    ]
    for _ in range(2):
        scratch += [
            vm((4, 2, 128, 1024), BF), vm((4, 128, 1024), BF), vm((3, 128, 1024), BF), vm((3, 128, 1024), BF),
            vm((128, 1024), BF), vm((128, 1024), BF),
        ]
    scratch += [vm((128, 1024), F32)]
    scratch += [
        vm((640, 1024), BF), vm((160, 1024), BF), vm((160, 1024), BF), vm((3, 160, 1024), BF), vm((80, 1024), BF),
        vm((160, 1024), BF), vm((80, 1024), BF),
    ]
    scratch += [
        vm((512, 1024), BF), vm((512, 512), BF), vm((512, 512), BF), vm((3, 128, 512), BF), vm((64, 512), BF),
        vm((128, 512), BF), vm((64, 512), BF), vm((4, 64, 128), BF),
        vm((384, 1024), BF), vm((384, 512), BF), vm((384, 512), BF), vm((7, 48, 512), BF), vm((48, 512), BF),
        vm((4, 48, 128), BF),
    ]
    scratch += [
        vm((4, 8, 1024), F32), vm((8, 1024), F32), vm((8, 512), F32), vm((8, 16, 128), F32), vm((7, 16, 128), F32),
        vm((16, 128), F32), vm((16, 128), F32), vm((16, 128), F32), vm((8, 16, 128), F32),
        pltpu.SemaphoreType.DMA((SEMS,)), pltpu.SemaphoreType.DMA((SEMS,)), pltpu.SemaphoreType.DMA((10,)),
    ]
    return pl.pallas_call(
        kernel,
        out_shape=(
            jax.ShapeDtypeStruct((128, 1024), BF), jax.ShapeDtypeStruct((128, 1024), BF),
            jax.ShapeDtypeStruct((512, 1024), BF), jax.ShapeDtypeStruct((128, 1024), BF),
            jax.ShapeDtypeStruct((128, 4096), BF),
            jax.ShapeDtypeStruct((128, 3072), BF),
        ) + tuple(jax.ShapeDtypeStruct((size,), F32) for size in (128, 128, 128, 128, 384, 128, 512, 128)),
        in_specs=[
            pl.BlockSpec(memory_space=pl.ANY if len(arg.shape) == 2 else pltpu.VMEM) for arg in args
        ],
        out_specs=[pl.BlockSpec(memory_space=pltpu.VMEM)] * 14,
        scratch_shapes=scratch,
        compiler_params=pltpu.CompilerParams(
            collective_id=0, has_side_effects=True, vmem_limit_bytes=62 * 2**20
        ),
    )(*args)


def shards(*args):
    out, ing, down, dense, up, qkv, v1, v2, v3, v4, vq, vd, vu, vw = block_call(*args)
    return (
        out, ing, v1, v2, v3, v4, qkv.astype(F32), vq, dense.astype(F32), vd, up.astype(F32), vu, down.astype(F32), vw,
    )


def solution(mesh):
    both, one, wide = P(("rep", "shard"), None), P("shard"), P("shard", None)
    placed = (
        both, both, P(("rep", "shard")), one, one, one, one, wide, one, wide, one, wide, one, wide, one,
    )
    return jax.shard_map(
        shards, mesh=mesh, in_specs=placed,
        out_specs=(both, both, one, one, one, one, wide, one, wide, one, wide, one, wide, one),
        check_vma=False,
    )
```

```python
import functools

import jax
import jax.numpy as jnp
from jax import lax
from jax.experimental import pallas as pl
from jax.experimental.pallas import tpu as pltpu
from jax.sharding import PartitionSpec as P

BF = jnp.bfloat16
F32 = jnp.float32
MESH = pl.DeviceIdType.MESH
SEMS = 176


def flip(value, mask):
    out = value
    bit = 1
    while bit <= mask:
        if mask & bit:
            out = out + bit - 2 * bit * lax.rem(lax.div(value, bit), 2)
        bit *= 2
    return out


def nt(left, right):
    return lax.dot_general(left, right, (((1,), (1,)), ((), ())), preferred_element_type=F32)


def nn(left, right):
    return jnp.dot(left, right, preferred_element_type=F32)


def fold(block):
    return jnp.sum(block.reshape(block.shape[0] // 8, 8, block.shape[1]), axis=0)


def kernel(
    hid_ref, g_ref, seg_ref, gain1_ref, shift1_ref, gain2_ref, shift2_ref, wqkv_ref, bqkv_ref, wdense_ref,
    bdense_ref, wup_ref, bup_ref, wdown_ref, bdown_ref,
    out_ref, ing_ref, f1_ref, f2_ref, f3_ref, vec_ref, PKO, SGO, SGX, WD, WN, OWNH, OWNG,
    HB, GB, SG, PK, WQ, WU, VEC, B24, XH, N1, N2, QKP, TAB, START, QTM, QM, KT, K, V, VT,
    GP, ACT, ACTT, PT, CTXT, CTX, DCM, DCTM, DG, DGT, DQT, DK, DV, M, MT,
    PB, PRA, PRT, PRZ, PFX, PRX, DB, DRA, DRT, DRZ, DFX, DRX, ACC,
    G1, X1, R1, S1, CY1, G2, X2, C2, R2, S2, G3, X3, C3, R3, S3,
    SUMS, CG, CDG, SV, SVR, LV, LVX, LC, LCR,
    ssem, rsem, lsem,
):
    r = lax.axis_index("rep")
    s = lax.axis_index("shard")
    k = lax.rem(r, 2)
    chip = lax.div(r, 2)
    y = lax.rem(chip, 4)
    h = lax.div(chip, 4)
    z = lax.div(s, 2)
    l = lax.rem(s, 2)
    b = 2 * z + k
    home = k == l
    off = k != l
    zs = (lax.rem(z + 2, 4), lax.rem(z + 1, 4), lax.rem(z + 3, 4))
    across_z, ahead, behind = zs

    def shard_to(m):
        return {"shard": flip(s, m)}

    def chip_to(m):
        return {"rep": flip(chip, m) * 2 + k}

    def z_to(zz):
        return {"shard": 2 * zz + l}

    partner = {"rep": chip * 2 + 1 - k}
    x_near = {"shard": 2 * z + 1 - l}
    x_far = {"rep": (1 - h) * 8 + y * 2 + k, "shard": 2 * z + 1 - l}
    x_cross = {"rep": chip * 2 + 1 - k, "shard": 2 * z + 1 - l}

    def lanes(start, size):
        return pl.ds(pl.multiple_of(start, 128), size)

    def rows(start, size):
        return pl.ds(pl.multiple_of(start, 16), size)

    barrier = pltpu.get_barrier_semaphore()
    peers = [shard_to(m) for m in range(1, 8)] + [chip_to(m) for m in range(1, 8)] + [partner, x_far, x_cross]
    peers += [{"rep": (4 * (1 - h) + y) * 2 + k, "shard": 2 * zz + l} for zz in zs]
    for peer in peers:
        pl.semaphore_signal(barrier, inc=1, device_id=peer, device_id_type=MESH)

    local = [
        pltpu.make_async_copy(hid_ref, OWNH, lsem.at[0]),
        pltpu.make_async_copy(g_ref, OWNG, lsem.at[1]),
        pltpu.make_async_copy(
            wup_ref.at[rows(32 * y, 32), lanes(512 * b, 512)], WU.at[z, l, rows(32 * y, 32)], lsem.at[2]),
    ]
    for j in range(3):
        local.append(pltpu.make_async_copy(
            wqkv_ref.at[:, lanes(1024 * j + 128 * b, 128)], WQ.at[z, l, :, 128 * j : 128 * j + 128], lsem.at[3 + j]))
    own_only = [
        pltpu.make_async_copy(hid_ref, HB.at[z, k], lsem.at[6]),
        pltpu.make_async_copy(g_ref, GB.at[z, k], lsem.at[7]),
        pltpu.make_async_copy(wdense_ref, WD, lsem.at[8]),
        pltpu.make_async_copy(wdown_ref, WN, lsem.at[9]),
    ]
    for copy in local:
        copy.start()

    @pl.when(home)
    def _():
        for copy in own_only:
            copy.start()

    PKO[...] = jnp.zeros_like(PKO)
    at = 0
    for ref in (gain1_ref, shift1_ref, gain2_ref, shift2_ref, bqkv_ref, bdense_ref, bup_ref, bdown_ref):
        size = ref.shape[0] // 128
        PKO[at : at + size] = ref[...].astype(F32).reshape(size, 128)
        at += size
    PK[s] = PKO[...]
    SGO[...] = jnp.broadcast_to(seg_ref[...].reshape(1, 128), (8, 128))
    SG[s] = SGO[...]
    for copy in local:
        copy.wait()

    @pl.when(home)
    def _():
        for copy in own_only:
            copy.wait()

    pl.semaphore_wait(barrier, len(peers))

    used = [0]
    sent = []

    class Copy:
        def __init__(self, src, dst, device, send, recv):
            at = used[0]
            used[0] += 1
            self.copy = pltpu.make_async_remote_copy(
                src_ref=src, dst_ref=dst, send_sem=ssem.at[at], recv_sem=rsem.at[at],
                device_id=device, device_id_type=MESH,
            )
            self.send = send
            self.recv = recv
            sent.append(self)
            self.under(send, self.copy.start)

        def under(self, role, action):
            if role is None:
                action()
            else:
                pl.when(role)(lambda: action())

        def wait_recv(self):
            self.under(self.recv, self.copy.wait_recv)

        def wait_send(self):
            self.under(self.send, self.copy.wait_send)

    def remote(src, dst, device, send=None, recv=None):
        return Copy(src, dst, device, send, recv)

    def arrived(copies):
        for copy in copies:
            copy.wait_recv()

    low = slice(0, 64)
    high = slice(64, 128)

    def same(ref, device):
        return remote(ref, ref, device)

    def gather_x(x_ref, XB):
        return remote(x_ref, XB.at[z, l], x_cross, off, off)

    def gather_z(first, XB):
        first.wait_recv()
        own = XB.at[z, k]
        return XB, same(own, z_to(ahead)), same(own, z_to(behind)), [same(own, partner)]

    def gather_next(state):
        XB, za, zb, cores = state
        za.wait_recv()
        d2a = same(XB.at[behind, k, low], z_to(ahead))
        cores.append(same(XB.at[behind, k], partner))
        zb.wait_recv()
        d2b = same(XB.at[ahead, k, high], z_to(behind))
        cores.append(same(XB.at[ahead, k], partner))
        return XB, d2a, d2b, cores

    def gather_straight(first, XB):
        first.wait_recv()
        own = XB.at[z, k]
        return [same(own, z_to(zz)) for zz in (across_z, ahead, behind)], [same(own, partner)]

    def gather_core(state, XB):
        copies, cores = state
        for copy, zz in zip(copies, (across_z, behind, ahead)):
            copy.wait_recv()
            cores.append(same(XB.at[zz, k], partner))
        return cores

    def gather_last(state):
        XB, d2a, d2b, cores = state
        arrived([d2a, d2b])
        cores.append(same(XB.at[across_z, k], partner))
        return cores

    def weight_z(ref, W, width, blocks):
        return [
            [remote(
                ref.at[:, lanes(1024 * j + width * (2 * zz + k), width)],
                W.at[z, l, :, width * j : width * j + width], z_to(zz)) for j in range(blocks)]
            for zz in (ahead, behind, across_z)
        ]

    def weight_x(W, zz):
        return [same(W.at[zz, l, low], x_near), same(W.at[zz, l, high], x_far)]

    y_peers = [{"rep": (4 * h + flip(y, m)) * 2 + k} for m in (1, 3, 2)]
    near32 = rows(32 * y, 16)
    far32 = rows(32 * y + 16, 16)
    both32 = rows(32 * y, 32)
    gather_h = gather_x(hid_ref, HB)
    up_z = [
        remote(wup_ref.at[both32, lanes(512 * (2 * zz + k), 512)], WU.at[z, l, both32], z_to(zz))
        for zz in (ahead, behind, across_z)
    ]
    qkv_z = weight_z(wqkv_ref, WQ, 128, 3)
    qkv_x = weight_x(WQ, z)
    gather_g = gather_x(g_ref, GB)
    gather_h = gather_z(gather_h, HB)
    small = [remote(PKO, PK.at[s], shard_to(m)) for m in range(1, 8)]
    small += [remote(SGO, SG.at[s], shard_to(m)) for m in range(1, 8)]
    arrived(up_z)
    up_x = [same(WU.at[:, l, near32], x_near), same(WU.at[:, l, far32], x_far)]
    for copies, zz in zip(qkv_z, (behind, ahead, across_z)):
        arrived(copies)
        qkv_x += weight_x(WQ, zz)
    arrived(up_x)
    up_y = [same(WU.at[:, :, both32], peer) for peer in y_peers]
    gather_h = gather_next(gather_h)
    gather_g = gather_straight(gather_g, GB)
    outer = [
        remote(wdown_ref.at[0:256], WN.at[0:256], x_near, home, off),
        remote(wdown_ref.at[256:512], WN.at[256:512], x_far, home, off),
        remote(wdense_ref.at[low], WD.at[low], x_near, home, off),
        remote(wdense_ref.at[high], WD.at[high], x_far, home, off),
    ]
    arrived(small)
    seg_core = remote(SG, SGX, partner)
    rest_h = gather_last(gather_h)

    for sp in range(8):
        block = PK[sp]
        at = slice(128 * sp, 128 * sp + 128)
        for j in range(4):
            VEC[j : j + 1, at] = block[j : j + 1]
        VEC[4:5, at] = block[7:8] + block[12:13]
        B24[3 * sp : 3 * sp + 3] = block[4:7]
    own = PK[b]
    bias_up = jnp.concatenate([own[8 + j : 9 + j] for j in range(4)], axis=1)
    bias_q = jnp.concatenate([B24[pl.ds(8 * j + b, 1)] for j in range(3)], axis=1)
    seg_core.wait_recv()
    ids = [jnp.where(home, SG[sp, 0:1], SGX[sp, 0:1]).astype(F32) for sp in range(8)]
    seg_row = jnp.concatenate(ids, axis=1)
    count = jnp.zeros((1, 1024), F32)
    for sp in range(8):
        column = jnp.transpose(jnp.broadcast_to(ids[sp], (128, 128)))[:, 0:1]
        count = count + jnp.sum((column < seg_row).astype(F32), axis=0, keepdims=True)
    START[...] = jnp.broadcast_to(count.astype(jnp.int32), (8, 1024))
    place = lax.broadcasted_iota(jnp.int32, (8, 1024), 1).astype(F32)
    row8 = lax.broadcasted_iota(jnp.int32, (8, 1024), 0)
    inverse = jnp.zeros((8, 1024), F32)
    for j in range(8):
        inverse = jnp.where(row8 == j, 10000.0 ** (-j / 8.0), inverse)
    angles = (place - count) * inverse
    TAB[0] = jnp.cos(angles)
    TAB[1] = jnp.sin(angles)
    gain1, shift1, gain2, shift2 = (VEC[j : j + 1] for j in range(4))

    arrived(qkv_x)

    def project(zz):
        at = rows(256 * zz, 256)
        cols = lanes(256 * zz, 256)
        block = HB[zz].reshape(256, 1024).astype(F32)
        center = block - jnp.mean(block, axis=-1, keepdims=True)
        spread = jnp.mean(center * center, axis=-1, keepdims=True)
        xhat = center * lax.rsqrt(spread + 1e-05)
        XH[at] = xhat.astype(BF)
        n1 = (xhat * gain1 + shift1).astype(BF)
        N1[at] = n1
        N2[at] = (xhat * gain2 + shift2).astype(BF)
        mixed = nn(n1, WQ[...].reshape(1024, 384)) + bias_q
        QKP[:, cols] = jnp.transpose(mixed[:, :256])
        V[at] = mixed[:, 256:].astype(BF)
        VT[:, cols] = jnp.transpose(mixed[:, 256:]).astype(BF)

    for copy, zz in zip(rest_h, (z, behind, ahead, across_z)):
        copy.wait_recv()
        project(zz)

    cosine = TAB[0]
    sine = TAB[1]
    for base in (0, 64, 128, 192):
        one = QKP[base : base + 8]
        two = QKP[base + 8 : base + 16]
        QKP[base : base + 8] = one * cosine - two * sine
        QKP[base + 8 : base + 16] = two * cosine + one * sine
    queries = QKP[0:128].astype(BF).astype(F32) * 0.125
    keys = QKP[128:256]
    low_rows = lax.broadcasted_iota(jnp.int32, (128, 1024), 0) < 64
    low_cols = lax.broadcasted_iota(jnp.int32, (1024, 128), 1) < 64
    QTM[0] = jnp.where(low_rows, queries, 0.0).astype(BF)
    QTM[1] = jnp.where(low_rows, 0.0, queries).astype(BF)
    back = jnp.transpose(queries)
    QM[0] = jnp.where(low_cols, back, 0.0).astype(BF)
    QM[1] = jnp.where(low_cols, 0.0, back).astype(BF)
    KT[...] = keys.astype(BF)
    K[...] = jnp.transpose(keys).astype(BF)

    def attention(head):
        hr = slice(64 * head, 64 * head + 64)
        for j in range(4):
            top = 256 * (j + 1)
            q = slice(256 * j, 256 * j + 256)
            scores = nn(K[0:top], QTM[head, :, q])
            ki = lax.broadcasted_iota(jnp.int32, (top, 256), 0)
            qi = lax.broadcasted_iota(jnp.int32, (top, 256), 1) + 256 * j
            allowed = (ki <= qi) & (ki >= START[0:1, q])
            scores = jnp.where(allowed, scores, -1e9)
            weight = jnp.exp(scores - jnp.max(scores, axis=0, keepdims=True))
            probs = (weight * (1.0 / jnp.sum(weight, axis=0, keepdims=True))).astype(BF)
            PT[head, 0:top, q] = probs
            CTXT[hr, q] = nn(VT[hr, 0:top], probs).astype(BF)

    attention(0)
    attention(1)

    def scatter_core(TB, RA):
        return [remote(TB.at[zz, 1 - k], RA.at[zz], partner) for zz in (across_z, ahead, behind, z)]

    def scatter_z(copies, TB, RA, RT, RZ):
        out = []
        for j, zz in enumerate(zs):
            copies[j].wait_recv()
            RT[j] = (TB[zz, k].astype(F32) + RA[zz].astype(F32)).astype(BF)
            out.append(remote(RT.at[j], RZ.at[j], z_to(zz)))
        copies[3].wait_recv()
        return out

    def scatter_x(copies, TB, RA, RZ, FX, RX):
        arrived(copies)
        total = TB[z, k].astype(F32) + RA[z].astype(F32)
        for j in range(3):
            total = total + RZ[j].astype(F32)
        ACC[...] = total
        FX[...] = total.astype(BF)
        return remote(FX, RX, x_cross, off, off)

    def scatter_end(copy, RX):
        copy.wait_recv()

        @pl.when(off)
        def _():
            ACC[...] = RX[...].astype(F32)

    CTX[...] = jnp.transpose(CTXT[...].astype(F32)).astype(BF)
    rest_g = gather_core(gather_g, GB)
    arrived(up_y)
    arrived(outer)

    @pl.loop(0, 4)
    def _(i):
        at = rows(256 * i, 256)
        cols = lanes(256 * i, 256)
        gate = nn(N2[at], WU[...].reshape(1024, 512)) + bias_up
        phi = 0.5 + 0.5 * lax.erf(gate * 0.7071067811865476)
        GP[at] = phi + gate * jnp.exp(-0.5 * gate * gate) * 0.3989422804014327
        active = gate * phi
        rounded = active.astype(BF)
        ACT[at] = rounded
        ACTT[:, cols] = jnp.transpose(active).astype(BF)
        total = nn(CTX[at], WD[...]) + nn(rounded, WN[...])
        PB[i] = total.astype(BF).reshape(2, 128, 1024)

    out_cores = scatter_core(PB, PRA)
    arrived(rest_g)

    def near_start(GR, X, size):
        part = lanes(512 * (1 - l), 512)
        top = slice(0, 4 * size)
        end = slice(4 * size, 8 * size)
        return [remote(GR.at[top, part], X.at[top], x_near), remote(GR.at[end, part], X.at[end], x_far)]

    def spread_start(near, GR, X, C, R, size):
        arrived(near)
        C[...] = (GR[:, lanes(512 * l, 512)].astype(F32) + X[...].astype(F32)).astype(BF)
        return [
            remote(
                C.at[rows(size * (2 * flip(y, m % 4) + flip(h, m // 4)), size)], R.at[m - 1], chip_to(m))
            for m in range(1, 8)
        ]

    def spread_sum(copies, C, R, S, size):
        arrived(copies)
        total = C[rows(size * (2 * y + h), size)].astype(F32)
        for m in range(7):
            total = total + R[m].astype(F32)
        S[...] = total.astype(BF)

    y_at = [flip(y, m) for m in (1, 3, 2)]
    h_peer = {"rep": (4 * (1 - h) + y) * 2 + k}

    def along_y(C, R, size):
        return [remote(C.at[rows(2 * size * yy, 2 * size)], R.at[m], y_peers[m]) for m, yy in enumerate(y_at)]

    def turn(S, out, size):
        at = rows(size * (2 * y + h), size)
        out[k, z, at] = S[:, lanes(128 * z, 128)]
        copies = []
        for zz in (across_z, ahead, behind, z):
            source = S.at[:, lanes(128 * zz, 128)]
            copies.append(remote(source, out.at[k, z, at], {"rep": (4 * (1 - h) + y) * 2 + k, "shard": 2 * zz + l}))
        for zz in (ahead, behind, across_z):
            copies.append(remote(S.at[:, lanes(128 * zz, 128)], out.at[k, z, at], z_to(zz)))
        return copies

    def quarter(out, yy, size):
        return out.at[k, :, rows(2 * size * yy, 2 * size)]

    def give_y(copies, out, size):
        arrived(copies)
        return [remote(quarter(out, y, size), quarter(out, y, size), peer) for peer in y_peers]

    def give_core(copies, out, size):
        last = [same(quarter(out, y, size), partner)]
        for copy, yy in zip(copies, y_at):
            copy.wait_recv()
            last.append(same(quarter(out, yy, size), partner))
        return last

    def put(GR, total):
        for sp in range(8):
            at = 512 * (sp % 2) + 128 * (sp // 2)
            GR[:, at : at + 128] = total[:, 128 * sp : 128 * sp + 128].astype(BF)

    grads = GB[...].reshape(1024, 1024)
    G1[0:512] = nn(ACTT[...], grads).astype(BF)
    G1[512:640] = nn(CTXT[...], grads).astype(BF)
    y1 = along_y(G1, R1, 80)

    low_256 = lax.broadcasted_iota(jnp.int32, (256, 128), 1) < 64
    low_t256 = lax.broadcasted_iota(jnp.int32, (128, 256), 0) < 64

    @pl.loop(0, 4)
    def _(i):
        at = rows(256 * i, 256)
        cols = lanes(256 * i, 256)
        grad = nt(GB[i].reshape(256, 1024), WD[...])
        DCM[0, at] = jnp.where(low_256, grad, 0.0).astype(BF)
        DCM[1, at] = jnp.where(low_256, 0.0, grad).astype(BF)
        turned = jnp.transpose(grad)
        DCTM[0, :, cols] = jnp.where(low_t256, turned, 0.0).astype(BF)
        DCTM[1, :, cols] = jnp.where(low_t256, 0.0, turned).astype(BF)

    DK[...] = jnp.zeros_like(DK)
    DV[...] = jnp.zeros_like(DV)

    def attention_back(head):
        hr = slice(64 * head, 64 * head + 64)
        for j in range(4):
            top = 256 * (j + 1)
            q = slice(256 * j, 256 * j + 256)
            probs = PT[head, 0:top, q]
            soft = probs.astype(F32)
            probs_grad = nn(V[0:top], DCTM[head, :, q])
            middle = jnp.sum(soft * probs_grad, axis=0, keepdims=True)
            score_grad = (soft * (probs_grad - middle)).astype(BF)
            DQT[hr, q] = nn(KT[hr, 0:top], score_grad) * 0.125
            DK[0:top] += nn(score_grad, QM[head, q])
            DV[0:top] += nn(probs, DCM[head, q])

    attention_back(0)
    out_z = scatter_z(out_cores, PB, PRA, PRT, PRZ)
    attention_back(1)

    QKP[0:128] = DQT[...]
    QKP[128:256] = jnp.transpose(DK[...])
    for base in (0, 64, 128, 192):
        one = QKP[base : base + 8]
        two = QKP[base + 8 : base + 16]
        QKP[base : base + 8] = one * cosine + two * sine
        QKP[base + 8 : base + 16] = two * cosine - one * sine
    MT[0:256] = QKP[...].astype(BF)
    MT[256:384] = jnp.transpose(DV[...]).astype(BF)

    put(G3, nn(MT[...], N1[...]))
    near3 = near_start(G3, X3, 48)
    M[:, 0:256] = jnp.transpose(QKP[...]).astype(BF)
    M[:, 256:384] = DV[...].astype(BF)
    CG[...] = jnp.zeros_like(CG)
    CDG[...] = jnp.zeros_like(CDG)

    @pl.loop(0, 4)
    def _(i):
        at = rows(256 * i, 256)
        cols = lanes(256 * i, 256)
        block = GB[i].reshape(256, 1024)
        CG[...] += fold(block.astype(F32))
        gate_grad = (nt(block, WN[...]) * GP[at]).astype(BF)
        DG[at] = gate_grad
        wide = gate_grad.astype(F32)
        CDG[...] += fold(wide)
        DGT[:, cols] = jnp.transpose(wide).astype(BF)

    put(G2, nn(DGT[...], N2[...]))
    near2 = near_start(G2, X2, 64)

    SUMS[...] = jnp.zeros_like(SUMS)
    in_cores = []
    in_z = []

    def norm_grads(zz):
        at = rows(256 * zz, 256)
        xhat = XH[at].astype(F32)
        one = nt(M[at], WQ[...].reshape(1024, 384))
        two = nt(DG[at], WU[...].reshape(1024, 512))
        DB[zz] = (one * gain1 + two * gain2).astype(BF).reshape(2, 128, 1024)
        in_cores.append(remote(DB.at[zz, 1 - k], DRA.at[zz], partner))
        SUMS[0] += fold(one * xhat)
        SUMS[1] += fold(one)
        SUMS[2] += fold(two * xhat)
        SUMS[3] += fold(two)

    def norm_send(j):
        zz = zs[j]
        in_cores[j].wait_recv()
        DRT[j] = (DB[zz, k].astype(F32) + DRA[zz].astype(F32)).astype(BF)
        in_z.append(remote(DRT.at[j], DRZ.at[j], z_to(zz)))

    norm_grads(across_z)
    spread3 = spread_start(near3, G3, X3, C3, R3, 48)
    norm_grads(ahead)
    norm_send(0)
    norm_grads(behind)
    norm_send(1)
    norm_grads(z)
    norm_send(2)
    arrived(y1)
    CY1[...] = (
        G1[rows(160 * y, 160)].astype(F32) + R1[0].astype(F32) + R1[1].astype(F32) + R1[2].astype(F32)
    ).astype(BF)
    x1 = [
        remote(CY1.at[rows(80 * h, 80)], X1.at[0], x_near, off, home),
        remote(CY1.at[rows(80 * (1 - h), 80)], X1.at[1], x_far, off, home),
        remote(CY1.at[rows(80 * (1 - h), 80)], X1.at[2], h_peer, home, home),
    ]
    out_x = scatter_x(out_z, PB, PRA, PRZ, PFX, PRX)

    SV[...] = jnp.zeros_like(SV)
    bias_grad = jnp.sum(fold(M[...].astype(F32)), axis=0, keepdims=True)
    B24[...] = jnp.zeros_like(B24)
    for j in range(3):
        B24[pl.ds(8 * j + b, 1)] = bias_grad[:, 128 * j : 128 * j + 128]
    for sp in range(8):
        at = slice(128 * sp, 128 * sp + 128)
        for j in range(4):
            SV[sp, j : j + 1] = jnp.sum(SUMS[j, :, at], axis=0, keepdims=True)
        SV[sp, 4:7] = B24[3 * sp : 3 * sp + 3]
    up_grad = jnp.sum(CDG[...], axis=0, keepdims=True)
    for j in range(4):
        SV[b, 8 + j : 9 + j] = up_grad[:, 128 * j : 128 * j + 128]
    SV[b, 12:13] = jnp.sum(CG[:, lanes(128 * b, 128)], axis=0, keepdims=True)
    vectors = [remote(SV.at[flip(s, m)], SVR.at[m - 1], shard_to(m)) for m in range(1, 8)]

    spread2 = spread_start(near2, G2, X2, C2, R2, 64)
    spread_sum(spread3, C3, R3, S3, 48)
    turn3 = turn(S3, f3_ref, 48)
    arrived(x1)

    @pl.when(home)
    def _():
        S1[...] = (
            CY1[rows(80 * h, 80)].astype(F32) + X1[0].astype(F32) + X1[1].astype(F32) + X1[2].astype(F32)
        ).astype(BF)
        f1_ref[y, h] = S1[...]

    give1 = [remote(S1, f1_ref.at[y, h], chip_to(m), home, home) for m in range(1, 8)]
    scatter_end(out_x, PRX)
    out_ref[...] = (OWNH[...].astype(F32) + ACC[...] + VEC[4:5]).astype(BF)
    give3 = give_y(turn3, f3_ref, 48)
    arrived(vectors)
    total = SV[s]
    for m in range(7):
        total = total + SVR[m]
    LV[...] = total
    pair_v = remote(LV, LVX, partner)
    spread_sum(spread2, C2, R2, S2, 64)
    turn2 = turn(S2, f2_ref, 64)
    in_cores[3].wait_recv()
    in_x = scatter_x(in_z, DB, DRA, DRZ, DFX, DRX)
    pair_v.wait_recv()
    LC[...] = LV[...] + LVX[...]
    LCR[chip] = LC[...]
    spread_v = [remote(LC, LCR.at[chip], chip_to(m)) for m in range(1, 8)]
    give2 = give_y(turn2, f2_ref, 64)
    arrived(give1)
    last1 = [remote(f1_ref, f1_ref, partner, home, off)]
    last3 = give_core(give3, f3_ref, 48)

    scatter_end(in_x, DRX)
    block = OWNH[...].astype(F32)
    center = block - jnp.mean(block, axis=-1, keepdims=True)
    spread = jnp.mean(center * center, axis=-1, keepdims=True)
    scale = lax.rsqrt(spread + 1e-05)
    xhat = center * scale
    grad = ACC[...]
    grad = grad - jnp.mean(grad, axis=-1, keepdims=True) - xhat * jnp.mean(grad * xhat, axis=-1, keepdims=True)
    ing_ref[...] = (OWNG[...].astype(F32) + scale * grad).astype(BF)

    arrived(spread_v)
    total = LCR[0]
    for m in range(1, 8):
        total = total + LCR[m]
    vec_ref[...] = total
    last2 = give_core(give2, f2_ref, 64)
    arrived(last1)
    arrived(last2)
    arrived(last3)
    for copy in sent:
        copy.wait_send()
    assert used[0] <= SEMS, used[0]


def block_call(*args):
    vm = pltpu.VMEM
    scratch = [
        vm((16, 128), F32), vm((8, 128), jnp.int32),
        vm((8, 8, 128), jnp.int32), vm((128, 1024), BF), vm((512, 1024), BF), vm((128, 1024), BF), vm((128, 1024), BF),
        vm((4, 2, 128, 1024), BF), vm((4, 2, 128, 1024), BF), vm((8, 8, 128), jnp.int32), vm((8, 16, 128), F32),
        vm((4, 2, 128, 384), BF), vm((4, 2, 128, 512), BF), vm((8, 1024), F32), vm((24, 128), F32),
        vm((1024, 1024), BF), vm((1024, 1024), BF), vm((1024, 1024), BF), vm((256, 1024), F32),
        vm((2, 8, 1024), F32), vm((8, 1024), jnp.int32),
        vm((2, 128, 1024), BF), vm((2, 1024, 128), BF), vm((128, 1024), BF), vm((1024, 128), BF),
        vm((1024, 128), BF), vm((128, 1024), BF),
        vm((1024, 512), F32), vm((1024, 512), BF), vm((512, 1024), BF), vm((2, 1024, 1024), BF),
        vm((128, 1024), BF), vm((1024, 128), BF), vm((2, 1024, 128), BF), vm((2, 128, 1024), BF),
        vm((1024, 512), BF), vm((512, 1024), BF), vm((128, 1024), F32), vm((1024, 128), F32), vm((1024, 128), F32),
        vm((1024, 384), BF), vm((384, 1024), BF),
    ]
    for _ in range(2):
        scratch += [
            vm((4, 2, 128, 1024), BF), vm((4, 128, 1024), BF), vm((3, 128, 1024), BF), vm((3, 128, 1024), BF),
            vm((128, 1024), BF), vm((128, 1024), BF),
        ]
    scratch += [vm((128, 1024), F32)]
    scratch += [
        vm((640, 1024), BF), vm((3, 80, 1024), BF), vm((3, 160, 1024), BF), vm((80, 1024), BF), vm((160, 1024), BF),
    ]
    scratch += [
        vm((512, 1024), BF), vm((512, 512), BF), vm((512, 512), BF), vm((7, 64, 512), BF), vm((64, 512), BF),
        vm((384, 1024), BF), vm((384, 512), BF), vm((384, 512), BF), vm((7, 48, 512), BF), vm((48, 512), BF),
    ]
    scratch += [
        vm((4, 8, 1024), F32), vm((8, 1024), F32), vm((8, 512), F32), vm((8, 16, 128), F32), vm((7, 16, 128), F32),
        vm((16, 128), F32), vm((16, 128), F32), vm((16, 128), F32), vm((8, 16, 128), F32),
        pltpu.SemaphoreType.DMA((SEMS,)), pltpu.SemaphoreType.DMA((SEMS,)), pltpu.SemaphoreType.DMA((10,)),
    ]
    return pl.pallas_call(
        kernel,
        out_shape=(
            jax.ShapeDtypeStruct((128, 1024), BF), jax.ShapeDtypeStruct((128, 1024), BF),
            jax.ShapeDtypeStruct((4, 2, 80, 1024), BF), jax.ShapeDtypeStruct((2, 4, 512, 128), BF),
            jax.ShapeDtypeStruct((2, 4, 384, 128), BF), jax.ShapeDtypeStruct((16, 128), F32),
        ),
        in_specs=[
            pl.BlockSpec(memory_space=pl.ANY if len(arg.shape) == 2 else pltpu.VMEM) for arg in args
        ],
        out_specs=[pl.BlockSpec(memory_space=pltpu.VMEM)] * 6,
        scratch_shapes=scratch,
        compiler_params=pltpu.CompilerParams(
            collective_id=0, has_side_effects=True, vmem_limit_bytes=62 * 2**20
        ),
    )(*args)


def finish(
    out_in, ing_in, f1_in, f2_in, f3_in, vec_ref,
    out_ref, ing_ref, v1_ref, v2_ref, v3_ref, v4_ref, qkv_ref, vq_ref, dense_ref, vd_ref, up_ref, vu_ref, down_ref,
    vw_ref, B1, B2, B3, B4, B5, O1, O2, O3, sems,
):
    take = [
        pltpu.make_async_copy(f3_in, B3, sems.at[0]),
        pltpu.make_async_copy(f2_in, B2, sems.at[1]),
        pltpu.make_async_copy(f1_in, B1, sems.at[2]),
        pltpu.make_async_copy(out_in, B4, sems.at[3]),
        pltpu.make_async_copy(ing_in, B5, sems.at[4]),
    ]
    for copy in take:
        copy.start()
    for ref, at in (
        (v1_ref, 0), (v2_ref, 1), (v3_ref, 2), (v4_ref, 3), (vq_ref, 4), (vu_ref, 8), (vd_ref, 12), (vw_ref, 12)
    ):
        size = ref.shape[0]
        ref[...] = vec_ref[at : at + size // 128].reshape(size)
    put = []

    def give(source, target):
        copy = pltpu.make_async_copy(source, target, sems.at[5 + len(put)])
        copy.start()
        put.append(copy)

    take[0].wait()
    for j in range(3):
        for sp in range(8):
            at = 1024 * j + 128 * sp
            O3[:, at : at + 128] = jnp.transpose(B3[sp % 2, sp // 2, 128 * j : 128 * j + 128].astype(F32))
        part = slice(1024 * j, 1024 * j + 1024)
        give(O3.at[:, part], qkv_ref.at[:, part])
    take[1].wait()
    for sp in range(8):
        for j in range(4):
            at = 512 * sp + 128 * j
            O2[:, at : at + 128] = jnp.transpose(B2[sp % 2, sp // 2, 128 * j : 128 * j + 128].astype(F32))
        if sp % 2:
            part = slice(512 * sp - 512, 512 * sp + 512)
            give(O2.at[:, part], up_ref.at[:, part])
    take[3].wait()
    give(B4, out_ref)
    take[4].wait()
    give(B5, ing_ref)
    take[2].wait()
    for j in range(4):
        O1[160 * j : 160 * j + 160] = B1[j].astype(F32).reshape(160, 1024)
        if j < 3:
            give(O1.at[160 * j : 160 * j + 160], down_ref.at[160 * j : 160 * j + 160])
    give(O1.at[480:512], down_ref.at[480:512])
    give(O1.at[512:640], dense_ref)
    for copy in put:
        copy.wait()


def shards(*args):
    given = block_call(*args)
    vm = pltpu.VMEM
    any_, whole = pl.BlockSpec(memory_space=pl.ANY), pl.BlockSpec(memory_space=vm)

    def flat(size):
        return jax.ShapeDtypeStruct((size,), F32)

    def wide(rows, columns, kind=F32):
        return jax.ShapeDtypeStruct((rows, columns), kind)

    return pl.pallas_call(
        finish,
        out_shape=(
            wide(128, 1024, BF), wide(128, 1024, BF), flat(128), flat(128), flat(128), flat(128), wide(128, 3072),
            flat(384), wide(128, 1024), flat(128), wide(128, 4096), flat(512), wide(512, 1024), flat(128),
        ),
        in_specs=[any_] * 5 + [whole],
        out_specs=[
            any_, any_, whole, whole, whole, whole, any_, whole, any_, whole, any_, whole, any_, whole,
        ],
        scratch_shapes=[
            vm((4, 2, 80, 1024), BF), vm((2, 4, 512, 128), BF), vm((2, 4, 384, 128), BF),
            vm((128, 1024), BF), vm((128, 1024), BF), vm((640, 1024), F32),
            vm((128, 4096), F32), vm((128, 3072), F32), pltpu.SemaphoreType.DMA((20,)),
        ],
        compiler_params=pltpu.CompilerParams(vmem_limit_bytes=62 * 2**20),
    )(*given)


def solution(mesh):
    both, one, wide = P(("rep", "shard"), None), P("shard"), P("shard", None)
    placed = (
        both, both, P(("rep", "shard")), one, one, one, one, wide, one, wide, one, wide, one, wide, one,
    )
    return jax.shard_map(
        shards, mesh=mesh, in_specs=placed,
        out_specs=(both, both, one, one, one, one, wide, one, wide, one, wide, one, wide, one),
        check_vma=False,
    )
```

```python
import functools

import jax
import jax.numpy as jnp
from jax import lax
from jax.experimental import pallas as pl
from jax.experimental.pallas import tpu as pltpu
from jax.sharding import PartitionSpec as P

BF = jnp.bfloat16
F32 = jnp.float32
MESH = pl.DeviceIdType.MESH
SEMS = 176


def flip(value, mask):
    out = value
    bit = 1
    while bit <= mask:
        if mask & bit:
            out = out + bit - 2 * bit * lax.rem(lax.div(value, bit), 2)
        bit *= 2
    return out


def nt(left, right):
    return lax.dot_general(left, right, (((1,), (1,)), ((), ())), preferred_element_type=F32)


def nn(left, right):
    return jnp.dot(left, right, preferred_element_type=F32)


def fold(block):
    return jnp.sum(block.reshape(block.shape[0] // 8, 8, block.shape[1]), axis=0)


def kernel(
    hid_ref, g_ref, seg_ref, gain1_ref, shift1_ref, gain2_ref, shift2_ref, wqkv_ref, bqkv_ref, wdense_ref,
    bdense_ref, wup_ref, bup_ref, wdown_ref, bdown_ref,
    out_ref, ing_ref, f1_ref, f2_ref, f3_ref, vec_ref, PKO, SGO, SGX, WD, WN, OWNH, OWNG,
    HB, GB, SG, PK, WQ, WU, VEC, B24, XH, N1, N2, QKP, TAB, START, QTM, QM, KT, K, V, VT,
    GP, ACT, ACTT, PT, CTXT, CTX, DCM, DCTM, DG, DGT, DQT, DK, DV, M, MT,
    PB, PRA, PRT, PRZ, PFX, PRX, DB, DRA, DRT, DRZ, DFX, DRX, ACC,
    G1, X1, R1, S1, CY1, G2, X2, C2, R2, S2, G3, X3, C3, R3, S3,
    SUMS, CG, CDG, SV, SVR, LV, LVX, LC, LCR,
    ssem, rsem, lsem,
):
    r = lax.axis_index("rep")
    s = lax.axis_index("shard")
    k = lax.rem(r, 2)
    chip = lax.div(r, 2)
    y = lax.rem(chip, 4)
    h = lax.div(chip, 4)
    z = lax.div(s, 2)
    l = lax.rem(s, 2)
    b = 2 * z + k
    home = k == l
    off = k != l
    zs = (lax.rem(z + 2, 4), lax.rem(z + 1, 4), lax.rem(z + 3, 4))
    across_z, ahead, behind = zs

    def shard_to(m):
        return {"shard": flip(s, m)}

    def chip_to(m):
        return {"rep": flip(chip, m) * 2 + k}

    def z_to(zz):
        return {"shard": 2 * zz + l}

    partner = {"rep": chip * 2 + 1 - k}
    x_near = {"shard": 2 * z + 1 - l}
    x_far = {"rep": (1 - h) * 8 + y * 2 + k, "shard": 2 * z + 1 - l}
    x_cross = {"rep": chip * 2 + 1 - k, "shard": 2 * z + 1 - l}

    def lanes(start, size):
        return pl.ds(pl.multiple_of(start, 128), size)

    def rows(start, size):
        return pl.ds(pl.multiple_of(start, 16), size)

    barrier = pltpu.get_barrier_semaphore()
    peers = [shard_to(m) for m in range(1, 8)] + [chip_to(m) for m in range(1, 8)] + [partner, x_far, x_cross]
    peers += [{"rep": (4 * (1 - h) + y) * 2 + k, "shard": 2 * zz + l} for zz in zs]
    for peer in peers:
        pl.semaphore_signal(barrier, inc=1, device_id=peer, device_id_type=MESH)

    local = [
        pltpu.make_async_copy(hid_ref, OWNH, lsem.at[0]),
        pltpu.make_async_copy(g_ref, OWNG, lsem.at[1]),
        pltpu.make_async_copy(
            wup_ref.at[rows(32 * y, 32), lanes(512 * b, 512)], WU.at[z, l, rows(32 * y, 32)], lsem.at[2]),
    ]
    for j in range(3):
        local.append(pltpu.make_async_copy(
            wqkv_ref.at[:, lanes(1024 * j + 128 * b, 128)], WQ.at[z, l, :, 128 * j : 128 * j + 128], lsem.at[3 + j]))
    own_only = [
        pltpu.make_async_copy(hid_ref, HB.at[z, k], lsem.at[6]),
        pltpu.make_async_copy(g_ref, GB.at[z, k], lsem.at[7]),
        pltpu.make_async_copy(wdense_ref, WD, lsem.at[8]),
        pltpu.make_async_copy(wdown_ref, WN, lsem.at[9]),
    ]
    for copy in local:
        copy.start()

    @pl.when(home)
    def _():
        for copy in own_only:
            copy.start()

    PKO[...] = jnp.zeros_like(PKO)
    at = 0
    for ref in (gain1_ref, shift1_ref, gain2_ref, shift2_ref, bqkv_ref, bdense_ref, bup_ref, bdown_ref):
        size = ref.shape[0] // 128
        PKO[at : at + size] = ref[...].astype(F32).reshape(size, 128)
        at += size
    PK[s] = PKO[...]
    SGO[...] = jnp.broadcast_to(seg_ref[...].reshape(1, 128), (8, 128))
    SG[s] = SGO[...]
    for copy in local:
        copy.wait()

    @pl.when(home)
    def _():
        for copy in own_only:
            copy.wait()

    pl.semaphore_wait(barrier, len(peers))

    used = [0]
    sent = []

    class Copy:
        def __init__(self, src, dst, device, send, recv):
            at = used[0]
            used[0] += 1
            self.copy = pltpu.make_async_remote_copy(
                src_ref=src, dst_ref=dst, send_sem=ssem.at[at], recv_sem=rsem.at[at],
                device_id=device, device_id_type=MESH,
            )
            self.send = send
            self.recv = recv
            sent.append(self)
            self.under(send, self.copy.start)

        def under(self, role, action):
            if role is None:
                action()
            else:
                pl.when(role)(lambda: action())

        def wait_recv(self):
            self.under(self.recv, self.copy.wait_recv)

        def wait_send(self):
            self.under(self.send, self.copy.wait_send)

    def remote(src, dst, device, send=None, recv=None):
        return Copy(src, dst, device, send, recv)

    def arrived(copies):
        for copy in copies:
            copy.wait_recv()

    low = slice(0, 64)
    high = slice(64, 128)

    def same(ref, device):
        return remote(ref, ref, device)

    def gather_x(x_ref, XB):
        return remote(x_ref, XB.at[z, l], x_cross, off, off)

    def gather_z(first, XB):
        first.wait_recv()
        own = XB.at[z, k]
        return XB, same(own, z_to(ahead)), same(own, z_to(behind)), [same(own, partner)]

    def gather_next(state):
        XB, za, zb, cores = state
        za.wait_recv()
        d2a = same(XB.at[behind, k, low], z_to(ahead))
        cores.append(same(XB.at[behind, k], partner))
        zb.wait_recv()
        d2b = same(XB.at[ahead, k, high], z_to(behind))
        cores.append(same(XB.at[ahead, k], partner))
        return XB, d2a, d2b, cores

    def gather_straight(first, XB):
        first.wait_recv()
        own = XB.at[z, k]
        return [same(own, z_to(zz)) for zz in (across_z, ahead, behind)], [same(own, partner)]

    def gather_core(state, XB):
        copies, cores = state
        for copy, zz in zip(copies, (across_z, behind, ahead)):
            copy.wait_recv()
            cores.append(same(XB.at[zz, k], partner))
        return cores

    def gather_last(state):
        XB, d2a, d2b, cores = state
        arrived([d2a, d2b])
        cores.append(same(XB.at[across_z, k], partner))
        return cores

    def weight_z(ref, W, width, blocks):
        return [
            [remote(
                ref.at[:, lanes(1024 * j + width * (2 * zz + k), width)],
                W.at[z, l, :, width * j : width * j + width], z_to(zz)) for j in range(blocks)]
            for zz in (ahead, behind, across_z)
        ]

    def weight_x(W, zz):
        return [same(W.at[zz, l, low], x_near), same(W.at[zz, l, high], x_far)]

    y_peers = [{"rep": (4 * h + flip(y, m)) * 2 + k} for m in (1, 3, 2)]
    near32 = rows(32 * y, 16)
    far32 = rows(32 * y + 16, 16)
    both32 = rows(32 * y, 32)
    gather_h = gather_x(hid_ref, HB)
    up_z = [
        remote(wup_ref.at[both32, lanes(512 * (2 * zz + k), 512)], WU.at[z, l, both32], z_to(zz))
        for zz in (ahead, behind, across_z)
    ]
    qkv_z = weight_z(wqkv_ref, WQ, 128, 3)
    qkv_x = weight_x(WQ, z)
    gather_g = gather_x(g_ref, GB)
    gather_h = gather_z(gather_h, HB)
    small = [remote(PKO, PK.at[s], shard_to(m)) for m in range(1, 8)]
    small += [remote(SGO, SG.at[s], shard_to(m)) for m in range(1, 8)]
    arrived(up_z)
    up_x = [same(WU.at[:, l, near32], x_near), same(WU.at[:, l, far32], x_far)]
    for copies, zz in zip(qkv_z, (behind, ahead, across_z)):
        arrived(copies)
        qkv_x += weight_x(WQ, zz)
    arrived(up_x)
    up_y = [same(WU.at[:, :, both32], peer) for peer in y_peers]
    gather_h = gather_next(gather_h)
    gather_g = gather_straight(gather_g, GB)
    outer = [
        remote(wdown_ref.at[0:256], WN.at[0:256], x_near, home, off),
        remote(wdown_ref.at[256:512], WN.at[256:512], x_far, home, off),
        remote(wdense_ref.at[low], WD.at[low], x_near, home, off),
        remote(wdense_ref.at[high], WD.at[high], x_far, home, off),
    ]
    arrived(small)
    seg_core = remote(SG, SGX, partner)
    rest_h = gather_last(gather_h)

    for sp in range(8):
        block = PK[sp]
        at = slice(128 * sp, 128 * sp + 128)
        for j in range(4):
            VEC[j : j + 1, at] = block[j : j + 1]
        VEC[4:5, at] = block[7:8] + block[12:13]
        B24[3 * sp : 3 * sp + 3] = block[4:7]
    own = PK[b]
    bias_up = jnp.concatenate([own[8 + j : 9 + j] for j in range(4)], axis=1)
    bias_q = jnp.concatenate([B24[pl.ds(8 * j + b, 1)] for j in range(3)], axis=1)
    seg_core.wait_recv()
    ids = [jnp.where(home, SG[sp, 0:1], SGX[sp, 0:1]).astype(F32) for sp in range(8)]
    seg_row = jnp.concatenate(ids, axis=1)
    count = jnp.zeros((1, 1024), F32)
    for sp in range(8):
        column = jnp.transpose(jnp.broadcast_to(ids[sp], (128, 128)))[:, 0:1]
        count = count + jnp.sum((column < seg_row).astype(F32), axis=0, keepdims=True)
    START[...] = jnp.broadcast_to(count.astype(jnp.int32), (8, 1024))
    place = lax.broadcasted_iota(jnp.int32, (8, 1024), 1).astype(F32)
    row8 = lax.broadcasted_iota(jnp.int32, (8, 1024), 0)
    inverse = jnp.zeros((8, 1024), F32)
    for j in range(8):
        inverse = jnp.where(row8 == j, 10000.0 ** (-j / 8.0), inverse)
    angles = (place - count) * inverse
    TAB[0] = jnp.cos(angles)
    TAB[1] = jnp.sin(angles)
    gain1, shift1, gain2, shift2 = (VEC[j : j + 1] for j in range(4))

    arrived(qkv_x)

    def project(zz):
        at = rows(256 * zz, 256)
        cols = lanes(256 * zz, 256)
        block = HB[zz].reshape(256, 1024).astype(F32)
        center = block - jnp.mean(block, axis=-1, keepdims=True)
        spread = jnp.mean(center * center, axis=-1, keepdims=True)
        xhat = center * lax.rsqrt(spread + 1e-05)
        XH[at] = xhat.astype(BF)
        n1 = (xhat * gain1 + shift1).astype(BF)
        N1[at] = n1
        N2[at] = (xhat * gain2 + shift2).astype(BF)
        mixed = nn(n1, WQ[...].reshape(1024, 384)) + bias_q
        QKP[:, cols] = jnp.transpose(mixed[:, :256])
        V[at] = mixed[:, 256:].astype(BF)
        VT[:, cols] = jnp.transpose(mixed[:, 256:]).astype(BF)

    for copy, zz in zip(rest_h, (z, behind, ahead, across_z)):
        copy.wait_recv()
        project(zz)

    cosine = TAB[0]
    sine = TAB[1]
    for base in (0, 64, 128, 192):
        one = QKP[base : base + 8]
        two = QKP[base + 8 : base + 16]
        QKP[base : base + 8] = one * cosine - two * sine
        QKP[base + 8 : base + 16] = two * cosine + one * sine
    queries = QKP[0:128].astype(BF).astype(F32) * 0.125
    keys = QKP[128:256]
    low_rows = lax.broadcasted_iota(jnp.int32, (128, 1024), 0) < 64
    low_cols = lax.broadcasted_iota(jnp.int32, (1024, 128), 1) < 64
    QTM[0] = jnp.where(low_rows, queries, 0.0).astype(BF)
    QTM[1] = jnp.where(low_rows, 0.0, queries).astype(BF)
    back = jnp.transpose(queries)
    QM[0] = jnp.where(low_cols, back, 0.0).astype(BF)
    QM[1] = jnp.where(low_cols, 0.0, back).astype(BF)
    KT[...] = keys.astype(BF)
    K[...] = jnp.transpose(keys).astype(BF)

    def attention(head):
        hr = slice(64 * head, 64 * head + 64)
        for j in range(4):
            top = 256 * (j + 1)
            q = slice(256 * j, 256 * j + 256)
            scores = nn(K[0:top], QTM[head, :, q])
            ki = lax.broadcasted_iota(jnp.int32, (top, 256), 0)
            qi = lax.broadcasted_iota(jnp.int32, (top, 256), 1) + 256 * j
            allowed = (ki <= qi) & (ki >= START[0:1, q])
            scores = jnp.where(allowed, scores, -1e9)
            weight = jnp.exp(scores - jnp.max(scores, axis=0, keepdims=True))
            probs = (weight * (1.0 / jnp.sum(weight, axis=0, keepdims=True))).astype(BF)
            PT[head, 0:top, q] = probs
            CTXT[hr, q] = nn(VT[hr, 0:top], probs).astype(BF)

    attention(0)
    attention(1)

    def scatter_core(TB, RA):
        return [remote(TB.at[zz, 1 - k], RA.at[zz], partner) for zz in (across_z, ahead, behind, z)]

    def scatter_z(copies, TB, RA, RT, RZ):
        out = []
        for j, zz in enumerate(zs):
            copies[j].wait_recv()
            RT[j] = (TB[zz, k].astype(F32) + RA[zz].astype(F32)).astype(BF)
            out.append(remote(RT.at[j], RZ.at[j], z_to(zz)))
        copies[3].wait_recv()
        return out

    def scatter_x(copies, TB, RA, RZ, FX, RX):
        arrived(copies)
        total = TB[z, k].astype(F32) + RA[z].astype(F32)
        for j in range(3):
            total = total + RZ[j].astype(F32)
        ACC[...] = total
        FX[...] = total.astype(BF)
        return remote(FX, RX, x_cross, off, off)

    def scatter_end(copy, RX):
        copy.wait_recv()

        @pl.when(off)
        def _():
            ACC[...] = RX[...].astype(F32)

    CTX[...] = jnp.transpose(CTXT[...].astype(F32)).astype(BF)
    rest_g = gather_core(gather_g, GB)
    arrived(up_y)
    arrived(outer)

    @pl.loop(0, 4)
    def _(i):
        at = rows(256 * i, 256)
        cols = lanes(256 * i, 256)
        gate = nn(N2[at], WU[...].reshape(1024, 512)) + bias_up
        phi = 0.5 + 0.5 * lax.erf(gate * 0.7071067811865476)
        GP[at] = phi + gate * jnp.exp(-0.5 * gate * gate) * 0.3989422804014327
        active = gate * phi
        rounded = active.astype(BF)
        ACT[at] = rounded
        ACTT[:, cols] = jnp.transpose(active).astype(BF)
        total = nn(CTX[at], WD[...]) + nn(rounded, WN[...])
        PB[i] = total.astype(BF).reshape(2, 128, 1024)

    out_cores = scatter_core(PB, PRA)
    arrived(rest_g)

    def near_start(GR, X, size):
        part = lanes(512 * (1 - l), 512)
        top = slice(0, 4 * size)
        end = slice(4 * size, 8 * size)
        return [remote(GR.at[top, part], X.at[top], x_near), remote(GR.at[end, part], X.at[end], x_far)]

    def spread_start(near, GR, X, C, R, size):
        arrived(near)
        C[...] = (GR[:, lanes(512 * l, 512)].astype(F32) + X[...].astype(F32)).astype(BF)
        return [
            remote(
                C.at[rows(size * (2 * flip(y, m % 4) + flip(h, m // 4)), size)], R.at[m - 1], chip_to(m))
            for m in range(1, 8)
        ]

    def spread_sum(copies, C, R, S, size):
        arrived(copies)
        total = C[rows(size * (2 * y + h), size)].astype(F32)
        for m in range(7):
            total = total + R[m].astype(F32)
        S[...] = total.astype(BF)

    y_at = [flip(y, m) for m in (1, 3, 2)]
    h_peer = {"rep": (4 * (1 - h) + y) * 2 + k}

    def along_y(C, R, size):
        return [remote(C.at[rows(2 * size * yy, 2 * size)], R.at[m], y_peers[m]) for m, yy in enumerate(y_at)]

    def turn(S, out, size):
        at = rows(size * (2 * y + h), size)
        out[k, z, at] = S[:, lanes(128 * z, 128)]
        copies = []
        for zz in (across_z, ahead, behind, z):
            source = S.at[:, lanes(128 * zz, 128)]
            copies.append(remote(source, out.at[k, z, at], {"rep": (4 * (1 - h) + y) * 2 + k, "shard": 2 * zz + l}))
        for zz in (ahead, behind, across_z):
            copies.append(remote(S.at[:, lanes(128 * zz, 128)], out.at[k, z, at], z_to(zz)))
        return copies

    def quarter(out, yy, size):
        return out.at[k, :, rows(2 * size * yy, 2 * size)]

    def give_y(copies, out, size):
        arrived(copies)
        return [remote(quarter(out, y, size), quarter(out, y, size), peer) for peer in y_peers]

    def give_core(copies, out, size):
        last = [same(quarter(out, y, size), partner)]
        for copy, yy in zip(copies, y_at):
            copy.wait_recv()
            last.append(same(quarter(out, yy, size), partner))
        return last

    def put(GR, total):
        for sp in range(8):
            at = 512 * (sp % 2) + 128 * (sp // 2)
            GR[:, at : at + 128] = total[:, 128 * sp : 128 * sp + 128].astype(BF)

    grads = GB[...].reshape(1024, 1024)
    G1[0:512] = nn(ACTT[...], grads).astype(BF)
    G1[512:640] = nn(CTXT[...], grads).astype(BF)
    y1 = along_y(G1, R1, 80)

    CG[...] = jnp.zeros_like(CG)
    CDG[...] = jnp.zeros_like(CDG)

    @pl.loop(0, 4)
    def _(i):
        at = rows(256 * i, 256)
        cols = lanes(256 * i, 256)
        block = GB[i].reshape(256, 1024)
        CG[...] += fold(block.astype(F32))
        gate_grad = (nt(block, WN[...]) * GP[at]).astype(BF)
        DG[at] = gate_grad
        wide = gate_grad.astype(F32)
        CDG[...] += fold(wide)
        DGT[:, cols] = jnp.transpose(wide).astype(BF)

    put(G2, nn(DGT[...], N2[...]))
    near2 = near_start(G2, X2, 64)
    out_z = scatter_z(out_cores, PB, PRA, PRT, PRZ)

    low_256 = lax.broadcasted_iota(jnp.int32, (256, 128), 1) < 64
    low_t256 = lax.broadcasted_iota(jnp.int32, (128, 256), 0) < 64

    @pl.loop(0, 4)
    def _(i):
        at = rows(256 * i, 256)
        cols = lanes(256 * i, 256)
        grad = nt(GB[i].reshape(256, 1024), WD[...])
        DCM[0, at] = jnp.where(low_256, grad, 0.0).astype(BF)
        DCM[1, at] = jnp.where(low_256, 0.0, grad).astype(BF)
        turned = jnp.transpose(grad)
        DCTM[0, :, cols] = jnp.where(low_t256, turned, 0.0).astype(BF)
        DCTM[1, :, cols] = jnp.where(low_t256, 0.0, turned).astype(BF)

    DK[...] = jnp.zeros_like(DK)
    DV[...] = jnp.zeros_like(DV)

    def attention_back(head):
        hr = slice(64 * head, 64 * head + 64)
        for j in range(4):
            top = 256 * (j + 1)
            q = slice(256 * j, 256 * j + 256)
            probs = PT[head, 0:top, q]
            soft = probs.astype(F32)
            probs_grad = nn(V[0:top], DCTM[head, :, q])
            middle = jnp.sum(soft * probs_grad, axis=0, keepdims=True)
            score_grad = (soft * (probs_grad - middle)).astype(BF)
            DQT[hr, q] = nn(KT[hr, 0:top], score_grad) * 0.125
            DK[0:top] += nn(score_grad, QM[head, q])
            DV[0:top] += nn(probs, DCM[head, q])

    attention_back(0)
    attention_back(1)
    spread2 = spread_start(near2, G2, X2, C2, R2, 64)

    QKP[0:128] = DQT[...]
    QKP[128:256] = jnp.transpose(DK[...])
    for base in (0, 64, 128, 192):
        one = QKP[base : base + 8]
        two = QKP[base + 8 : base + 16]
        QKP[base : base + 8] = one * cosine + two * sine
        QKP[base + 8 : base + 16] = two * cosine - one * sine
    MT[0:256] = QKP[...].astype(BF)
    MT[256:384] = jnp.transpose(DV[...]).astype(BF)

    put(G3, nn(MT[...], N1[...]))
    near3 = near_start(G3, X3, 48)
    M[:, 0:256] = jnp.transpose(QKP[...]).astype(BF)
    M[:, 256:384] = DV[...].astype(BF)
    SUMS[...] = jnp.zeros_like(SUMS)
    in_cores = []
    in_z = []

    def norm_grads(zz):
        at = rows(256 * zz, 256)
        xhat = XH[at].astype(F32)
        one = nt(M[at], WQ[...].reshape(1024, 384))
        two = nt(DG[at], WU[...].reshape(1024, 512))
        DB[zz] = (one * gain1 + two * gain2).astype(BF).reshape(2, 128, 1024)
        in_cores.append(remote(DB.at[zz, 1 - k], DRA.at[zz], partner))
        SUMS[0] += fold(one * xhat)
        SUMS[1] += fold(one)
        SUMS[2] += fold(two * xhat)
        SUMS[3] += fold(two)

    def norm_send(j):
        zz = zs[j]
        in_cores[j].wait_recv()
        DRT[j] = (DB[zz, k].astype(F32) + DRA[zz].astype(F32)).astype(BF)
        in_z.append(remote(DRT.at[j], DRZ.at[j], z_to(zz)))

    norm_grads(across_z)
    norm_grads(ahead)
    arrived(y1)
    CY1[...] = (
        G1[rows(160 * y, 160)].astype(F32) + R1[0].astype(F32) + R1[1].astype(F32) + R1[2].astype(F32)
    ).astype(BF)
    x1 = [
        remote(CY1.at[rows(80 * h, 80)], X1.at[0], x_near, off, home),
        remote(CY1.at[rows(80 * (1 - h), 80)], X1.at[1], x_far, off, home),
        remote(CY1.at[rows(80 * (1 - h), 80)], X1.at[2], h_peer, home, home),
    ]
    norm_send(0)
    norm_grads(behind)
    norm_send(1)
    norm_grads(z)
    norm_send(2)
    spread3 = spread_start(near3, G3, X3, C3, R3, 48)
    out_x = scatter_x(out_z, PB, PRA, PRZ, PFX, PRX)
    spread_sum(spread2, C2, R2, S2, 64)
    turn2 = turn(S2, f2_ref, 64)

    SV[...] = jnp.zeros_like(SV)
    bias_grad = jnp.sum(fold(M[...].astype(F32)), axis=0, keepdims=True)
    B24[...] = jnp.zeros_like(B24)
    for j in range(3):
        B24[pl.ds(8 * j + b, 1)] = bias_grad[:, 128 * j : 128 * j + 128]
    for sp in range(8):
        at = slice(128 * sp, 128 * sp + 128)
        for j in range(4):
            SV[sp, j : j + 1] = jnp.sum(SUMS[j, :, at], axis=0, keepdims=True)
        SV[sp, 4:7] = B24[3 * sp : 3 * sp + 3]
    up_grad = jnp.sum(CDG[...], axis=0, keepdims=True)
    for j in range(4):
        SV[b, 8 + j : 9 + j] = up_grad[:, 128 * j : 128 * j + 128]
    SV[b, 12:13] = jnp.sum(CG[:, lanes(128 * b, 128)], axis=0, keepdims=True)
    vectors = [remote(SV.at[flip(s, m)], SVR.at[m - 1], shard_to(m)) for m in range(1, 8)]

    arrived(x1)

    @pl.when(home)
    def _():
        S1[...] = (
            CY1[rows(80 * h, 80)].astype(F32) + X1[0].astype(F32) + X1[1].astype(F32) + X1[2].astype(F32)
        ).astype(BF)
        f1_ref[y, h] = S1[...]

    give1 = [remote(S1, f1_ref.at[y, h], chip_to(m), home, home) for m in range(1, 8)]
    scatter_end(out_x, PRX)
    out_ref[...] = (OWNH[...].astype(F32) + ACC[...] + VEC[4:5]).astype(BF)
    spread_sum(spread3, C3, R3, S3, 48)
    turn3 = turn(S3, f3_ref, 48)
    give2 = give_y(turn2, f2_ref, 64)
    arrived(vectors)
    total = SV[s]
    for m in range(7):
        total = total + SVR[m]
    LV[...] = total
    pair_v = remote(LV, LVX, partner)
    in_cores[3].wait_recv()
    in_x = scatter_x(in_z, DB, DRA, DRZ, DFX, DRX)
    pair_v.wait_recv()
    LC[...] = LV[...] + LVX[...]
    LCR[chip] = LC[...]
    spread_v = [remote(LC, LCR.at[chip], chip_to(m)) for m in range(1, 8)]
    give3 = give_y(turn3, f3_ref, 48)
    last1 = [remote(f1_ref.at[y, h], f1_ref.at[y, h], partner, home, off)]
    for m in range(1, 8):
        give1[m - 1].wait_recv()
        piece = f1_ref.at[flip(y, m % 4), flip(h, m // 4)]
        last1.append(remote(piece, piece, partner, home, off))
    last2 = give_core(give2, f2_ref, 64)

    scatter_end(in_x, DRX)
    block = OWNH[...].astype(F32)
    center = block - jnp.mean(block, axis=-1, keepdims=True)
    spread = jnp.mean(center * center, axis=-1, keepdims=True)
    scale = lax.rsqrt(spread + 1e-05)
    xhat = center * scale
    grad = ACC[...]
    grad = grad - jnp.mean(grad, axis=-1, keepdims=True) - xhat * jnp.mean(grad * xhat, axis=-1, keepdims=True)
    ing_ref[...] = (OWNG[...].astype(F32) + scale * grad).astype(BF)

    arrived(spread_v)
    total = LCR[0]
    for m in range(1, 8):
        total = total + LCR[m]
    vec_ref[...] = total
    last3 = give_core(give3, f3_ref, 48)
    arrived(last1)
    arrived(last2)
    arrived(last3)
    for copy in sent:
        copy.wait_send()
    assert used[0] <= SEMS, used[0]


def block_call(*args):
    vm = pltpu.VMEM
    scratch = [
        vm((16, 128), F32), vm((8, 128), jnp.int32),
        vm((8, 8, 128), jnp.int32), vm((128, 1024), BF), vm((512, 1024), BF), vm((128, 1024), BF), vm((128, 1024), BF),
        vm((4, 2, 128, 1024), BF), vm((4, 2, 128, 1024), BF), vm((8, 8, 128), jnp.int32), vm((8, 16, 128), F32),
        vm((4, 2, 128, 384), BF), vm((4, 2, 128, 512), BF), vm((8, 1024), F32), vm((24, 128), F32),
        vm((1024, 1024), BF), vm((1024, 1024), BF), vm((1024, 1024), BF), vm((256, 1024), F32),
        vm((2, 8, 1024), F32), vm((8, 1024), jnp.int32),
        vm((2, 128, 1024), BF), vm((2, 1024, 128), BF), vm((128, 1024), BF), vm((1024, 128), BF),
        vm((1024, 128), BF), vm((128, 1024), BF),
        vm((1024, 512), F32), vm((1024, 512), BF), vm((512, 1024), BF), vm((2, 1024, 1024), BF),
        vm((128, 1024), BF), vm((1024, 128), BF), vm((2, 1024, 128), BF), vm((2, 128, 1024), BF),
        vm((1024, 512), BF), vm((512, 1024), BF), vm((128, 1024), F32), vm((1024, 128), F32), vm((1024, 128), F32),
        vm((1024, 384), BF), vm((384, 1024), BF),
    ]
    for _ in range(2):
        scratch += [
            vm((4, 2, 128, 1024), BF), vm((4, 128, 1024), BF), vm((3, 128, 1024), BF), vm((3, 128, 1024), BF),
            vm((128, 1024), BF), vm((128, 1024), BF),
        ]
    scratch += [vm((128, 1024), F32)]
    scratch += [
        vm((640, 1024), BF), vm((3, 80, 1024), BF), vm((3, 160, 1024), BF), vm((80, 1024), BF), vm((160, 1024), BF),
    ]
    scratch += [
        vm((512, 1024), BF), vm((512, 512), BF), vm((512, 512), BF), vm((7, 64, 512), BF), vm((64, 512), BF),
        vm((384, 1024), BF), vm((384, 512), BF), vm((384, 512), BF), vm((7, 48, 512), BF), vm((48, 512), BF),
    ]
    scratch += [
        vm((4, 8, 1024), F32), vm((8, 1024), F32), vm((8, 512), F32), vm((8, 16, 128), F32), vm((7, 16, 128), F32),
        vm((16, 128), F32), vm((16, 128), F32), vm((16, 128), F32), vm((8, 16, 128), F32),
        pltpu.SemaphoreType.DMA((SEMS,)), pltpu.SemaphoreType.DMA((SEMS,)), pltpu.SemaphoreType.DMA((10,)),
    ]
    return pl.pallas_call(
        kernel,
        out_shape=(
            jax.ShapeDtypeStruct((128, 1024), BF), jax.ShapeDtypeStruct((128, 1024), BF),
            jax.ShapeDtypeStruct((4, 2, 80, 1024), BF), jax.ShapeDtypeStruct((2, 4, 512, 128), BF),
            jax.ShapeDtypeStruct((2, 4, 384, 128), BF), jax.ShapeDtypeStruct((16, 128), F32),
        ),
        in_specs=[
            pl.BlockSpec(memory_space=pl.ANY if len(arg.shape) == 2 else pltpu.VMEM) for arg in args
        ],
        out_specs=[pl.BlockSpec(memory_space=pltpu.VMEM)] * 6,
        scratch_shapes=scratch,
        compiler_params=pltpu.CompilerParams(
            collective_id=0, has_side_effects=True, vmem_limit_bytes=62 * 2**20
        ),
    )(*args)


def finish(
    out_in, ing_in, f1_in, f2_in, f3_in, vec_ref,
    out_ref, ing_ref, v1_ref, v2_ref, v3_ref, v4_ref, qkv_ref, vq_ref, dense_ref, vd_ref, up_ref, vu_ref, down_ref,
    vw_ref, B1, B2, B3, B4, B5, O1, O2, O3, sems,
):
    take = [
        pltpu.make_async_copy(f3_in, B3, sems.at[0]),
        pltpu.make_async_copy(f2_in, B2, sems.at[1]),
        pltpu.make_async_copy(f1_in, B1, sems.at[2]),
        pltpu.make_async_copy(out_in, B4, sems.at[3]),
        pltpu.make_async_copy(ing_in, B5, sems.at[4]),
    ]
    for copy in take:
        copy.start()
    for ref, at in (
        (v1_ref, 0), (v2_ref, 1), (v3_ref, 2), (v4_ref, 3), (vq_ref, 4), (vu_ref, 8), (vd_ref, 12), (vw_ref, 12)
    ):
        size = ref.shape[0]
        ref[...] = vec_ref[at : at + size // 128].reshape(size)
    put = []

    def give(source, target):
        copy = pltpu.make_async_copy(source, target, sems.at[5 + len(put)])
        copy.start()
        put.append(copy)

    take[0].wait()
    for j in range(3):
        for sp in range(8):
            at = 1024 * j + 128 * sp
            O3[:, at : at + 128] = jnp.transpose(B3[sp % 2, sp // 2, 128 * j : 128 * j + 128].astype(F32))
        part = slice(1024 * j, 1024 * j + 1024)
        give(O3.at[:, part], qkv_ref.at[:, part])
    take[1].wait()
    for sp in range(8):
        for j in range(4):
            at = 512 * sp + 128 * j
            O2[:, at : at + 128] = jnp.transpose(B2[sp % 2, sp // 2, 128 * j : 128 * j + 128].astype(F32))
        if sp % 2:
            part = slice(512 * sp - 512, 512 * sp + 512)
            give(O2.at[:, part], up_ref.at[:, part])
    take[3].wait()
    give(B4, out_ref)
    take[4].wait()
    give(B5, ing_ref)
    take[2].wait()
    for j in range(4):
        O1[160 * j : 160 * j + 160] = B1[j].astype(F32).reshape(160, 1024)
        if j < 3:
            give(O1.at[160 * j : 160 * j + 160], down_ref.at[160 * j : 160 * j + 160])
    give(O1.at[480:512], down_ref.at[480:512])
    give(O1.at[512:640], dense_ref)
    for copy in put:
        copy.wait()


def shards(*args):
    given = block_call(*args)
    vm = pltpu.VMEM
    any_, whole = pl.BlockSpec(memory_space=pl.ANY), pl.BlockSpec(memory_space=vm)

    def flat(size):
        return jax.ShapeDtypeStruct((size,), F32)

    def wide(rows, columns, kind=F32):
        return jax.ShapeDtypeStruct((rows, columns), kind)

    return pl.pallas_call(
        finish,
        out_shape=(
            wide(128, 1024, BF), wide(128, 1024, BF), flat(128), flat(128), flat(128), flat(128), wide(128, 3072),
            flat(384), wide(128, 1024), flat(128), wide(128, 4096), flat(512), wide(512, 1024), flat(128),
        ),
        in_specs=[any_] * 5 + [whole],
        out_specs=[
            any_, any_, whole, whole, whole, whole, any_, whole, any_, whole, any_, whole, any_, whole,
        ],
        scratch_shapes=[
            vm((4, 2, 80, 1024), BF), vm((2, 4, 512, 128), BF), vm((2, 4, 384, 128), BF),
            vm((128, 1024), BF), vm((128, 1024), BF), vm((640, 1024), F32),
            vm((128, 4096), F32), vm((128, 3072), F32), pltpu.SemaphoreType.DMA((20,)),
        ],
        compiler_params=pltpu.CompilerParams(vmem_limit_bytes=62 * 2**20),
    )(*given)


def solution(mesh):
    both, one, wide = P(("rep", "shard"), None), P("shard"), P("shard", None)
    placed = (
        both, both, P(("rep", "shard")), one, one, one, one, wide, one, wide, one, wide, one, wide, one,
    )
    return jax.shard_map(
        shards, mesh=mesh, in_specs=placed,
        out_specs=(both, both, one, one, one, one, wide, one, wide, one, wide, one, wide, one),
        check_vma=False,
    )
```

```python
import functools

import jax
import jax.numpy as jnp
from jax import lax
from jax.experimental import pallas as pl
from jax.experimental.pallas import tpu as pltpu
from jax.sharding import PartitionSpec as P

BF = jnp.bfloat16
F32 = jnp.float32
MESH = pl.DeviceIdType.MESH
SEMS = 176


def flip(value, mask):
    out = value
    bit = 1
    while bit <= mask:
        if mask & bit:
            out = out + bit - 2 * bit * lax.rem(lax.div(value, bit), 2)
        bit *= 2
    return out


def nt(left, right):
    return lax.dot_general(left, right, (((1,), (1,)), ((), ())), preferred_element_type=F32)


def nn(left, right):
    return jnp.dot(left, right, preferred_element_type=F32)


def fold(block):
    return jnp.sum(block.reshape(block.shape[0] // 8, 8, block.shape[1]), axis=0)


def kernel(
    hid_ref, g_ref, seg_ref, gain1_ref, shift1_ref, gain2_ref, shift2_ref, wqkv_ref, bqkv_ref, wdense_ref,
    bdense_ref, wup_ref, bup_ref, wdown_ref, bdown_ref,
    out_ref, ing_ref, f1_ref, f2_ref, f3_ref, vec_ref, PKO, SGO, SGX, WD, WN, OWNH, OWNG,
    HB, GB, SG, PK, WQ, WU, VEC, B24, XH, N1, N2, QKP, TAB, START, QTM, QM, KT, K, V, VT,
    GP, ACT, ACTT, PT, CTXT, CTX, DCM, DCTM, DG, DGT, DQT, DK, DV, M, MT,
    PB, PRA, PRT, PRZ, PFX, PRX, DB, DRA, DRT, DRZ, DFX, DRX, ACC, ACCO,
    G1, X1, R1, S1, CY1, G2, X2, C2, R2, S2, G3, X3, C3, R3, S3,
    SUMS, CG, CDG, SV, SVR, LV, LVX, LC, LCR,
    ssem, rsem, lsem,
):
    r = lax.axis_index("rep")
    s = lax.axis_index("shard")
    k = lax.rem(r, 2)
    chip = lax.div(r, 2)
    y = lax.rem(chip, 4)
    h = lax.div(chip, 4)
    z = lax.div(s, 2)
    l = lax.rem(s, 2)
    b = 2 * z + k
    home = k == l
    off = k != l
    zs = (lax.rem(z + 2, 4), lax.rem(z + 1, 4), lax.rem(z + 3, 4))
    across_z, ahead, behind = zs

    def shard_to(m):
        return {"shard": flip(s, m)}

    def chip_to(m):
        return {"rep": flip(chip, m) * 2 + k}

    def z_to(zz):
        return {"shard": 2 * zz + l}

    partner = {"rep": chip * 2 + 1 - k}
    x_near = {"shard": 2 * z + 1 - l}
    x_far = {"rep": (1 - h) * 8 + y * 2 + k, "shard": 2 * z + 1 - l}
    x_cross = {"rep": chip * 2 + 1 - k, "shard": 2 * z + 1 - l}

    def lanes(start, size):
        return pl.ds(pl.multiple_of(start, 128), size)

    def rows(start, size):
        return pl.ds(pl.multiple_of(start, 16), size)

    barrier = pltpu.get_barrier_semaphore()
    peers = [shard_to(m) for m in range(1, 8)] + [chip_to(m) for m in range(1, 8)] + [partner, x_far, x_cross]
    peers += [{"rep": (4 * (1 - h) + y) * 2 + k, "shard": 2 * zz + l} for zz in zs]
    for peer in peers:
        pl.semaphore_signal(barrier, inc=1, device_id=peer, device_id_type=MESH)

    local = [
        pltpu.make_async_copy(hid_ref, OWNH, lsem.at[0]),
        pltpu.make_async_copy(g_ref, OWNG, lsem.at[1]),
        pltpu.make_async_copy(
            wup_ref.at[rows(32 * y, 32), lanes(512 * b, 512)], WU.at[z, l, rows(32 * y, 32)], lsem.at[2]),
    ]
    for j in range(3):
        local.append(pltpu.make_async_copy(
            wqkv_ref.at[:, lanes(1024 * j + 128 * b, 128)], WQ.at[z, l, :, 128 * j : 128 * j + 128], lsem.at[3 + j]))
    own_only = [
        pltpu.make_async_copy(hid_ref, HB.at[z, k], lsem.at[6]),
        pltpu.make_async_copy(g_ref, GB.at[z, k], lsem.at[7]),
        pltpu.make_async_copy(wdense_ref, WD, lsem.at[8]),
        pltpu.make_async_copy(wdown_ref, WN, lsem.at[9]),
    ]
    for copy in local:
        copy.start()

    @pl.when(home)
    def _():
        for copy in own_only:
            copy.start()

    PKO[...] = jnp.zeros_like(PKO)
    at = 0
    for ref in (gain1_ref, shift1_ref, gain2_ref, shift2_ref, bqkv_ref, bdense_ref, bup_ref, bdown_ref):
        size = ref.shape[0] // 128
        PKO[at : at + size] = ref[...].astype(F32).reshape(size, 128)
        at += size
    PK[s] = PKO[...]
    SGO[...] = jnp.broadcast_to(seg_ref[...].reshape(1, 128), (8, 128))
    SG[s] = SGO[...]
    for copy in local:
        copy.wait()

    @pl.when(home)
    def _():
        for copy in own_only:
            copy.wait()

    pl.semaphore_wait(barrier, len(peers))

    used = [0]
    sent = []

    class Copy:
        def __init__(self, src, dst, device, send, recv):
            at = used[0]
            used[0] += 1
            self.copy = pltpu.make_async_remote_copy(
                src_ref=src, dst_ref=dst, send_sem=ssem.at[at], recv_sem=rsem.at[at],
                device_id=device, device_id_type=MESH,
            )
            self.send = send
            self.recv = recv
            sent.append(self)
            self.under(send, self.copy.start)

        def under(self, role, action):
            if role is None:
                action()
            else:
                pl.when(role)(lambda: action())

        def wait_recv(self):
            self.under(self.recv, self.copy.wait_recv)

        def wait_send(self):
            self.under(self.send, self.copy.wait_send)

    def remote(src, dst, device, send=None, recv=None):
        return Copy(src, dst, device, send, recv)

    def arrived(copies):
        for copy in copies:
            copy.wait_recv()

    low = slice(0, 64)
    high = slice(64, 128)

    def same(ref, device):
        return remote(ref, ref, device)

    def gather_x(x_ref, XB):
        return remote(x_ref, XB.at[z, l], x_cross, off, off)

    def gather_z(first, XB):
        first.wait_recv()
        own = XB.at[z, k]
        return XB, same(own, z_to(ahead)), same(own, z_to(behind)), [same(own, partner)]

    def gather_next(state):
        XB, za, zb, cores = state
        za.wait_recv()
        d2a = same(XB.at[behind, k, low], z_to(ahead))
        cores.append(same(XB.at[behind, k], partner))
        zb.wait_recv()
        d2b = same(XB.at[ahead, k, high], z_to(behind))
        cores.append(same(XB.at[ahead, k], partner))
        return XB, d2a, d2b, cores

    def gather_straight(first, XB):
        first.wait_recv()
        own = XB.at[z, k]
        return [same(own, z_to(zz)) for zz in (across_z, ahead, behind)], [same(own, partner)]

    def gather_core(state, XB):
        copies, cores = state
        for copy, zz in zip(copies, (across_z, behind, ahead)):
            copy.wait_recv()
            cores.append(same(XB.at[zz, k], partner))
        return cores

    def gather_last(state):
        XB, d2a, d2b, cores = state
        arrived([d2a, d2b])
        cores.append(same(XB.at[across_z, k], partner))
        return cores

    def weight_z(ref, W, width, blocks):
        return [
            [remote(
                ref.at[:, lanes(1024 * j + width * (2 * zz + k), width)],
                W.at[z, l, :, width * j : width * j + width], z_to(zz)) for j in range(blocks)]
            for zz in (ahead, behind, across_z)
        ]

    def weight_x(W, zz):
        return [same(W.at[zz, l, low], x_near), same(W.at[zz, l, high], x_far)]

    y_peers = [{"rep": (4 * h + flip(y, m)) * 2 + k} for m in (1, 3, 2)]
    near32 = rows(32 * y, 16)
    far32 = rows(32 * y + 16, 16)
    both32 = rows(32 * y, 32)
    gather_h = gather_x(hid_ref, HB)
    up_z = [
        remote(wup_ref.at[both32, lanes(512 * (2 * zz + k), 512)], WU.at[z, l, both32], z_to(zz))
        for zz in (ahead, behind, across_z)
    ]
    qkv_z = weight_z(wqkv_ref, WQ, 128, 3)
    qkv_x = weight_x(WQ, z)
    gather_g = gather_x(g_ref, GB)
    gather_h = gather_z(gather_h, HB)
    small = [remote(PKO, PK.at[s], shard_to(m)) for m in range(1, 8)]
    small += [remote(SGO, SG.at[s], shard_to(m)) for m in range(1, 8)]
    arrived(up_z)
    up_x = [same(WU.at[:, l, near32], x_near), same(WU.at[:, l, far32], x_far)]
    for copies, zz in zip(qkv_z, (behind, ahead, across_z)):
        arrived(copies)
        qkv_x += weight_x(WQ, zz)
    arrived(up_x)
    up_y = [same(WU.at[:, :, both32], peer) for peer in y_peers]
    gather_h = gather_next(gather_h)
    gather_g = gather_straight(gather_g, GB)
    outer = [
        remote(wdown_ref.at[0:256], WN.at[0:256], x_near, home, off),
        remote(wdown_ref.at[256:512], WN.at[256:512], x_far, home, off),
        remote(wdense_ref.at[low], WD.at[low], x_near, home, off),
        remote(wdense_ref.at[high], WD.at[high], x_far, home, off),
    ]
    arrived(small)
    seg_core = remote(SG, SGX, partner)
    rest_h = gather_last(gather_h)

    for sp in range(8):
        block = PK[sp]
        at = slice(128 * sp, 128 * sp + 128)
        for j in range(4):
            VEC[j : j + 1, at] = block[j : j + 1]
        VEC[4:5, at] = block[7:8] + block[12:13]
        B24[3 * sp : 3 * sp + 3] = block[4:7]
    own = PK[b]
    bias_up = jnp.concatenate([own[8 + j : 9 + j] for j in range(4)], axis=1)
    bias_q = jnp.concatenate([B24[pl.ds(8 * j + b, 1)] for j in range(3)], axis=1)
    seg_core.wait_recv()
    ids = [jnp.where(home, SG[sp, 0:1], SGX[sp, 0:1]).astype(F32) for sp in range(8)]
    seg_row = jnp.concatenate(ids, axis=1)
    count = jnp.zeros((1, 1024), F32)
    for sp in range(8):
        column = jnp.transpose(jnp.broadcast_to(ids[sp], (128, 128)))[:, 0:1]
        count = count + jnp.sum((column < seg_row).astype(F32), axis=0, keepdims=True)
    START[...] = jnp.broadcast_to(count.astype(jnp.int32), (8, 1024))
    place = lax.broadcasted_iota(jnp.int32, (8, 1024), 1).astype(F32)
    row8 = lax.broadcasted_iota(jnp.int32, (8, 1024), 0)
    inverse = jnp.zeros((8, 1024), F32)
    for j in range(8):
        inverse = jnp.where(row8 == j, 10000.0 ** (-j / 8.0), inverse)
    angles = (place - count) * inverse
    TAB[0] = jnp.cos(angles)
    TAB[1] = jnp.sin(angles)
    gain1, shift1, gain2, shift2 = (VEC[j : j + 1] for j in range(4))

    arrived(qkv_x)

    def project(zz):
        at = rows(256 * zz, 256)
        cols = lanes(256 * zz, 256)
        block = HB[zz].reshape(256, 1024).astype(F32)
        center = block - jnp.mean(block, axis=-1, keepdims=True)
        spread = jnp.mean(center * center, axis=-1, keepdims=True)
        xhat = center * lax.rsqrt(spread + 1e-05)
        XH[at] = xhat.astype(BF)
        n1 = (xhat * gain1 + shift1).astype(BF)
        N1[at] = n1
        N2[at] = (xhat * gain2 + shift2).astype(BF)
        mixed = nn(n1, WQ[...].reshape(1024, 384)) + bias_q
        QKP[:, cols] = jnp.transpose(mixed[:, :256])
        V[at] = mixed[:, 256:].astype(BF)
        VT[:, cols] = jnp.transpose(mixed[:, 256:]).astype(BF)

    for copy, zz in zip(rest_h, (z, behind, ahead, across_z)):
        copy.wait_recv()
        project(zz)

    cosine = TAB[0]
    sine = TAB[1]
    for base in (0, 64, 128, 192):
        one = QKP[base : base + 8]
        two = QKP[base + 8 : base + 16]
        QKP[base : base + 8] = one * cosine - two * sine
        QKP[base + 8 : base + 16] = two * cosine + one * sine
    queries = QKP[0:128].astype(BF).astype(F32) * 0.125
    keys = QKP[128:256]
    low_rows = lax.broadcasted_iota(jnp.int32, (128, 1024), 0) < 64
    low_cols = lax.broadcasted_iota(jnp.int32, (1024, 128), 1) < 64
    QTM[0] = jnp.where(low_rows, queries, 0.0).astype(BF)
    QTM[1] = jnp.where(low_rows, 0.0, queries).astype(BF)
    back = jnp.transpose(queries)
    QM[0] = jnp.where(low_cols, back, 0.0).astype(BF)
    QM[1] = jnp.where(low_cols, 0.0, back).astype(BF)
    KT[...] = keys.astype(BF)
    K[...] = jnp.transpose(keys).astype(BF)

    def attention(head):
        hr = slice(64 * head, 64 * head + 64)
        for j in range(4):
            top = 256 * (j + 1)
            q = slice(256 * j, 256 * j + 256)
            scores = nn(K[0:top], QTM[head, :, q])
            ki = lax.broadcasted_iota(jnp.int32, (top, 256), 0)
            qi = lax.broadcasted_iota(jnp.int32, (top, 256), 1) + 256 * j
            allowed = (ki <= qi) & (ki >= START[0:1, q])
            scores = jnp.where(allowed, scores, -1e9)
            weight = jnp.exp(scores - jnp.max(scores, axis=0, keepdims=True))
            probs = (weight * (1.0 / jnp.sum(weight, axis=0, keepdims=True))).astype(BF)
            PT[head, 0:top, q] = probs
            CTXT[hr, q] = nn(VT[hr, 0:top], probs).astype(BF)

    attention(0)
    attention(1)

    def scatter_core(TB, RA):
        return [remote(TB.at[zz, 1 - k], RA.at[zz], partner) for zz in (across_z, ahead, behind, z)]

    def scatter_z(copies, TB, RA, RT, RZ):
        out = []
        for j, zz in enumerate(zs):
            copies[j].wait_recv()
            RT[j] = (TB[zz, k].astype(F32) + RA[zz].astype(F32)).astype(BF)
            out.append(remote(RT.at[j], RZ.at[j], z_to(zz)))
        copies[3].wait_recv()
        return out

    def scatter_x(copies, TB, RA, RZ, FX, RX, ACC):
        arrived(copies)
        total = TB[z, k].astype(F32) + RA[z].astype(F32)
        for j in range(3):
            total = total + RZ[j].astype(F32)
        ACC[...] = total
        FX[...] = total.astype(BF)
        return remote(FX, RX, x_cross, off, off)

    def scatter_end(copy, RX, ACC):
        copy.wait_recv()

        @pl.when(off)
        def _():
            ACC[...] = RX[...].astype(F32)

    CTX[...] = jnp.transpose(CTXT[...].astype(F32)).astype(BF)
    rest_g = gather_core(gather_g, GB)
    arrived(up_y)
    arrived(outer)

    @pl.loop(0, 4)
    def _(i):
        at = rows(256 * i, 256)
        cols = lanes(256 * i, 256)
        gate = nn(N2[at], WU[...].reshape(1024, 512)) + bias_up
        phi = 0.5 + 0.5 * lax.erf(gate * 0.7071067811865476)
        GP[at] = phi + gate * jnp.exp(-0.5 * gate * gate) * 0.3989422804014327
        active = gate * phi
        rounded = active.astype(BF)
        ACT[at] = rounded
        ACTT[:, cols] = jnp.transpose(active).astype(BF)
        total = nn(CTX[at], WD[...]) + nn(rounded, WN[...])
        PB[i] = total.astype(BF).reshape(2, 128, 1024)

    out_cores = scatter_core(PB, PRA)
    arrived(rest_g)

    def near_start(GR, X, size):
        part = lanes(512 * (1 - l), 512)
        top = slice(0, 4 * size)
        end = slice(4 * size, 8 * size)
        return [remote(GR.at[top, part], X.at[top], x_near), remote(GR.at[end, part], X.at[end], x_far)]

    def spread_start(near, GR, X, C, R, size):
        arrived(near)
        C[...] = (GR[:, lanes(512 * l, 512)].astype(F32) + X[...].astype(F32)).astype(BF)
        return [
            remote(
                C.at[rows(size * (2 * flip(y, m % 4) + flip(h, m // 4)), size)], R.at[m - 1], chip_to(m))
            for m in range(1, 8)
        ]

    def spread_sum(copies, C, R, S, size):
        arrived(copies)
        total = C[rows(size * (2 * y + h), size)].astype(F32)
        for m in range(7):
            total = total + R[m].astype(F32)
        S[...] = total.astype(BF)

    y_at = [flip(y, m) for m in (1, 3, 2)]
    h_peer = {"rep": (4 * (1 - h) + y) * 2 + k}

    def along_y(C, R, size):
        return [remote(C.at[rows(2 * size * yy, 2 * size)], R.at[m], y_peers[m]) for m, yy in enumerate(y_at)]

    def turn(S, out, size):
        at = rows(size * (2 * y + h), size)
        out[k, z, at] = S[:, lanes(128 * z, 128)]
        copies = []
        for zz in (across_z, ahead, behind, z):
            source = S.at[:, lanes(128 * zz, 128)]
            copies.append(remote(source, out.at[k, z, at], {"rep": (4 * (1 - h) + y) * 2 + k, "shard": 2 * zz + l}))
        for zz in (ahead, behind, across_z):
            copies.append(remote(S.at[:, lanes(128 * zz, 128)], out.at[k, z, at], z_to(zz)))
        return copies

    def quarter(out, yy, size):
        return out.at[k, :, rows(2 * size * yy, 2 * size)]

    def give_y(copies, out, size):
        arrived(copies)
        return [remote(quarter(out, y, size), quarter(out, y, size), peer) for peer in y_peers]

    def give_core(copies, out, size):
        last = [same(quarter(out, y, size), partner)]
        for copy, yy in zip(copies, y_at):
            copy.wait_recv()
            last.append(same(quarter(out, yy, size), partner))
        return last

    def put(GR, total):
        for sp in range(8):
            at = 512 * (sp % 2) + 128 * (sp // 2)
            GR[:, at : at + 128] = total[:, 128 * sp : 128 * sp + 128].astype(BF)

    grads = GB[...].reshape(1024, 1024)
    G1[0:512] = nn(ACTT[...], grads).astype(BF)
    G1[512:640] = nn(CTXT[...], grads).astype(BF)
    y1 = along_y(G1, R1, 80)

    CG[...] = jnp.zeros_like(CG)
    CDG[...] = jnp.zeros_like(CDG)

    @pl.loop(0, 4)
    def _(i):
        at = rows(256 * i, 256)
        cols = lanes(256 * i, 256)
        block = GB[i].reshape(256, 1024)
        CG[...] += fold(block.astype(F32))
        gate_grad = (nt(block, WN[...]) * GP[at]).astype(BF)
        DG[at] = gate_grad
        wide = gate_grad.astype(F32)
        CDG[...] += fold(wide)
        DGT[:, cols] = jnp.transpose(wide).astype(BF)

    put(G2, nn(DGT[...], N2[...]))
    near2 = near_start(G2, X2, 64)
    out_z = scatter_z(out_cores, PB, PRA, PRT, PRZ)

    low_256 = lax.broadcasted_iota(jnp.int32, (256, 128), 1) < 64
    low_t256 = lax.broadcasted_iota(jnp.int32, (128, 256), 0) < 64

    @pl.loop(0, 4)
    def _(i):
        at = rows(256 * i, 256)
        cols = lanes(256 * i, 256)
        grad = nt(GB[i].reshape(256, 1024), WD[...])
        DCM[0, at] = jnp.where(low_256, grad, 0.0).astype(BF)
        DCM[1, at] = jnp.where(low_256, 0.0, grad).astype(BF)
        turned = jnp.transpose(grad)
        DCTM[0, :, cols] = jnp.where(low_t256, turned, 0.0).astype(BF)
        DCTM[1, :, cols] = jnp.where(low_t256, 0.0, turned).astype(BF)

    DK[...] = jnp.zeros_like(DK)
    DV[...] = jnp.zeros_like(DV)

    def attention_back(head):
        hr = slice(64 * head, 64 * head + 64)
        for j in range(4):
            top = 256 * (j + 1)
            q = slice(256 * j, 256 * j + 256)
            probs = PT[head, 0:top, q]
            soft = probs.astype(F32)
            probs_grad = nn(V[0:top], DCTM[head, :, q])
            middle = jnp.sum(soft * probs_grad, axis=0, keepdims=True)
            score_grad = (soft * (probs_grad - middle)).astype(BF)
            DQT[hr, q] = nn(KT[hr, 0:top], score_grad) * 0.125
            DK[0:top] += nn(score_grad, QM[head, q])
            DV[0:top] += nn(probs, DCM[head, q])

    attention_back(0)
    attention_back(1)
    spread2 = spread_start(near2, G2, X2, C2, R2, 64)

    QKP[0:128] = DQT[...]
    QKP[128:256] = jnp.transpose(DK[...])
    for base in (0, 64, 128, 192):
        one = QKP[base : base + 8]
        two = QKP[base + 8 : base + 16]
        QKP[base : base + 8] = one * cosine + two * sine
        QKP[base + 8 : base + 16] = two * cosine - one * sine
    MT[0:256] = QKP[...].astype(BF)
    MT[256:384] = jnp.transpose(DV[...]).astype(BF)

    put(G3, nn(MT[...], N1[...]))
    near3 = near_start(G3, X3, 48)
    M[:, 0:256] = jnp.transpose(QKP[...]).astype(BF)
    M[:, 256:384] = DV[...].astype(BF)
    SUMS[...] = jnp.zeros_like(SUMS)
    in_cores = []
    in_z = []

    def norm_grads(zz):
        at = rows(256 * zz, 256)
        xhat = XH[at].astype(F32)
        one = nt(M[at], WQ[...].reshape(1024, 384))
        two = nt(DG[at], WU[...].reshape(1024, 512))
        DB[zz] = (one * gain1 + two * gain2).astype(BF).reshape(2, 128, 1024)
        in_cores.append(remote(DB.at[zz, 1 - k], DRA.at[zz], partner))
        SUMS[0] += fold(one * xhat)
        SUMS[1] += fold(one)
        SUMS[2] += fold(two * xhat)
        SUMS[3] += fold(two)

    def norm_send(j):
        zz = zs[j]
        in_cores[j].wait_recv()
        DRT[j] = (DB[zz, k].astype(F32) + DRA[zz].astype(F32)).astype(BF)
        in_z.append(remote(DRT.at[j], DRZ.at[j], z_to(zz)))

    norm_grads(across_z)
    norm_grads(ahead)
    arrived(y1)
    CY1[...] = (
        G1[rows(160 * y, 160)].astype(F32) + R1[0].astype(F32) + R1[1].astype(F32) + R1[2].astype(F32)
    ).astype(BF)
    x1 = [
        remote(CY1.at[rows(80 * h, 80)], X1.at[0], x_near, off, home),
        remote(CY1.at[rows(80 * (1 - h), 80)], X1.at[1], x_far, off, home),
        remote(CY1.at[rows(80 * (1 - h), 80)], X1.at[2], h_peer, home, home),
    ]
    norm_send(0)
    norm_grads(behind)
    norm_send(1)
    norm_grads(z)
    norm_send(2)
    spread3 = spread_start(near3, G3, X3, C3, R3, 48)
    spread_sum(spread2, C2, R2, S2, 64)
    turn2 = turn(S2, f2_ref, 64)

    SV[...] = jnp.zeros_like(SV)
    bias_grad = jnp.sum(fold(M[...].astype(F32)), axis=0, keepdims=True)
    B24[...] = jnp.zeros_like(B24)
    for j in range(3):
        B24[pl.ds(8 * j + b, 1)] = bias_grad[:, 128 * j : 128 * j + 128]
    for sp in range(8):
        at = slice(128 * sp, 128 * sp + 128)
        for j in range(4):
            SV[sp, j : j + 1] = jnp.sum(SUMS[j, :, at], axis=0, keepdims=True)
        SV[sp, 4:7] = B24[3 * sp : 3 * sp + 3]
    up_grad = jnp.sum(CDG[...], axis=0, keepdims=True)
    for j in range(4):
        SV[b, 8 + j : 9 + j] = up_grad[:, 128 * j : 128 * j + 128]
    SV[b, 12:13] = jnp.sum(CG[:, lanes(128 * b, 128)], axis=0, keepdims=True)
    vectors = [remote(SV.at[flip(s, m)], SVR.at[m - 1], shard_to(m)) for m in range(1, 8)]

    arrived(x1)

    @pl.when(home)
    def _():
        S1[...] = (
            CY1[rows(80 * h, 80)].astype(F32) + X1[0].astype(F32) + X1[1].astype(F32) + X1[2].astype(F32)
        ).astype(BF)
        f1_ref[y, h] = S1[...]

    give1 = [remote(S1, f1_ref.at[y, h], chip_to(m), home, home) for m in range(1, 8)]
    spread_sum(spread3, C3, R3, S3, 48)
    turn3 = turn(S3, f3_ref, 48)
    give2 = give_y(turn2, f2_ref, 64)
    out_x = scatter_x(out_z, PB, PRA, PRZ, PFX, PRX, ACCO)
    arrived(vectors)
    total = SV[s]
    for m in range(7):
        total = total + SVR[m]
    LV[...] = total
    pair_v = remote(LV, LVX, partner)
    in_cores[3].wait_recv()
    in_x = scatter_x(in_z, DB, DRA, DRZ, DFX, DRX, ACC)
    pair_v.wait_recv()
    LC[...] = LV[...] + LVX[...]
    LCR[chip] = LC[...]
    spread_v = [remote(LC, LCR.at[chip], chip_to(m)) for m in range(1, 8)]
    give3 = give_y(turn3, f3_ref, 48)
    last1 = [remote(f1_ref.at[y, h], f1_ref.at[y, h], partner, home, off)]
    for m in range(1, 8):
        give1[m - 1].wait_recv()
        piece = f1_ref.at[flip(y, m % 4), flip(h, m // 4)]
        last1.append(remote(piece, piece, partner, home, off))
    last2 = give_core(give2, f2_ref, 64)

    scatter_end(out_x, PRX, ACCO)
    out_ref[...] = (OWNH[...].astype(F32) + ACCO[...] + VEC[4:5]).astype(BF)
    scatter_end(in_x, DRX, ACC)
    block = OWNH[...].astype(F32)
    center = block - jnp.mean(block, axis=-1, keepdims=True)
    spread = jnp.mean(center * center, axis=-1, keepdims=True)
    scale = lax.rsqrt(spread + 1e-05)
    xhat = center * scale
    grad = ACC[...]
    grad = grad - jnp.mean(grad, axis=-1, keepdims=True) - xhat * jnp.mean(grad * xhat, axis=-1, keepdims=True)
    ing_ref[...] = (OWNG[...].astype(F32) + scale * grad).astype(BF)

    arrived(spread_v)
    total = LCR[0]
    for m in range(1, 8):
        total = total + LCR[m]
    vec_ref[...] = total
    last3 = give_core(give3, f3_ref, 48)
    arrived(last1)
    arrived(last2)
    arrived(last3)
    for copy in sent:
        copy.wait_send()
    assert used[0] <= SEMS, used[0]


def block_call(*args):
    vm = pltpu.VMEM
    scratch = [
        vm((16, 128), F32), vm((8, 128), jnp.int32),
        vm((8, 8, 128), jnp.int32), vm((128, 1024), BF), vm((512, 1024), BF), vm((128, 1024), BF), vm((128, 1024), BF),
        vm((4, 2, 128, 1024), BF), vm((4, 2, 128, 1024), BF), vm((8, 8, 128), jnp.int32), vm((8, 16, 128), F32),
        vm((4, 2, 128, 384), BF), vm((4, 2, 128, 512), BF), vm((8, 1024), F32), vm((24, 128), F32),
        vm((1024, 1024), BF), vm((1024, 1024), BF), vm((1024, 1024), BF), vm((256, 1024), F32),
        vm((2, 8, 1024), F32), vm((8, 1024), jnp.int32),
        vm((2, 128, 1024), BF), vm((2, 1024, 128), BF), vm((128, 1024), BF), vm((1024, 128), BF),
        vm((1024, 128), BF), vm((128, 1024), BF),
        vm((1024, 512), F32), vm((1024, 512), BF), vm((512, 1024), BF), vm((2, 1024, 1024), BF),
        vm((128, 1024), BF), vm((1024, 128), BF), vm((2, 1024, 128), BF), vm((2, 128, 1024), BF),
        vm((1024, 512), BF), vm((512, 1024), BF), vm((128, 1024), F32), vm((1024, 128), F32), vm((1024, 128), F32),
        vm((1024, 384), BF), vm((384, 1024), BF),
    ]
    for _ in range(2):
        scratch += [
            vm((4, 2, 128, 1024), BF), vm((4, 128, 1024), BF), vm((3, 128, 1024), BF), vm((3, 128, 1024), BF),
            vm((128, 1024), BF), vm((128, 1024), BF),
        ]
    scratch += [vm((128, 1024), F32), vm((128, 1024), F32)]
    scratch += [
        vm((640, 1024), BF), vm((3, 80, 1024), BF), vm((3, 160, 1024), BF), vm((80, 1024), BF), vm((160, 1024), BF),
    ]
    scratch += [
        vm((512, 1024), BF), vm((512, 512), BF), vm((512, 512), BF), vm((7, 64, 512), BF), vm((64, 512), BF),
        vm((384, 1024), BF), vm((384, 512), BF), vm((384, 512), BF), vm((7, 48, 512), BF), vm((48, 512), BF),
    ]
    scratch += [
        vm((4, 8, 1024), F32), vm((8, 1024), F32), vm((8, 512), F32), vm((8, 16, 128), F32), vm((7, 16, 128), F32),
        vm((16, 128), F32), vm((16, 128), F32), vm((16, 128), F32), vm((8, 16, 128), F32),
        pltpu.SemaphoreType.DMA((SEMS,)), pltpu.SemaphoreType.DMA((SEMS,)), pltpu.SemaphoreType.DMA((10,)),
    ]
    return pl.pallas_call(
        kernel,
        out_shape=(
            jax.ShapeDtypeStruct((128, 1024), BF), jax.ShapeDtypeStruct((128, 1024), BF),
            jax.ShapeDtypeStruct((4, 2, 80, 1024), BF), jax.ShapeDtypeStruct((2, 4, 512, 128), BF),
            jax.ShapeDtypeStruct((2, 4, 384, 128), BF), jax.ShapeDtypeStruct((16, 128), F32),
        ),
        in_specs=[
            pl.BlockSpec(memory_space=pl.ANY if len(arg.shape) == 2 else pltpu.VMEM) for arg in args
        ],
        out_specs=[pl.BlockSpec(memory_space=pltpu.VMEM)] * 6,
        scratch_shapes=scratch,
        compiler_params=pltpu.CompilerParams(
            collective_id=0, has_side_effects=True, vmem_limit_bytes=62 * 2**20
        ),
    )(*args)


def finish(
    out_in, ing_in, f1_in, f2_in, f3_in, vec_ref,
    out_ref, ing_ref, v1_ref, v2_ref, v3_ref, v4_ref, qkv_ref, vq_ref, dense_ref, vd_ref, up_ref, vu_ref, down_ref,
    vw_ref, B1, B2, B3, B4, B5, O1, O2, O3, sems,
):
    take = [
        pltpu.make_async_copy(f3_in, B3, sems.at[0]),
        pltpu.make_async_copy(f2_in, B2, sems.at[1]),
        pltpu.make_async_copy(f1_in, B1, sems.at[2]),
        pltpu.make_async_copy(out_in, B4, sems.at[3]),
        pltpu.make_async_copy(ing_in, B5, sems.at[4]),
    ]
    for copy in take:
        copy.start()
    for ref, at in (
        (v1_ref, 0), (v2_ref, 1), (v3_ref, 2), (v4_ref, 3), (vq_ref, 4), (vu_ref, 8), (vd_ref, 12), (vw_ref, 12)
    ):
        size = ref.shape[0]
        ref[...] = vec_ref[at : at + size // 128].reshape(size)
    put = []

    def give(source, target):
        copy = pltpu.make_async_copy(source, target, sems.at[5 + len(put)])
        copy.start()
        put.append(copy)

    take[0].wait()
    for j in range(3):
        for sp in range(8):
            at = 1024 * j + 128 * sp
            O3[:, at : at + 128] = jnp.transpose(B3[sp % 2, sp // 2, 128 * j : 128 * j + 128].astype(F32))
        part = slice(1024 * j, 1024 * j + 1024)
        give(O3.at[:, part], qkv_ref.at[:, part])
    take[1].wait()
    for sp in range(8):
        for j in range(4):
            at = 512 * sp + 128 * j
            O2[:, at : at + 128] = jnp.transpose(B2[sp % 2, sp // 2, 128 * j : 128 * j + 128].astype(F32))
        if sp % 2:
            part = slice(512 * sp - 512, 512 * sp + 512)
            give(O2.at[:, part], up_ref.at[:, part])
    take[3].wait()
    give(B4, out_ref)
    take[4].wait()
    give(B5, ing_ref)
    take[2].wait()
    for j in range(4):
        O1[160 * j : 160 * j + 160] = B1[j].astype(F32).reshape(160, 1024)
        if j < 3:
            give(O1.at[160 * j : 160 * j + 160], down_ref.at[160 * j : 160 * j + 160])
    give(O1.at[480:512], down_ref.at[480:512])
    give(O1.at[512:640], dense_ref)
    for copy in put:
        copy.wait()


def shards(*args):
    given = block_call(*args)
    vm = pltpu.VMEM
    any_, whole = pl.BlockSpec(memory_space=pl.ANY), pl.BlockSpec(memory_space=vm)

    def flat(size):
        return jax.ShapeDtypeStruct((size,), F32)

    def wide(rows, columns, kind=F32):
        return jax.ShapeDtypeStruct((rows, columns), kind)

    return pl.pallas_call(
        finish,
        out_shape=(
            wide(128, 1024, BF), wide(128, 1024, BF), flat(128), flat(128), flat(128), flat(128), wide(128, 3072),
            flat(384), wide(128, 1024), flat(128), wide(128, 4096), flat(512), wide(512, 1024), flat(128),
        ),
        in_specs=[any_] * 5 + [whole],
        out_specs=[
            any_, any_, whole, whole, whole, whole, any_, whole, any_, whole, any_, whole, any_, whole,
        ],
        scratch_shapes=[
            vm((4, 2, 80, 1024), BF), vm((2, 4, 512, 128), BF), vm((2, 4, 384, 128), BF),
            vm((128, 1024), BF), vm((128, 1024), BF), vm((640, 1024), F32),
            vm((128, 4096), F32), vm((128, 3072), F32), pltpu.SemaphoreType.DMA((20,)),
        ],
        compiler_params=pltpu.CompilerParams(vmem_limit_bytes=62 * 2**20),
    )(*given)


def solution(mesh):
    both, one, wide = P(("rep", "shard"), None), P("shard"), P("shard", None)
    placed = (
        both, both, P(("rep", "shard")), one, one, one, one, wide, one, wide, one, wide, one, wide, one,
    )
    return jax.shard_map(
        shards, mesh=mesh, in_specs=placed,
        out_specs=(both, both, one, one, one, one, wide, one, wide, one, wide, one, wide, one),
        check_vma=False,
    )
```
